32 devices in a mesh: dp: 4 (over z), seq: 8 (over y, x, core).
Axes of the slice: x: 2, y: 2, z: 4, core: 2. Of those that a mesh axis runs over, the one named last changes fastest.
Arguments:
- tokens: bfloat16 [8, 1024, 1600], P('dp', 'seq'), may hold values from -6 to 6
- lengths: int32 [8], P('dp'), may hold values from 256 to 1024, as said below
- cotangent: bfloat16 [8, 1024, 1600], P('dp', 'seq'), may hold values from -6 to 6
- w_qkv: bfloat16 [1600, 2240], P('seq'), may hold values from -0.15625 to 0.15625
- w_ao: bfloat16 [1600, 1600], P('seq'), may hold values from -0.15625 to 0.15625
- w_in: bfloat16 [1600, 6400], P('seq'), may hold values from -0.15625 to 0.15625
- w_xp: bfloat16 [3200, 132], P('seq'), may hold values from -0.21875 to 0.21875
- w_dt: bfloat16 [100, 3200], replicated, may hold values from -0.625 to 0.625
- w_so: bfloat16 [3200, 1600], P('seq'), may hold values from -0.109375 to 0.109375
- w_gu: bfloat16 [1600, 2, 5504], P(None, None, 'seq'), may hold values from -0.15625 to 0.15625
- w_down: bfloat16 [5504, 1600], P('seq'), may hold values from -0.15625 to 0.15625
- norm_in: float32 [1600], replicated, may hold values from 0.5 to 1.5
- norm_attn: float32 [1600], replicated, may hold values from 0.5 to 1.5
- norm_ssm: float32 [3200], replicated, may hold values from 0.5 to 1.5
- norm_ffn: float32 [1600], replicated, may hold values from 0.5 to 1.5
- conv_w: float32 [4, 3200], replicated, may hold values from -3 to 3
- conv_b: float32 [3200], replicated, may hold values from -0.5 to 0.5
- dt_bias: float32 [3200], replicated, may hold values from -6 to -2
- a_log: float32 [16, 3200], replicated, may hold values from -3 to 2.5
- d_skip: float32 [3200], replicated, may hold values from 0.5 to 1.5
Outputs:
- block_out: bfloat16 [8, 1024, 1600], P('dp', 'seq')
- grad_tokens: float32 [8, 1024, 1600], P('dp', 'seq')
- grad_w_qkv: float32 [1600, 2240], P('seq')
- grad_w_ao: float32 [1600, 1600], P('seq')
- grad_w_in: float32 [1600, 6400], P('seq')
- grad_w_xp: float32 [3200, 132], P('seq')
- grad_w_dt: float32 [100, 3200], P(None, 'seq')
- grad_w_so: float32 [3200, 1600], P('seq')
- grad_w_gu: float32 [1600, 2, 5504], P(None, None, 'seq')
- grad_w_down: float32 [5504, 1600], P('seq')
- grad_norm_in: float32 [1600], P('seq')
- grad_norm_attn: float32 [1600], P('seq')
- grad_norm_ssm: float32 [3200], P('seq')
- grad_norm_ffn: float32 [1600], P('seq')
- grad_conv_w: float32 [4, 3200], P(None, 'seq')
- grad_conv_b: float32 [3200], P('seq')
- grad_dt_bias: float32 [3200], P('seq')
- grad_a_log: float32 [16, 3200], P(None, 'seq')
- grad_d_skip: float32 [3200], P('seq')
The draws below stay inside these ranges and needn't reach their ends.
Inputs may be any that keep to these rules, and one draw needn't show every extreme that they name: `lengths`: in each aligned group of 2 sequences (one dp index) one sequence, which one drawn from the seed, has length 1024; one other sequence of some group has length 256.
All inputs are finite; a program needn't handle non-finite values.
Results may differ from the reference program's by a relative error of at most 0.025.
Values may be sent and summed in bfloat16 or wider, within the bound.
A program may use at most 512 MiB of HBM per device.

```python
import math
import jax
import jax.numpy as jnp
from jax import lax

D = 1600
HEADS = 25
HEAD = 64
KVH = 5
INNER = 3200
NST = 16
KCONV = 4
DTR = 100
FF = 5504
NSEQ = 2
SEQCAP = 1024
SEQS = 8


def draw_lengths(key, part):
    key = jax.random.fold_in(key, 11)
    first_key = jax.random.fold_in(key, 1)
    second_key = jax.random.fold_in(key, 2)
    third_key = jax.random.fold_in(key, 3)
    fourth_key = jax.random.fold_in(key, 4)
    groups = SEQS // NSEQ
    shortest = SEQCAP // 4
    drawn_lengths = jax.random.randint(first_key, (groups, NSEQ), shortest, SEQCAP + 1)
    chosen = jax.random.randint(second_key, (groups,), 0, NSEQ)
    short_group = jax.random.randint(third_key, (), 0, groups)
    short_offset = jax.random.randint(fourth_key, (), 1, NSEQ)
    slot_index = jnp.arange(NSEQ)[None, :]
    group_index = jnp.arange(groups)[:, None]
    longest = slot_index == chosen[:, None]
    short_slot = (group_index == short_group) & (slot_index == (chosen[:, None] + short_offset) % NSEQ)
    result_lengths = jnp.where(longest, SEQCAP, jnp.where(short_slot, shortest, drawn_lengths))
    return result_lengths.reshape(SEQS).astype(jnp.int32)


def shard_levels(key, shape, cuts, low, high):
    loudness = 1.0
    for position, shards_of in cuts:
        steps = jax.random.uniform(jax.random.fold_in(jax.random.fold_in(key, 6), position), (shards_of,), jnp.float32, low / len(cuts), high / len(cuts))
        loudness = loudness * jnp.repeat(jnp.exp(steps), shape[position] // shards_of).reshape((-1,) + (1,) * (len(shape) - 1 - position))
    return loudness


def bell_draw(own_key, extent, width, most, split=(), kind=jnp.bfloat16):
    level = shard_levels(own_key, extent, split, -0.22, 0.18) if split else 1.0
    values = jax.random.normal(own_key, extent, jnp.float32) * width * level
    return jnp.minimum(jnp.maximum(values, -most), most).astype(kind)


def setup_inputs(seed: int = 0) -> dict:
    streams_of = jax.random.split(jax.random.key(seed), 21)
    tokens = bell_draw(streams_of[0], (SEQS, SEQCAP, D), 1.0, 6.0, ((0, 4), (1, 8)))
    lengths = draw_lengths(jax.random.fold_in(streams_of[20], 71), 0)
    cotangent = bell_draw(streams_of[2], (SEQS, SEQCAP, D), 1.0, 6.0, ((0, 4), (1, 8)))
    w_qkv = bell_draw(streams_of[3], (D, HEADS * HEAD + 2 * KVH * HEAD), D ** -0.5, 0.15625, ((0, 8),))
    w_ao = bell_draw(streams_of[4], (HEADS * HEAD, D), (HEADS * HEAD) ** -0.5, 0.15625, ((0, 8),))
    w_in = bell_draw(streams_of[5], (D, 2 * INNER), D ** -0.5, 0.15625, ((0, 8),))
    w_xp = bell_draw(streams_of[6], (INNER, DTR + 2 * NST), (INNER // 4) ** -0.5, 0.21875, ((0, 8),))
    w_dt = bell_draw(streams_of[7], (DTR, INNER), DTR ** -0.5, 0.625)
    w_so = bell_draw(streams_of[8], (INNER, D), INNER ** -0.5, 0.109375, ((0, 8),))
    w_gu = bell_draw(streams_of[9], (D, 2, FF), D ** -0.5, 0.15625, ((2, 8),))
    w_down = bell_draw(streams_of[10], (FF, D), (FF // 4) ** -0.5, 0.15625, ((0, 8),))
    norm_in = jnp.clip(1.0 + 0.1 * jax.random.normal(streams_of[11], (D,), jnp.float32), 0.5, 1.5)
    norm_attn = jnp.clip(1.0 + 0.1 * jax.random.normal(streams_of[12], (HEADS * HEAD,), jnp.float32), 0.5, 1.5)
    norm_ssm = jnp.clip(1.0 + 0.1 * jax.random.normal(streams_of[13], (INNER,), jnp.float32), 0.5, 1.5)
    norm_ffn = jnp.clip(1.0 + 0.1 * jax.random.normal(streams_of[14], (D,), jnp.float32), 0.5, 1.5)
    conv_w = bell_draw(streams_of[15], (KCONV, INNER), KCONV ** -0.5, 3.0, (), jnp.float32)
    conv_b = jnp.clip(jax.random.uniform(streams_of[16], (INNER,), jnp.float32, -0.5, 0.5), -0.5, 0.5)
    dt_bias = jnp.clip(jax.random.uniform(streams_of[17], (INNER,), jnp.float32, -6.0, -2.0), -6.0, -2.0)
    a_log = jnp.clip(jax.random.uniform(streams_of[18], (NST, INNER), jnp.float32, -3.0, 2.5), -3.0, 2.5)
    d_skip = jnp.clip(jax.random.uniform(streams_of[19], (INNER,), jnp.float32, 0.5, 1.5), 0.5, 1.5)
    return dict(tokens=tokens, lengths=lengths, cotangent=cotangent, w_qkv=w_qkv, w_ao=w_ao, w_in=w_in, w_xp=w_xp, w_dt=w_dt, w_so=w_so, w_gu=w_gu, w_down=w_down, norm_in=norm_in, norm_attn=norm_attn, norm_ssm=norm_ssm, norm_ffn=norm_ffn, conv_w=conv_w, conv_b=conv_b, dt_bias=dt_bias, a_log=a_log, d_skip=d_skip)


EPSILON = 1e-05
NEGATIVE = -1e+30

@jax.custom_vjp
def low(v):
    return lax.optimization_barrier(v.astype(jnp.bfloat16)).astype(jnp.float32)

@jax.custom_vjp
def low_back(v):
    return v

def low_keep(v):
    return (low(v), None)

def low_pass(kept, grad):
    return (grad,)

def back_keep(v):
    return (v, None)

def back_low(kept, grad):
    return (low(grad),)
low.defvjp(low_keep, low_pass)
low_back.defvjp(back_keep, back_low)

def matmul(left, right):
    return jnp.dot(left, right, precision=lax.Precision.HIGHEST, preferred_element_type=jnp.float32)

def scaled_norm(values, gain):
    return values * lax.rsqrt(lax.optimization_barrier(jnp.mean(values * values, axis=-1, keepdims=True)) + EPSILON) * gain

def forward(x_float, seq_length, w_qkv, w_ao, w_in, w_xp, w_dt, w_so, w_gu, w_down, norm_in, norm_attn, norm_ssm, norm_ffn, conv_w, conv_b, dt_bias, a_log, d_skip):
    query_dim = HEADS * HEAD
    kv_dim = KVH * HEAD
    group_heads = HEADS // KVH
    score_scale = HEAD ** (-0.5)
    normed = low(scaled_norm(x_float, norm_in))
    qkv_out = low_back(matmul(normed, w_qkv))
    queries = low(qkv_out[:, :query_dim]).reshape(SEQCAP, KVH, group_heads, HEAD)
    key_rows = low(qkv_out[:, query_dim:query_dim + kv_dim]).reshape(SEQCAP, KVH, HEAD)
    value_rows = low(qkv_out[:, query_dim + kv_dim:]).reshape(SEQCAP, KVH, HEAD)
    qblock = math.gcd(SEQCAP, 512)
    key_pos = jnp.arange(SEQCAP).astype(jnp.int32)

    @jax.checkpoint
    def attend(block_index):
        start = (block_index * qblock).astype(jnp.int32)
        query_part = lax.dynamic_slice_in_dim(queries, start, qblock, 0)
        query_pos = start + jnp.arange(qblock).astype(jnp.int32)
        scores = low_back(jnp.einsum('tgrd,jgd->grtj', query_part, key_rows, precision=lax.Precision.HIGHEST) * score_scale)
        allowed = (key_pos[None, :] <= query_pos[:, None]) & (key_pos[None, :] < seq_length)
        scores = jnp.where(allowed, scores, NEGATIVE)
        highest = lax.optimization_barrier(jnp.max(scores, axis=-1, keepdims=True))
        exponent = jnp.where(allowed, jnp.exp(scores - highest), 0.0)
        weights = low(exponent / lax.optimization_barrier(jnp.sum(exponent, axis=-1, keepdims=True)))
        mixed = jnp.einsum('grtj,jgd->tgrd', weights, value_rows, precision=lax.Precision.HIGHEST)
        return mixed.reshape(qblock, query_dim)
    attended = lax.map(attend, jnp.arange(SEQCAP // qblock).astype(jnp.int32)).reshape(SEQCAP, query_dim)
    attended = low_back(attended)
    attn_low = low(scaled_norm(attended, norm_attn))
    x_and_z = low_back(matmul(normed, w_in))
    x_conv = low(x_and_z[:, :INNER])
    z_gate = x_and_z[:, INNER:]
    padded = jnp.concatenate([jnp.zeros((KCONV - 1, INNER), jnp.float32), x_conv], axis=0)
    conv_pre = conv_b + sum((conv_w[offset] * padded[offset:offset + SEQCAP] for offset in range(KCONV)))
    mixer_in = jax.nn.silu(conv_pre)
    projected = low_back(matmul(low(mixer_in), w_xp))
    step_pre = low_back(matmul(low(projected[:, :DTR]), w_dt)) + dt_bias
    step_size = jax.nn.softplus(step_pre)
    b_input = projected[:, DTR:DTR + NST]
    c_output = projected[:, DTR + NST:]
    decay_rate = -jnp.exp(a_log)
    scan_block = math.gcd(SEQCAP, 128)

    @jax.checkpoint
    def run_block(carried, series):

        def advance(inner_state, current):
            step_now, b_now, c_now, input_now = current
            inner_state = jnp.exp(step_now[None, :] * decay_rate) * inner_state + b_now[:, None] * (step_now * input_now)[None, :]
            return (inner_state, lax.optimization_barrier(jnp.sum(c_now[:, None] * inner_state, axis=0)))
        return lax.scan(advance, carried, series)
    series = tuple((v.reshape(SEQCAP // scan_block, scan_block, v.shape[1]) for v in (step_size, b_input, c_output, mixer_in)))
    _, scanned = lax.scan(run_block, jnp.zeros((NST, INNER), jnp.float32), series)
    mamba_core = scanned.reshape(SEQCAP, INNER) + d_skip * mixer_in
    gated_out = mamba_core * jax.nn.silu(z_gate)
    ssm_low = low(scaled_norm(gated_out, norm_ssm))
    mixed_out = low_back(0.5 * (matmul(attn_low, w_ao) + matmul(ssm_low, w_so)))
    residual = x_float + mixed_out
    normed_two = low(scaled_norm(residual, norm_ffn))
    gate_up = low_back(matmul(normed_two, w_gu.reshape(D, 2 * FF)))
    activated = low(jax.nn.silu(gate_up[:, :FF]) * gate_up[:, FF:])
    ffn_out = low_back(matmul(activated, w_down))
    return residual + ffn_out

def reference(tokens, lengths, cotangent, w_qkv, w_ao, w_in, w_xp, w_dt, w_so, w_gu, w_down, norm_in, norm_attn, norm_ssm, norm_ffn, conv_w, conv_b, dt_bias, a_log, d_skip):
    params = tuple((p.astype(jnp.float32) for p in (w_qkv, w_ao, w_in, w_xp, w_dt, w_so, w_gu, w_down, norm_in, norm_attn, norm_ssm, norm_ffn, conv_w, conv_b, dt_bias, a_log, d_skip)))

    def per_sequence(totals, current):
        token_rows, cot_rows, seq_length = current
        x_float = token_rows.astype(jnp.float32)

        def apply(inputs, *weights_f):
            return forward(inputs, seq_length, *weights_f)
        outseq, pullback = jax.vjp(apply, x_float, *params)
        is_valid = (jnp.arange(SEQCAP).astype(jnp.int32) < seq_length)[:, None]
        gradients = pullback(cot_rows.astype(jnp.float32) * is_valid)
        totals = tuple((a + b for a, b in zip(totals, gradients[1:])))
        return (totals, (outseq.astype(jnp.bfloat16), gradients[0]))
    zeroes = tuple((jnp.zeros_like(p) for p in params))
    totals, stacked = lax.scan(per_sequence, zeroes, (tokens, cotangent, lengths))
    return (stacked[0], stacked[1]) + totals
```

```python
import functools
import math

import jax
import jax.numpy as jnp
from jax import lax
from jax.experimental import pallas as pl
from jax.experimental.pallas import tpu as pltpu
from jax.sharding import PartitionSpec as P

HEADS = 25
HEAD = 64
KVH = 5
INNER = 3200
NST = 16
KCONV = 4
DTR = 100
EPSILON = 1e-05
NEGATIVE = -1e30
CHUNK = 16
LOG2E = math.log2(math.e)
LN2 = math.log(2.0)

BF = jnp.bfloat16
F32 = jnp.float32
NT = (((1,), (1,)), ((), ()))
TN = (((0,), (0,)), ((), ()))
GIANT = 60 * 1024 * 1024
MESH = pl.DeviceIdType.MESH


def ntdot(a, b):
    return lax.dot_general(a, b, NT, preferred_element_type=F32)


def tndot(a, b):
    return lax.dot_general(a, b, TN, preferred_element_type=F32)


def dot(a, b):
    return jnp.dot(a, b, preferred_element_type=F32)


def silu_grad(values):
    logistic = jax.nn.sigmoid(values)
    return logistic * (1.0 + values * (1.0 - logistic))


def chunk_masks():
    spread = NST * CHUNK
    row = lax.broadcasted_iota(jnp.int32, (CHUNK, spread), 0)
    col = lax.broadcasted_iota(jnp.int32, (CHUNK, spread), 1)
    own = (col // NST == row).astype(F32)
    tile = (col % NST == row).astype(BF)
    return own, tile


def scan_fwd_kernel(pre_ref, mix_ref, bt_ref, c_ref, rate_ref, skip_ref, core_ref, start_ref,
                    h_ref, dt_ref, u_ref, wide_ref, hs_ref):
    length, cols = pre_ref.shape[2:]
    own, tile = chunk_masks()

    @pl.when(pl.program_id(1) == 0)
    def _():
        for ref in (h_ref, dt_ref, u_ref, wide_ref):
            ref[...] = jnp.zeros_like(ref)
        wide_ref[:, :cols] = rate_ref[...] * LOG2E

    start_ref[0, 0] = h_ref[:, :cols]
    dt = jax.nn.softplus(pre_ref[0, 0])
    dt_ref[:, :cols] = dt
    u_ref[:, :cols] = dt * mix_ref[0, 0]
    rate = wide_ref[...]
    spread = NST * CHUNK

    def chunk(k, h):
        base = pl.multiple_of(k * CHUNK, CHUNK)
        bt = bt_ref[0, 0, k]
        for t in range(CHUNK):
            a = jnp.exp2(dt_ref[pl.ds(base + t, 1), :] * rate)
            h = a * h + bt[:, t : t + 1] * u_ref[pl.ds(base + t, 1), :]
            hs_ref[pl.ds(pl.multiple_of((base + t) * NST, NST), NST), :] = h.astype(BF)
        return h

    h_ref[...] = lax.fori_loop(0, length // CHUNK, chunk, h_ref[...])
    crep = dot(c_ref[0, 0].astype(BF), tile)
    for k in range(length // CHUNK):
        at = slice(k * CHUNK, (k + 1) * CHUNK)
        cb = (crep[at] * own).astype(BF)
        core_ref[0, 0, at, :] = dot(cb, hs_ref[k * spread : (k + 1) * spread])[:, :cols] + skip_ref[...] * mix_ref[0, 0, at, :]

def scan_forward(pre, mix, bt, c, rate, skip):
    n, seqs, length, cols = pre.shape
    wide = -(-cols // 128) * 128
    big = lambda w: pl.BlockSpec((1, 1, length, w), lambda s, i: (i, s, 0, 0))
    whole = lambda r: pl.BlockSpec((r, cols), lambda s, i: (0, 0))
    return pl.pallas_call(
        scan_fwd_kernel,
        grid=(seqs, n),
        in_specs=[
            big(cols), big(cols),
            pl.BlockSpec((1, 1) + bt.shape[2:], lambda s, i: (i, s, 0, 0, 0)),
            big(NST), whole(NST), whole(1),
        ],
        out_specs=[big(cols), pl.BlockSpec((1, 1, NST, cols), lambda s, i: (i, s, 0, 0))],
        out_shape=[
            jax.ShapeDtypeStruct(pre.shape, F32),
            jax.ShapeDtypeStruct((n, seqs, NST, cols), F32),
        ],
        scratch_shapes=[
            pltpu.VMEM((NST, wide), F32),
            pltpu.VMEM((length, wide), F32),
            pltpu.VMEM((length, wide), F32),
            pltpu.VMEM((NST, wide), F32),
            pltpu.VMEM((NST * length, wide), BF),
        ],
        compiler_params=pltpu.CompilerParams(vmem_limit_bytes=GIANT),
    )(pre, mix, bt, c, rate, skip)

def scan_bwd_kernel(pre_ref, mix_ref, gin_ref, start_ref, bt_ref, ct_ref, b_ref, rate_ref, skip_ref,
                    gpre_ref, gmix_ref, gb_ref, gc_ref, grate_ref, gskip_ref,
                    carry_ref, dt_ref, u_ref, gy_ref, wide_ref, hs_ref, gs_ref, q_ref):
    length, cols = pre_ref.shape[2:]
    own, tile = chunk_masks()
    spread = NST * CHUNK
    half = NST // 2
    folded = (lax.broadcasted_iota(jnp.int32, (2 * CHUNK, spread), 1) // half
              == lax.broadcasted_iota(jnp.int32, (2 * CHUNK, spread), 0)).astype(BF)

    @pl.when(pl.program_id(1) == 0)
    def _():
        carry_ref[...] = jnp.zeros_like(carry_ref)

    @pl.when((pl.program_id(1) == 0) & (pl.program_id(0) == 0))
    def _():
        grate_ref[...] = jnp.zeros_like(grate_ref)
        gskip_ref[...] = jnp.zeros_like(gskip_ref)
        for ref in (dt_ref, u_ref, gy_ref, wide_ref):
            ref[...] = jnp.zeros_like(ref)
        wide_ref[0:NST, :cols] = rate_ref[...] * LOG2E

    dt = jax.nn.softplus(pre_ref[0, 0])
    dt_ref[:, :cols] = dt
    u_ref[:, :cols] = dt * mix_ref[0, 0]
    gy_ref[:, :cols] = gin_ref[0, 0]
    wide_ref[NST:, :cols] = start_ref[0, 0]
    gskip_ref[...] += jnp.sum(gin_ref[0, 0] * mix_ref[0, 0], axis=0, keepdims=True)
    rate = wide_ref[0:NST]
    hs_ref[0:NST] = wide_ref[NST:].astype(BF)

    def ahead(k, h):
        base = pl.multiple_of(k * CHUNK, CHUNK)
        bt = bt_ref[0, 0, k]
        for t in range(CHUNK):
            a = jnp.exp2(dt_ref[pl.ds(base + t, 1), :] * rate)
            h = a * h + bt[:, t : t + 1] * u_ref[pl.ds(base + t, 1), :]
            hs_ref[pl.ds(pl.multiple_of((base + t + 1) * NST, NST), NST), :] = h.astype(BF)
        return h

    lax.fori_loop(0, length // CHUNK, ahead, wide_ref[NST:])

    def back(r, state):
        carry, grate = state
        k = length // CHUNK - 1 - r
        base = pl.multiple_of(k * CHUNK, CHUNK)
        ct = ct_ref[0, 0, k]
        qr_late = None
        for t in reversed(range(CHUNK)):
            at = pl.ds(pl.multiple_of((base + t) * NST, NST), NST)
            dt_row = dt_ref[pl.ds(base + t, 1), :]
            a = jnp.exp2(dt_row * rate)
            g = ct[:, t : t + 1] * gy_ref[pl.ds(base + t, 1), :] + carry
            carry = a * g
            q = carry * hs_ref[at, :].astype(F32)
            grate = grate + q * dt_row
            gs_ref[at, :] = g.astype(BF)
            qr = q * rate
            qr = qr[:half] + qr[half:]
            if t % 2:
                qr_late = qr
            else:
                both = jnp.concatenate([qr, qr_late], axis=0).astype(BF)
                q_ref[pl.ds(pl.multiple_of((base + t) * half, NST), NST), :] = both
        return carry, grate

    carry, grate = lax.fori_loop(
        0, length // CHUNK, back, (carry_ref[...], jnp.zeros(carry_ref.shape, F32))
    )
    carry_ref[...] = carry
    grate_ref[...] += grate[:, :cols]
    brep = dot(b_ref[0, 0].astype(BF), tile)
    gy_low = gy_ref[...].astype(BF)
    u_low = u_ref[...].astype(BF)
    gcs, gbs = [], []
    for pair in range(length // CHUNK // 2):
        gdts = dot(folded, q_ref[pair * spread : (pair + 1) * spread]) * LN2
        for k in (2 * pair, 2 * pair + 1):
            rows = slice(k * CHUNK, (k + 1) * CHUNK)
            deep = slice(k * spread, (k + 1) * spread)
            mix, dt_now, gy = mix_ref[0, 0, rows, :], dt_ref[rows, :cols], gin_ref[0, 0, rows, :]
            gs = gs_ref[deep]
            gu = dot((brep[rows] * own).astype(BF), gs)[:, :cols]
            gdt = gdts[(k % 2) * CHUNK : (k % 2 + 1) * CHUNK, :cols] + gu * mix
            gpre_ref[0, 0, rows, :] = gdt * jax.nn.sigmoid(pre_ref[0, 0, rows, :])
            gmix_ref[0, 0, rows, :] = gu * dt_now + skip_ref[...] * gy
            hs = hs_ref[k * spread + NST : (k + 1) * spread + NST]
            gcs.append((ntdot(gy_low[rows], hs) * own).astype(BF))
            gbs.append((ntdot(u_low[rows], gs) * own).astype(BF))
    gc_ref[0, 0] = ntdot(jnp.concatenate(gcs, axis=0), tile)
    gb_ref[0, 0] = ntdot(jnp.concatenate(gbs, axis=0), tile)

def scan_backward(pre, mix, gy, start, bt, ct, b, rate, skip):
    n, seqs, length, cols = pre.shape
    wide = -(-cols // 128) * 128
    at = lambda s, i: (n - 1 - i, s, 0, 0)
    big = lambda w: pl.BlockSpec((1, 1, length, w), at)
    whole = lambda r: pl.BlockSpec((r, cols), lambda s, i: (0, 0))
    turned = pl.BlockSpec((1, 1) + bt.shape[2:], lambda s, i: (n - 1 - i, s, 0, 0, 0))
    shape = lambda w: jax.ShapeDtypeStruct((n, seqs, length, w), F32)
    return pl.pallas_call(
        scan_bwd_kernel,
        grid=(seqs, n),
        in_specs=[
            big(cols), big(cols), big(cols), pl.BlockSpec((1, 1, NST, cols), at),
            turned, turned, big(NST), whole(NST), whole(1),
        ],
        out_specs=[big(cols), big(cols), big(NST), big(NST), whole(NST), whole(1)],
        out_shape=[
            shape(cols), shape(cols), shape(NST), shape(NST),
            jax.ShapeDtypeStruct((NST, cols), F32),
            jax.ShapeDtypeStruct((1, cols), F32),
        ],
        scratch_shapes=[
            pltpu.VMEM((NST, wide), F32),
            pltpu.VMEM((length, wide), F32),
            pltpu.VMEM((length, wide), F32),
            pltpu.VMEM((length, wide), F32),
            pltpu.VMEM((2 * NST, wide), F32),
            pltpu.VMEM((length * NST + NST, wide), BF),
            pltpu.VMEM((length * NST, wide), BF),
            pltpu.VMEM((length * NST // 2, wide), BF),
        ],
        compiler_params=pltpu.CompilerParams(vmem_limit_bytes=GIANT),
    )(pre, mix, gy, start, bt, ct, b, rate, skip)


def pick(ref, blocks, slots, slot):
    value = ref[0:blocks, 0, :, 0:HEAD].reshape(-1, HEAD)
    for other in range(1, slots):
        here = ref[0:blocks, 0, :, other * HEAD : (other + 1) * HEAD].reshape(-1, HEAD)
        value = jnp.where(slot == other, here, value)
    return value


def masked_scores(queries, keys, first, length):
    scores = ntdot(queries, keys)
    rows = first + lax.broadcasted_iota(jnp.int32, (scores.shape[0], 1), 0)
    bound = jnp.minimum(rows, length - 1)
    return jnp.where(lax.broadcasted_iota(jnp.int32, scores.shape, 1) <= bound, scores, NEGATIVE)


def attn_fwd_kernel(slot_ref, len_ref, q_ref, k_ref, v_ref, out_ref, lse_ref):
    n, _, length, width = q_ref.shape
    heads, slots = width // HEAD, k_ref.shape[3] // HEAD
    group = 2
    seq_length = len_ref[pl.program_id(0)]
    for i in range(n // group):
        at = slice(i * group, (i + 1) * group)
        for j in range(heads):
            lanes = slice(j * HEAD, (j + 1) * HEAD)
            blocks = (i + 1) * group
            queries = q_ref[at, 0, :, lanes].reshape(group * length, HEAD) * HEAD ** (-0.5)
            keys = pick(k_ref, blocks, slots, slot_ref[j])
            values = pick(v_ref, blocks, slots, slot_ref[j])
            scores = masked_scores(queries.astype(BF), keys, i * group * length, seq_length)
            top = jnp.max(scores, axis=1, keepdims=True)
            probs = jnp.exp(scores - top)
            total = jnp.sum(probs, axis=1, keepdims=True)
            mixed = dot(probs.astype(BF), values) * (slot_ref[heads + j].astype(F32) / total)
            out_ref[at, 0, :, lanes] = mixed.reshape(group, length, HEAD)
            lse_ref[at, 0, :, j : j + 1] = (top + jnp.log(total)).reshape(group, length, 1)


def attn_forward(slot, lengths, q, k, v):
    n, seqs, length, width = q.shape
    big = lambda w: pl.BlockSpec((n, 1, length, w), lambda s: (0, s, 0, 0))
    smem = pl.BlockSpec(memory_space=pltpu.SMEM)
    return pl.pallas_call(
        attn_fwd_kernel,
        grid=(seqs,),
        in_specs=[smem, smem, big(width), big(k.shape[3]), big(k.shape[3])],
        out_specs=[big(width), big(width // HEAD)],
        out_shape=[
            jax.ShapeDtypeStruct(q.shape, F32),
            jax.ShapeDtypeStruct((n, seqs, length, width // HEAD), F32),
        ],
        compiler_params=pltpu.CompilerParams(vmem_limit_bytes=GIANT),
    )(slot, lengths, q, k, v)


def attn_bwd_kernel(slot_ref, len_ref, q_ref, k_ref, v_ref, gh_ref, att_ref, lse_ref,
                    gq_ref, gk_ref, gv_ref, gk_acc, gv_acc):
    n, _, length, width = q_ref.shape
    heads, slots = width // HEAD, k_ref.shape[3] // HEAD
    group = 2
    seq_length = len_ref[pl.program_id(0)]
    gk_acc[...] = jnp.zeros_like(gk_acc)
    gv_acc[...] = jnp.zeros_like(gv_acc)
    for i in range(n // group):
        at = slice(i * group, (i + 1) * group)
        blocks = (i + 1) * group
        for j in range(heads):
            lanes = slice(j * HEAD, (j + 1) * HEAD)
            slot = slot_ref[j]
            queries = q_ref[at, 0, :, lanes].reshape(group * length, HEAD) * HEAD ** (-0.5)
            queries = queries.astype(BF)
            keys = pick(k_ref, blocks, slots, slot)
            values = pick(v_ref, blocks, slots, slot)
            grad = gh_ref[at, 0, :, lanes].reshape(group * length, HEAD)
            attended = att_ref[at, 0, :, lanes].reshape(group * length, HEAD)
            delta = jnp.sum(grad.astype(F32) * attended, axis=1, keepdims=True)
            lse = lse_ref[at, 0, :, j : j + 1].reshape(group * length, 1)
            scores = masked_scores(queries, keys, i * group * length, seq_length)
            probs = jnp.exp(scores - lse)
            grad_scores = (probs * (ntdot(grad, values) - delta)).astype(BF)
            gq = dot(grad_scores, keys) * HEAD ** (-0.5)
            gq_ref[at, 0, :, lanes] = gq.astype(BF).reshape(group, length, HEAD)
            rows = slice(0, blocks * length)
            gk_acc[slot, rows] += tndot(grad_scores, queries)
            gv_acc[slot, rows] += tndot(probs.astype(BF), grad)
    for other in range(slots):
        lanes = slice(other * HEAD, (other + 1) * HEAD)
        gk_ref[:, 0, :, lanes] = gk_acc[other].astype(BF).reshape(n, length, HEAD)
        gv_ref[:, 0, :, lanes] = gv_acc[other].astype(BF).reshape(n, length, HEAD)


def attn_backward(slot, lengths, q, k, v, gh, att, lse):
    n, seqs, length, width = q.shape
    big = lambda w: pl.BlockSpec((n, 1, length, w), lambda s: (0, s, 0, 0))
    smem = pl.BlockSpec(memory_space=pltpu.SMEM)
    kw = k.shape[3]
    return pl.pallas_call(
        attn_bwd_kernel,
        grid=(seqs,),
        in_specs=[smem, smem, big(width), big(kw), big(kw), big(width), big(width), big(width // HEAD)],
        out_specs=[big(width), big(kw), big(kw)],
        out_shape=[jax.ShapeDtypeStruct(x.shape, BF) for x in (q, k, v)],
        scratch_shapes=[pltpu.VMEM((kw // HEAD, n * length, HEAD), F32)] * 2,
        compiler_params=pltpu.CompilerParams(vmem_limit_bytes=GIANT),
    )(slot, lengths, q, k, v, gh, att, lse)


def greet(peers, axis="seq"):
    barrier = pltpu.get_barrier_semaphore()
    for peer in peers:
        pl.semaphore_signal(barrier, inc=1, device_id={axis: peer}, device_id_type=MESH)
    pl.semaphore_wait(barrier, len(peers))

def send(src, dst, send_sem, recv_sem, peer, axis="seq"):
    return pltpu.make_async_remote_copy(src_ref=src, dst_ref=dst, send_sem=send_sem, recv_sem=recv_sem,
        device_id={axis: peer}, device_id_type=MESH)

def ag_parts(n, x_ref, o_ref, local_sem, far_send, far_recv, near_send, near_recv):
    me = lax.axis_index("seq")
    core, chip, chips = me % 2, me // 2, n // 2
    sib = me + 1 - 2 * core
    far = [((chip + d) % chips) * 2 + core for d in range(1, chips)]
    mine = pltpu.make_async_copy(x_ref, o_ref.at[me], local_sem)
    out = [
        send(x_ref, o_ref.at[me], far_send.at[d], far_recv.at[d], far[d - 1]) for d in range(1, chips)
    ]
    near = [send(x_ref, o_ref.at[me], near_send.at[0], near_recv.at[0], sib)]

    def begin():
        for c in [mine] + out + near:
            c.start()

    def finish():
        for d in range(1, chips):
            out[d - 1].wait_recv()
            block = ((chip + chips - d) % chips) * 2 + core
            c = send(o_ref.at[block], o_ref.at[block], near_send.at[d], near_recv.at[d], sib)
            c.start()
            near.append(c)
        mine.wait()
        for c in near:
            c.wait()
        for c in out:
            c.wait_send()

    return begin, finish


def ag_kernel(n, x_ref, o_ref, *sems):
    me = lax.axis_index("seq")
    core, chip, chips = me % 2, me // 2, n // 2
    greet([me + 1 - 2 * core] + [((chip + d) % chips) * 2 + core for d in range(1, chips)])
    begin, finish = ag_parts(n, x_ref, o_ref, *sems)
    begin()
    finish()


def all_gather_any(x, n, cid):
    chips = n // 2
    return pl.pallas_call(functools.partial(ag_kernel, n),
        out_shape=jax.ShapeDtypeStruct((n,) + x.shape, x.dtype),
        in_specs=[pl.BlockSpec(memory_space=pl.ANY)],
        out_specs=pl.BlockSpec(memory_space=pl.ANY),
        scratch_shapes=[pltpu.SemaphoreType.DMA] + [pltpu.SemaphoreType.DMA((chips,))] * 4,
        compiler_params=pltpu.CompilerParams(collective_id=cid, has_side_effects=True),
    )(x)

def rs_kernel(n, p_ref, after_ref, o_ref, own, near, sums, got, local_sem, near_send, near_recv, far_send, far_recv):
    me = lax.axis_index("seq")
    core, chip, chips = me % 2, me // 2, n // 2
    sib = me + 1 - 2 * core
    step = lambda d: (chip + d) % chips
    far = [step(d) * 2 + core for d in range(1, chips)]
    greet([sib] + far)
    order = list(range(1, chips)) + [0]
    loads, nears, fars = {}, {}, {}
    for d in order:
        nears[d] = send(p_ref.at[step(d) * 2 + 1 - core], near.at[d], near_send.at[d], near_recv.at[d], sib)
        nears[d].start()
        loads[d] = pltpu.make_async_copy(p_ref.at[step(d) * 2 + core], own.at[d], local_sem.at[d])
        loads[d].start()
    rows = own.shape[1]
    slab = 16
    def each(body):
        def run(i, _):
            body(pl.ds(pl.multiple_of(i * slab, slab), slab))
            return 0
        lax.fori_loop(0, rows // slab, run, 0, unroll=2)
    for d in order:
        loads[d].wait()
        nears[d].wait_recv()
        if d:
            def add(at):
                sums[d - 1, at] = (own[d, at].astype(F32) + near[d, at].astype(F32)).astype(BF)
            each(add)
            fars[d] = send(sums.at[d - 1], got.at[d - 1], far_send.at[d - 1], far_recv.at[d - 1], far[d - 1])
            fars[d].start()
        else:
            def add(at):
                o_ref[at] = own[0, at].astype(F32) + near[0, at].astype(F32)
            each(add)
    for d in range(1, chips):
        fars[d].wait_recv()
        def add(at):
            o_ref[at] = o_ref[at] + got[d - 1, at].astype(F32)
        each(add)
    for d in order:
        nears[d].wait_send()
        if d: fars[d].wait_send()

def reduce_scatter_any(p, after, n, cid):
    chips = n // 2
    blk = p.shape[1:]
    return pl.pallas_call(functools.partial(rs_kernel, n),
        out_shape=jax.ShapeDtypeStruct(blk, F32),
        in_specs=[pl.BlockSpec(memory_space=pl.ANY)] * 2,
        out_specs=pl.BlockSpec(memory_space=pltpu.VMEM),
        scratch_shapes=[pltpu.VMEM((chips,) + blk, p.dtype), pltpu.VMEM((chips,) + blk, p.dtype),
            pltpu.VMEM((chips-1,) + blk, p.dtype), pltpu.VMEM((chips-1,) + blk, p.dtype),
            pltpu.SemaphoreType.DMA((chips,)), pltpu.SemaphoreType.DMA((chips,)), pltpu.SemaphoreType.DMA((chips,)),
            pltpu.SemaphoreType.DMA((chips-1,)), pltpu.SemaphoreType.DMA((chips-1,))],
        compiler_params=pltpu.CompilerParams(collective_id=cid, has_side_effects=True, vmem_limit_bytes=GIANT),
    )(p, after)

def stat_kernel(n, axis, x_ref, o_ref, got, send_sem, recv_sem):
    me = lax.axis_index(axis)
    peers = [(me + d) % n for d in range(1, n)]
    greet(peers, axis)
    copies = []
    for d in range(1, n):
        c = send(x_ref, got.at[d - 1], send_sem.at[d - 1], recv_sem.at[d - 1], peers[d - 1], axis)
        c.start()
        copies.append(c)
    total = x_ref[...]
    for d in range(1, n):
        copies[d - 1].wait_recv()
        total = total + got[d - 1]
    o_ref[...] = total
    for c in copies:
        c.wait_send()


def small_sum(x, n, cid, axis="seq"):
    return pl.pallas_call(
        functools.partial(stat_kernel, n, axis),
        out_shape=jax.ShapeDtypeStruct(x.shape, F32),
        in_specs=[pl.BlockSpec(memory_space=pltpu.VMEM)],
        out_specs=pl.BlockSpec(memory_space=pltpu.VMEM),
        scratch_shapes=[pltpu.VMEM((n - 1,) + x.shape, F32)] + [pltpu.SemaphoreType.DMA((n - 1,))] * 2,
        compiler_params=pltpu.CompilerParams(collective_id=cid, has_side_effects=True, vmem_limit_bytes=GIANT),
    )(x)


def square(me):
    core, x, y = me % 2, (me // 2) % 2, me // 4
    seat = lambda yy, xx, cc: (yy * 2 + xx) * 2 + cc
    return core, (seat(y, x, 1 - core), seat(y, 1 - x, core), seat(1 - y, x, core), seat(1 - y, 1 - x, core))

def ag4_parts(n, x_ref, o_ref, local_sem, far_send, far_recv, near_send, near_recv):
    me = lax.axis_index("seq")
    core, (sib, east, north, across) = square(me)
    half = x_ref.shape[0] // 2
    cut = (pl.ds(0, half), pl.ds(half, half))
    mine = pltpu.make_async_copy(x_ref, o_ref.at[me], local_sem)
    far, near = {}, []
    for slot, h, peer in ((0, 0, east), (2, 1, north), (1, 1, east), (3, 0, north)):
        far[slot] = send(x_ref.at[cut[h]], o_ref.at[me, cut[h]], far_send.at[slot], far_recv.at[slot], peer)
    near.append(send(x_ref, o_ref.at[me], near_send.at[6], near_recv.at[6], sib))

    def begin():
        mine.start()
        for slot in (0, 2, 1, 3):
            far[slot].start()
        near[0].start()

    def pass_on(slot, block, h):
        ref = o_ref.at[block, cut[h]]
        c = send(ref, ref, near_send.at[slot], near_recv.at[slot], sib)
        c.start()
        near.append(c)

    def finish():
        for slot, block, h, relay, to in (
            (0, east, 0, 4, north), (2, north, 1, 5, east), (1, east, 1, None, None), (3, north, 0, None, None)
        ):
            far[slot].wait_recv()
            if relay is not None:
                ref = o_ref.at[block, cut[h]]
                far[relay] = send(ref, ref, far_send.at[relay], far_recv.at[relay], to)
                far[relay].start()
            pass_on(slot, block, h)
        for slot, h in ((4, 0), (5, 1)):
            far[slot].wait_recv()
            pass_on(slot, across, h)
        mine.wait()
        for c in near:
            c.wait()
        for c in far.values():
            c.wait_send()

    return begin, finish


def ag4_kernel(x_ref, o_ref, *sems):
    core, (sib, east, north, across) = square(lax.axis_index("seq"))
    greet([sib, east, north])
    begin, finish = ag4_parts(8, x_ref, o_ref, *sems)
    begin()
    finish()


def all_gather4(x, n, cid):
    return pl.pallas_call(ag4_kernel,
        out_shape=jax.ShapeDtypeStruct((n,) + x.shape, x.dtype),
        in_specs=[pl.BlockSpec(memory_space=pl.ANY)],
        out_specs=pl.BlockSpec(memory_space=pl.ANY),
        scratch_shapes=[pltpu.SemaphoreType.DMA] + [pltpu.SemaphoreType.DMA((6,))] * 2 + [pltpu.SemaphoreType.DMA((7,))] * 2,
        compiler_params=pltpu.CompilerParams(collective_id=cid, has_side_effects=True),
    )(x)

def rs4_kernel(p_ref, after_ref, o_ref, own, near, got, local_sem, near_send, near_recv, far_send, far_recv):
    me = lax.axis_index("seq")
    core, (sib, east, north, across) = square(me)
    greet([sib, east, north])
    rows = own.shape[1]
    half = rows // 2
    cut = (pl.ds(0, half), pl.ds(half, half))
    seats = (across, east, north, me)
    loads, nears, far = [], [], {}
    for i, seat in enumerate(seats):
        other = seat + 1 - 2 * core
        c = send(p_ref.at[other], near.at[i], near_send.at[i], near_recv.at[i], sib)
        c.start(); nears.append(c)
        c = pltpu.make_async_copy(p_ref.at[seat], own.at[i], local_sem.at[i])
        c.start(); loads.append(c)
    slab = 16
    def each(first, count, body):
        def run(i, _):
            body(pl.ds(pl.multiple_of(first + i * slab, slab), slab), pl.ds(pl.multiple_of(i * slab, slab), slab))
            return 0
        lax.fori_loop(0, count // slab, run, 0, unroll=2)
    def fold(i):
        loads[i].wait(); nears[i].wait_recv()
        def add(at, _):
            own[i, at] = (own[i, at].astype(F32) + near[i, at].astype(F32)).astype(own.dtype)
        each(0, rows, add)
    def go(slot, i, h, peer):
        far[slot] = send(own.at[i, cut[h]], got.at[slot], far_send.at[slot], far_recv.at[slot], peer)
        far[slot].start()
    fold(0)
    go(0, 0, 0, east)
    go(1, 0, 1, north)
    fold(1)
    go(2, 1, 0, east)
    fold(2)
    go(3, 2, 1, north)
    def join(i, h, slot):
        far[slot].wait_recv()
        def add(at, src):
            own[i, at] = (own[i, at].astype(F32) + got[slot, src].astype(F32)).astype(own.dtype)
        each(h * half, half, add)
    join(2, 0, 0)
    go(4, 2, 0, north)
    join(1, 1, 1)
    go(5, 1, 1, east)
    loads[3].wait(); nears[3].wait_recv()
    def first(h, slot):
        far[slot].wait_recv()
        def add(at, src):
            o_ref[at] = own[3, at].astype(F32) + near[3, at].astype(F32) + got[slot, src].astype(F32)
        each(h * half, half, add)
    first(0, 2)
    first(1, 3)
    def last(h, slot):
        far[slot].wait_recv()
        def add(at, src):
            o_ref[at] = o_ref[at] + got[slot, src].astype(F32)
        each(h * half, half, add)
    last(0, 4)
    last(1, 5)
    for c in nears: c.wait_send()
    for c in far.values(): c.wait_send()

def reduce_scatter4(p, after, n, cid):
    blk = p.shape[1:]
    return pl.pallas_call(rs4_kernel,
        out_shape=jax.ShapeDtypeStruct(blk, F32),
        in_specs=[pl.BlockSpec(memory_space=pl.ANY)] * 2,
        out_specs=pl.BlockSpec(memory_space=pltpu.VMEM),
        scratch_shapes=[pltpu.VMEM((4,) + blk, p.dtype), pltpu.VMEM((4,) + blk, p.dtype),
            pltpu.VMEM((6, blk[0] // 2) + blk[1:], p.dtype)] + [pltpu.SemaphoreType.DMA((4,))] * 3 + [pltpu.SemaphoreType.DMA((6,))] * 2,
        compiler_params=pltpu.CompilerParams(collective_id=cid, has_side_effects=True, vmem_limit_bytes=GIANT),
    )(p, after)


def start_kernel(n, x_ref, w_ref, o_ref, c_ref, swap_sem, swap_send, swap_recv, *sems):
    me = lax.axis_index("seq")
    others = [(me + d) % n for d in range(1, n)]
    greet(others)
    own = pltpu.make_async_copy(w_ref.at[me], c_ref.at[me], swap_sem)
    own.start()
    gather_start, gather_end = (ag4_parts if n == 8 else ag_parts)(n, x_ref, o_ref, *sems)
    gather_start()
    swaps = []
    for d in range(1, n):
        c = send(w_ref.at[others[d - 1]], c_ref.at[me], swap_send.at[d - 1], swap_recv.at[d - 1], others[d - 1])
        c.start()
        swaps.append(c)
    gather_end()
    own.wait()
    for c in swaps:
        c.wait()


def gather_and_exchange(x, w, n, cid):
    chips = n // 2
    far, near = (6, 7) if n == 8 else (chips, chips)
    anywhere = pl.BlockSpec(memory_space=pl.ANY)
    dma = pltpu.SemaphoreType.DMA
    return pl.pallas_call(
        functools.partial(start_kernel, n),
        out_shape=[jax.ShapeDtypeStruct((n,) + x.shape, x.dtype), jax.ShapeDtypeStruct(w.shape, w.dtype)],
        in_specs=[anywhere] * 2,
        out_specs=[anywhere] * 2,
        scratch_shapes=[dma, dma((n - 1,)), dma((n - 1,)), dma, dma((far,)), dma((far,)), dma((near,)), dma((near,))],
        compiler_params=pltpu.CompilerParams(collective_id=cid, has_side_effects=True),
    )(x, w)


def all_gather(x, n, cid):
    return (all_gather4 if n == 8 else all_gather_any)(x, n, cid)


def reduce_scatter(p, n, cid, after=None):
    after = jnp.zeros((8, 128), F32) if after is None else after
    return (reduce_scatter4 if n == 8 else reduce_scatter_any)(p, after, n, cid)


def mm_rs4_kernel(turned, *refs):
    terms = len(turned)
    a_refs, b_refs = refs[:terms], refs[terms : 2 * terms]
    after_ref, o_ref, part, near, got, near_send, near_recv, far_send, far_recv = refs[2 * terms :]
    me = lax.axis_index("seq")
    core, (sib, east, north, across) = square(me)
    x, y = (me // 2) % 2, me // 4
    greet([sib, east, north])
    rows = part.shape[2]
    half = rows // 2
    cut = (pl.ds(0, half), pl.ds(half, half))
    slab = 16
    own = part.at[1]

    def near_copy(i):
        return send(part.at[0, i], near.at[i], near_send.at[i], near_recv.at[i], sib)

    hops = ((0, 0, east), (0, 1, north), (1, 0, east), (2, 1, north), (2, 0, north), (1, 1, east))

    def far_copy(slot):
        i, h, peer = hops[slot]
        return send(own.at[i, cut[h]], got.at[slot], far_send.at[slot], far_recv.at[slot], peer)

    def each(first, count, body):
        def run(i, _):
            at = pl.multiple_of(i * slab, slab)
            body(pl.ds(pl.multiple_of(first + at, slab), slab), pl.ds(at, slab))
            return 0

        lax.fori_loop(0, count // slab, run, 0, unroll=2)

    def fold(i):
        near_copy(i).wait_recv()

        def add(at, _):
            own[i, at] = (own[i, at].astype(F32) + near[i, at].astype(F32)).astype(BF)

        each(0, rows, add)

    def step(s, _):
        i, mine = s // 2, s % 2
        yy, xx = (y + (i + 1) % 2) % 2, (x + 1 - i // 2) % 2
        seat = (yy * 2 + xx) * 2 + (core + 1 - mine) % 2
        total = None
        for a, b, t in zip(a_refs, b_refs, turned):
            term = (ntdot if t else dot)(a[seat], b[...])
            total = term if total is None else total + term
        part[mine, i] = total.astype(BF)

        @pl.when(mine == 0)
        def _():
            near_copy(i).start()

        @pl.when(s == 3)
        def _():
            fold(0)
            far_copy(0).start()
            far_copy(1).start()

        @pl.when(s == 5)
        def _():
            fold(1)
            far_copy(2).start()

        @pl.when(s == 6)
        def _():
            fold(2)
            far_copy(3).start()

        return 0

    lax.fori_loop(0, 8, step, 0)

    def join(i, h, slot):
        far_copy(slot).wait_recv()

        def add(at, src):
            own[i, at] = (own[i, at].astype(F32) + got[slot, src].astype(F32)).astype(BF)

        each(h * half, half, add)

    join(2, 0, 0)
    far_copy(4).start()
    join(1, 1, 1)
    far_copy(5).start()
    near_copy(3).wait_recv()

    def first(h, slot):
        far_copy(slot).wait_recv()

        def add(at, src):
            o_ref[at] = own[3, at].astype(F32) + near[3, at].astype(F32) + got[slot, src].astype(F32)

        each(h * half, half, add)

    first(0, 2)
    first(1, 3)

    def last(h, slot):
        far_copy(slot).wait_recv()

        def add(at, src):
            o_ref[at] = o_ref[at] + got[slot, src].astype(F32)

        each(h * half, half, add)

    last(0, 4)
    last(1, 5)
    for i in range(4):
        near_copy(i).wait_send()
    for slot in range(6):
        far_copy(slot).wait_send()


def product_scatter(pairs, n, cid, after=None):
    after = jnp.zeros((8, 128), F32) if after is None else after
    rows = pairs[0][0].shape[0] // n
    cols = pairs[0][1].shape[0 if pairs[0][2] else 1]
    if n != 8:
        total = sum((ntdot if t else dot)(a, b) for a, b, t in pairs)
        return reduce_scatter(total.astype(BF).reshape(n, rows, cols), n, cid, after)
    vmem = pl.BlockSpec(memory_space=pltpu.VMEM)
    dma = pltpu.SemaphoreType.DMA
    return pl.pallas_call(
        functools.partial(mm_rs4_kernel, tuple(t for _, _, t in pairs)),
        out_shape=jax.ShapeDtypeStruct((rows, cols), F32),
        in_specs=[vmem] * (2 * len(pairs)) + [pl.BlockSpec(memory_space=pl.ANY)],
        out_specs=vmem,
        scratch_shapes=[
            pltpu.VMEM((2, 4, rows, cols), BF),
            pltpu.VMEM((4, rows, cols), BF),
            pltpu.VMEM((6, rows // 2, cols), BF),
            dma((4,)), dma((4,)), dma((6,)), dma((6,)),
        ],
        compiler_params=pltpu.CompilerParams(collective_id=cid, has_side_effects=True, vmem_limit_bytes=GIANT),
    )(*(a.reshape(n, rows, a.shape[1]) for a, _, _ in pairs), *(b for _, b, _ in pairs), after)


class HeadPlan:
    def __init__(self, n):
        self.n = n
        self.per = -(-HEADS // n)
        group = HEADS // KVH
        self.first_kv, self.slots = [], 1
        for i in range(n):
            low, high = i * self.per, min((i + 1) * self.per, HEADS) - 1
            if low >= HEADS:
                self.first_kv.append(KVH)
            else:
                self.first_kv.append(low // group)
                self.slots = max(self.slots, high // group - low // group + 1)
        self.width = self.per * HEAD
        self.kv_width = self.slots * HEAD

    def head_table(self):
        group = HEADS // KVH
        rows = []
        for i in range(self.n):
            heads = [i * self.per + j for j in range(self.per)]
            rows.append(
                [h // group - self.first_kv[i] if h < HEADS else 0 for h in heads]
                + [int(h < HEADS) for h in heads]
            )
        return jnp.array(rows, jnp.int32)

    def kv_used(self, i):
        group = HEADS // KVH
        heads = range(i * self.per, min((i + 1) * self.per, HEADS))
        return sorted({h // group for h in heads})

    def split_columns(self, w):
        rows = w.shape[0]
        q = jnp.pad(w[:, : HEADS * HEAD], ((0, 0), (0, self.n * self.width - HEADS * HEAD)))
        parts = []
        for i in range(self.n):
            pieces = [q[:, i * self.width : (i + 1) * self.width]]
            for kind in range(2):
                start = HEADS * HEAD + kind * KVH * HEAD
                used = self.kv_used(i)
                for slot in range(self.slots):
                    g = self.first_kv[i] + slot
                    if g in used:
                        pieces.append(w[:, start + g * HEAD : start + (g + 1) * HEAD])
                    else:
                        pieces.append(jnp.zeros((rows, HEAD), w.dtype))
            parts.append(jnp.concatenate(pieces, axis=1))
        return jnp.stack(parts)

    def join_columns(self, g):
        q = [g[i, :, : self.width] for i in range(self.n)]
        q = jnp.concatenate(q, axis=1)[:, : HEADS * HEAD].astype(F32)
        kv = []
        for kind in range(2):
            for head in range(KVH):
                total = 0.0
                for i in range(self.n):
                    if head in self.kv_used(i):
                        at = self.width + kind * self.kv_width + (head - self.first_kv[i]) * HEAD
                        total = total + g[i, :, at : at + HEAD].astype(F32)
                kv.append(total)
        return jnp.concatenate([q] + kv, axis=1)


def reblock(rows, have, want, total):
    n, me = lax.axis_size("seq"), lax.axis_index("seq")
    result = jnp.zeros((want,) + rows.shape[1:], rows.dtype)
    pad = jnp.pad(rows, ((want, want), (0, 0)))
    for shift in range(-(n - 1), n):
        pairs = []
        for i in range(n):
            j = i + shift
            if 0 <= j < n:
                low = max(i * have, j * want)
                high = min((i + 1) * have, (j + 1) * want, total)
                if low < high:
                    pairs.append((i, j))
        if not pairs:
            continue
        start = want + (me + shift) * want - me * have
        piece = lax.dynamic_slice_in_dim(pad, jnp.clip(start, 0, have + want), want, 0)
        if shift:
            piece = lax.ppermute(piece, "seq", pairs)
        else:
            ok = jnp.array([(i, i) in pairs for i in range(n)])[me]
            piece = jnp.where(ok, piece, jnp.zeros_like(piece))
        result = result + piece
    return result


def per_device(tokens, lengths, cotangent, w_qkv, w_ao, w_in, w_xp, w_dt, w_so, w_gu, w_down,
               norm_in, norm_attn, norm_ssm, norm_ffn, conv_w, conv_b, dt_bias, a_log, d_skip):
    seqs, slot_len, width = tokens.shape
    n, me, replicas = lax.axis_size("seq"), lax.axis_index("seq"), lax.axis_size("dp")
    local, rows = seqs * slot_len, seqs * slot_len * n
    cols = INNER // n
    plan = HeadPlan(n)
    w_rows, ao_rows = w_qkv.shape[0], w_ao.shape[0]
    pos = me * slot_len + jnp.arange(slot_len, dtype=jnp.int32)
    is_valid = pos[None, :] < lengths[:, None]
    table = plan.head_table()[me]
    tie = lax.optimization_barrier
    flat = lambda v: v.reshape(rows, v.shape[-1])
    gather = lambda v, cid: flat(all_gather(v, n, cid))
    scatter = lambda v, cid, after=None: reduce_scatter(
        v.astype(BF).reshape(n, local, v.shape[-1]), n, cid, after
    )
    later = lambda g, zero: g + zero.astype(g.dtype)
    exchange = lambda v: lax.all_to_all(v, "seq", 0, 0, tiled=True)
    blocks = lambda v: v.reshape(n, seqs, slot_len, v.shape[-1])
    mine = lambda v: lax.dynamic_slice_in_dim(v, me * cols, cols, v.ndim - 1)
    over = lambda g: lax.psum(g, "dp")

    def row_sums(a, b, cid):
        both = jnp.stack([a, b]).reshape(-1, 128)
        return small_sum(both, n, cid).reshape(2, rows)

    wdt = mine(w_dt)
    taps, bias, dtb, skip = mine(conv_w), mine(conv_b), mine(dt_bias), mine(d_skip)
    rate = -jnp.exp(mine(a_log))
    ssm_gain = mine(norm_ssm)
    attn_gain = lax.dynamic_slice_in_dim(
        jnp.pad(norm_attn, (0, n * plan.width - HEADS * HEAD)), me * plan.width, plan.width, 0
    )

    x = tokens.astype(F32).reshape(local, width)
    scale_in = lax.rsqrt(jnp.mean(x * x, axis=-1, keepdims=True) + EPSILON)
    normed, qkv_cols = gather_and_exchange(
        (x * scale_in * norm_in).astype(BF), plan.split_columns(w_qkv), n, 1
    )
    normed, qkv_cols = flat(normed), qkv_cols.reshape(n * w_rows, -1)
    qkv = dot(normed, qkv_cols).astype(BF)
    behind = 0.0 * normed[0, 0].astype(F32)
    in_parts = later(jnp.transpose(w_in.reshape(w_rows, 2, n, cols), (1, 2, 0, 3)), behind)
    wx = exchange(in_parts[0]).reshape(n * w_rows, cols)
    wz = exchange(in_parts[1]).reshape(n * w_rows, cols)
    behind = 0.0 * qkv[0, 0].astype(F32)
    ao_all = lax.all_gather(later(w_ao, behind), "seq", axis=0, tiled=True)
    ao_mine = lax.dynamic_slice_in_dim(
        jnp.pad(ao_all, ((0, n * plan.width - HEADS * HEAD), (0, 0))), me * plan.width, plan.width, 0
    )
    upstream = (cotangent.astype(F32) * is_valid[..., None]).reshape(local, width)
    upstream_all = lax.all_gather(later(upstream.astype(BF), behind), "seq", axis=0, tiled=True)
    q = blocks(qkv[:, : plan.width])
    k = blocks(qkv[:, plan.width : plan.width + plan.kv_width])
    v = blocks(qkv[:, plan.width + plan.kv_width :])
    attended, lse = attn_forward(table, lengths, q, k, v)
    attended_rows = flat(attended)

    x_conv = blocks(dot(normed, wx).astype(BF))
    z_gate = dot(normed, wz)
    edge = KCONV - 1
    before = jnp.concatenate(
        [jnp.zeros((1, seqs, edge, cols), BF), x_conv[:-1, :, slot_len - edge :]], axis=0
    )
    padded = jnp.concatenate([before, x_conv], axis=2).astype(F32)
    conv_pre = bias + sum(taps[o] * padded[:, :, o : o + slot_len] for o in range(KCONV))
    mixer_in = jax.nn.silu(conv_pre)
    mixer_low = flat(mixer_in).astype(BF)
    projected = lax.psum(dot(mixer_low, w_xp), "seq")
    step_low = projected[:, :DTR].astype(BF)
    b_input, c_output = projected[:, DTR : DTR + NST], projected[:, DTR + NST :]
    step_pre = blocks(dot(step_low, wdt) + dtb)
    turn = lambda m: jnp.swapaxes(m.reshape(n, seqs, slot_len // CHUNK, CHUNK, NST), 3, 4)
    bt, ct = turn(b_input), turn(c_output)
    core, start = scan_forward(step_pre, mixer_in, bt, blocks(c_output), rate, skip[None])
    core = flat(core)
    gated = core * jax.nn.silu(z_gate)
    squares = row_sums(
        jnp.sum(attended_rows * attended_rows, axis=1), jnp.sum(gated * gated, axis=1), 2
    )
    r_attn = lax.rsqrt(squares[0] / (HEADS * HEAD) + EPSILON)[:, None]
    r_ssm = lax.rsqrt(squares[1] / INNER + EPSILON)[:, None]
    attn_low = (attended_rows * r_attn * attn_gain).astype(BF)
    ssm_low = (gated * r_ssm * ssm_gain).astype(BF)
    mixed = product_scatter(((attn_low, ao_mine, False), (ssm_low, w_so, False)), n, 3)
    residual = x + 0.5 * mixed
    r_ffn = lax.rsqrt(jnp.mean(residual * residual, axis=-1, keepdims=True) + EPSILON)
    normed_two = gather((residual * r_ffn * norm_ffn).astype(BF), 4)
    w_gate, w_up = w_gu[:, 0], w_gu[:, 1]
    gate, up = dot(normed_two, w_gate), dot(normed_two, w_up)
    activated = (jax.nn.silu(gate) * up).astype(BF)

    grad_act = ntdot(upstream_all, w_down)
    grad_gate = (grad_act * up * silu_grad(gate)).astype(BF)
    grad_up = (grad_act * jax.nn.silu(gate)).astype(BF)
    g_down = tndot(activated, upstream_all).astype(BF)
    g_gate, g_up = tndot(normed_two, grad_gate).astype(BF), tndot(normed_two, grad_up).astype(BF)
    s_down, s_gate, s_up = over((g_down, g_gate, g_up))
    grad_two = product_scatter(((grad_gate, w_gate, True), (grad_up, w_up, True)), n, 5)
    def norm_pull(grad, values, r, gain):
        dotted = jnp.mean(grad * gain * values, axis=-1, keepdims=True)
        return r * (grad * gain - values * (r * r * dotted)), jnp.sum(grad * values * r, axis=0)

    add, g_norm_ffn = norm_pull(grad_two, residual, r_ffn, norm_ffn)
    grad_residual = upstream + add
    mix_low = gather(grad_residual.astype(BF), 7)
    d_attn = 0.5 * ntdot(mix_low, ao_mine)
    d_ssm = 0.5 * ntdot(mix_low, w_so)
    inner = row_sums(
        jnp.sum(d_attn * attn_gain * attended_rows, axis=1),
        jnp.sum(d_ssm * ssm_gain * gated, axis=1),
        8,
    )
    t_attn = (inner[0] / (HEADS * HEAD))[:, None] * r_attn * r_attn
    t_ssm = (inner[1] / INNER)[:, None] * r_ssm * r_ssm
    grad_heads = (r_attn * (d_attn * attn_gain - attended_rows * t_attn)).astype(BF)
    grad_gated = r_ssm * (d_ssm * ssm_gain - gated * t_ssm)
    g_norm_attn = jnp.sum(d_attn * attended_rows * r_attn, axis=0)
    g_norm_ssm = jnp.sum(d_ssm * gated * r_ssm, axis=0)

    gq, gk, gv = attn_backward(table, lengths, q, k, v, blocks(grad_heads), attended, lse)
    grad_qkv = flat(jnp.concatenate([gq, gk, gv], axis=3))
    grad_core = grad_gated * jax.nn.silu(z_gate)
    grad_z = (grad_gated * core * silu_grad(z_gate)).astype(BF)
    g_ao = reblock((0.5 * tndot(attn_low, mix_low)).astype(BF), plan.width, ao_rows, HEADS * HEAD)
    g_so = (0.5 * tndot(ssm_low, mix_low)).astype(BF)
    g_z = exchange(tndot(normed, grad_z).astype(BF).reshape(n, w_rows, cols))
    g_qkv = exchange(tndot(normed, grad_qkv).astype(BF).reshape(n, w_rows, -1))
    g_qkv = plan.join_columns(g_qkv).astype(BF)
    grad_core, grad_z, grad_qkv = tie((grad_core, grad_z, grad_qkv))
    gpre, gmix, gb, gc, grate, gskip = scan_backward(
        step_pre, mixer_in, blocks(grad_core), start, bt, ct, blocks(b_input), rate, skip[None]
    )
    gpre = flat(gpre)
    nothing = lambda *sums: 0.0 * sum(g.reshape(-1)[0].astype(F32) for g in sums)
    after_one = nothing(s_down, s_gate, s_up, grate)
    s_ao, s_so, s_z, s_qkv = over(tuple(later(g, after_one) for g in (g_ao, g_so, g_z, g_qkv)))
    g_dt_bias = jnp.sum(gpre, axis=0)
    grad_step = gpre.astype(BF)
    grad_projected = jnp.concatenate([ntdot(grad_step, wdt), flat(gb), flat(gc)], axis=1)
    grad_projected = gather(scatter(grad_projected, 9, jnp.full((8, 128), after_one)).astype(BF), 10)
    grad_mixer = gmix + blocks(ntdot(grad_projected, w_xp))
    grad_conv = grad_mixer * silu_grad(conv_pre)
    g_conv_b = jnp.sum(grad_conv, axis=(0, 1, 2))
    g_conv_w = jnp.stack(
        [jnp.sum(grad_conv * padded[:, :, o : o + slot_len], axis=(0, 1, 2)) for o in range(KCONV)]
    )
    after = jnp.concatenate(
        [grad_conv[1:, :, :edge], jnp.zeros((1, seqs, edge, cols), F32)], axis=0
    )
    extended = jnp.concatenate([grad_conv, after], axis=2)
    grad_x = sum(taps[o] * extended[:, :, edge - o : edge - o + slot_len] for o in range(KCONV))
    grad_x = flat(grad_x).astype(BF)
    g_x = exchange(tndot(normed, grad_x).astype(BF).reshape(n, w_rows, cols))
    g_xp = tndot(mixer_low, grad_projected).astype(BF)
    g_wdt = tndot(step_low, grad_step).astype(BF)
    after_two = nothing(s_ao, s_so, s_z, s_qkv)
    s_x, s_xp, s_wdt = over(tuple(later(g, after_two) for g in (g_x, g_xp, g_wdt)))
    grad_normed = product_scatter(
        ((grad_x, wx, True), (grad_z, wz, True), (grad_qkv, qkv_cols, True)), n, 11, jnp.full((8, 128), after_two)
    )
    block_out = residual + product_scatter(((activated, w_down, False),), n, 6, grad_normed[:8, :128])
    add_in, g_norm_in = norm_pull(grad_normed, x, scale_in, norm_in)
    grad_tokens = grad_residual + add_in

    s_in = jnp.stack([s_x, s_z])
    s_in = jnp.transpose(s_in, (2, 0, 1, 3)).reshape(w_rows, 2 * INNER)
    s_gu = jnp.stack([s_gate, s_up], axis=1)

    place = lambda g: lax.dynamic_update_slice_in_dim(
        jnp.zeros((n * plan.width,), F32), g, me * plan.width, 0
    )[: HEADS * HEAD]

    def pad_rows(v):
        v = v.reshape(-1)
        return jnp.pad(v, (0, -v.size % 1024)).reshape(-1, 128)

    shared = jnp.stack([g_norm_in, place(g_norm_attn), g_norm_ffn])
    total = small_sum(pad_rows(shared), n, 12).reshape(-1)[: shared.size].reshape(shared.shape)
    shared = lax.dynamic_slice_in_dim(total, me * w_rows, w_rows, 1)
    owned = jnp.concatenate(
        [g_norm_ssm[None], g_conv_w, g_conv_b[None], g_dt_bias[None], grate * rate, gskip], axis=0
    )
    small = pad_rows(jnp.concatenate([shared.reshape(-1), owned.reshape(-1)]))
    small = small_sum(small, replicas, 13, "dp").reshape(-1)
    s_shared = small[: shared.size].reshape(shared.shape)
    s_owned = small[shared.size : shared.size + owned.size].reshape(owned.shape)
    full = lambda g: g.astype(F32)

    return (
        block_out.astype(BF).reshape(seqs, slot_len, width),
        grad_tokens.reshape(seqs, slot_len, width),
        full(s_qkv),
        full(s_ao),
        full(s_in),
        full(s_xp),
        full(s_wdt),
        full(s_so),
        full(s_gu),
        full(s_down),
        s_shared[0],
        s_shared[1],
        s_owned[0],
        s_shared[2],
        s_owned[1 : 1 + KCONV],
        s_owned[1 + KCONV],
        s_owned[2 + KCONV],
        s_owned[3 + KCONV : 3 + KCONV + NST],
        s_owned[3 + KCONV + NST],
    )


def solution(mesh):
    rows, cols, flat = P("seq", None), P(None, "seq"), P("seq")
    act = P("dp", "seq", None)
    hid = P(None, None, "seq")
    in_specs = (act, P("dp"), act, rows, rows, rows, rows, P(), rows, hid, rows) + (P(),) * 9
    out_specs = (act, act, rows, rows, rows, rows, cols, rows, hid, rows,
                 flat, flat, flat, flat, cols, flat, flat, cols, flat)
    return jax.shard_map(per_device, mesh=mesh, in_specs=in_specs, out_specs=out_specs, check_vma=False)
```

```python
import functools
import math

import jax
import jax.numpy as jnp
from jax import lax
from jax.experimental import pallas as pl
from jax.experimental.pallas import tpu as pltpu
from jax.sharding import PartitionSpec as P

HEADS = 25
HEAD = 64
KVH = 5
INNER = 3200
NST = 16
KCONV = 4
DTR = 100
EPSILON = 1e-05
NEGATIVE = -1e30
CHUNK = 16
LOG2E = math.log2(math.e)
LN2 = math.log(2.0)

BF = jnp.bfloat16
F32 = jnp.float32
NT = (((1,), (1,)), ((), ()))
TN = (((0,), (0,)), ((), ()))
GIANT = 60 * 1024 * 1024
MESH = pl.DeviceIdType.MESH


def ntdot(a, b):
    return lax.dot_general(a, b, NT, preferred_element_type=F32)


def tndot(a, b):
    return lax.dot_general(a, b, TN, preferred_element_type=F32)


def dot(a, b):
    return jnp.dot(a, b, preferred_element_type=F32)


def silu_grad(values):
    logistic = jax.nn.sigmoid(values)
    return logistic * (1.0 + values * (1.0 - logistic))


def chunk_masks():
    spread = NST * CHUNK
    row = lax.broadcasted_iota(jnp.int32, (CHUNK, spread), 0)
    col = lax.broadcasted_iota(jnp.int32, (CHUNK, spread), 1)
    own = (col // NST == row).astype(F32)
    tile = (col % NST == row).astype(BF)
    return own, tile


def turn_chunks(proj, bt_ref, ct_ref):
    turned = jnp.swapaxes(proj[:, : 8 * NST], 0, 1)
    for k in range(proj.shape[0] // CHUNK):
        at = slice(k * CHUNK, (k + 1) * CHUNK)
        bt_ref[k] = turned[:NST, at]
        if ct_ref is not None:
            ct_ref[k] = turned[NST : 2 * NST, at]


def scan_fwd_kernel(proj_ref, mix_ref, rows_ref, wz_ref, wdt_ref, dtb_ref, rate_ref, skip_ref,
                    core_ref, z_ref, sq_ref, start_ref, h_ref, dt_ref, u_ref, wide_ref, hs_ref, bt_ref):
    length, cols = mix_ref.shape[2:]
    own, tile = chunk_masks()

    @pl.when(pl.program_id(1) == 0)
    def _():
        for ref in (h_ref, dt_ref, u_ref, wide_ref):
            ref[...] = jnp.zeros_like(ref)
        wide_ref[:, :cols] = rate_ref[...] * LOG2E

    start_ref[0, 0] = h_ref[:, :cols]
    proj = proj_ref[0, 0]
    turn_chunks(proj, bt_ref, None)
    pre = dot(proj[:, 2 * NST :].astype(BF), wdt_ref[...]) + dtb_ref[...]
    dt = jax.nn.softplus(pre)
    dt_ref[:, :cols] = dt
    u_ref[:, :cols] = dt * mix_ref[0, 0]
    rate = wide_ref[...]
    spread = NST * CHUNK

    def chunk(k, h):
        base = pl.multiple_of(k * CHUNK, CHUNK)
        bt = bt_ref[k]
        for t in range(CHUNK):
            a = jnp.exp2(dt_ref[pl.ds(base + t, 1), :] * rate)
            h = a * h + bt[:, t : t + 1] * u_ref[pl.ds(base + t, 1), :]
            hs_ref[pl.ds(pl.multiple_of((base + t) * NST, NST), NST), :] = h.astype(BF)
        return h

    h_ref[...] = lax.fori_loop(0, length // CHUNK, chunk, h_ref[...])
    z = dot(rows_ref[0, 0], wz_ref[...])
    z_ref[0, 0] = z
    crep = dot(proj[:, NST : 2 * NST].astype(BF), tile)
    for k in range(length // CHUNK):
        at = slice(k * CHUNK, (k + 1) * CHUNK)
        cb = (crep[at] * own).astype(BF)
        core_ref[0, 0, at, :] = (
            dot(cb, hs_ref[k * spread : (k + 1) * spread])[:, :cols] + skip_ref[...] * mix_ref[0, 0, at, :]
        )
    gated = core_ref[0, 0] * (z * jax.nn.sigmoid(z))
    sq_ref[0, 0] = jnp.sum(gated * gated, axis=1, keepdims=True)


def scan_forward(proj, mix, rows, wz, wdt, dtb, rate, skip):
    n, seqs, length, cols = mix.shape
    wide = -(-cols // 128) * 128
    big = lambda w: pl.BlockSpec((1, 1, length, w), lambda s, i: (i, s, 0, 0))
    whole = lambda a: pl.BlockSpec(a.shape, lambda s, i: (0, 0))
    shape = lambda w: jax.ShapeDtypeStruct((n, seqs, length, w), F32)
    return pl.pallas_call(
        scan_fwd_kernel,
        grid=(seqs, n),
        in_specs=[big(proj.shape[3]), big(cols), big(rows.shape[3])] + [whole(a) for a in (wz, wdt, dtb, rate, skip)],
        out_specs=[big(cols), big(cols), big(1), pl.BlockSpec((1, 1, NST, cols), lambda s, i: (i, s, 0, 0))],
        out_shape=[shape(cols), shape(cols), shape(1), jax.ShapeDtypeStruct((n, seqs, NST, cols), F32)],
        scratch_shapes=[
            pltpu.VMEM((NST, wide), F32),
            pltpu.VMEM((length, wide), F32),
            pltpu.VMEM((length, wide), F32),
            pltpu.VMEM((NST, wide), F32),
            pltpu.VMEM((NST * length, wide), BF),
            pltpu.VMEM((length // CHUNK, NST, CHUNK), F32),
        ],
        compiler_params=pltpu.CompilerParams(vmem_limit_bytes=GIANT),
    )(proj, mix, rows, wz, wdt, dtb, rate, skip)


def scan_bwd_kernel(proj_ref, mix_ref, d_ref, core_ref, z_ref, stat_ref, start_ref, wdt_ref, dtb_ref, rate_ref, skip_ref,
                    gain_ref, gpre_ref, gmix_ref, gz_ref, gb_ref, gc_ref, grate_ref, sums_ref,
                    carry_ref, dt_ref, u_ref, gy_ref, wide_ref, hs_ref, gs_ref, q_ref, bt_ref, ct_ref):
    length, cols = mix_ref.shape[2:]
    own, tile = chunk_masks()
    spread = NST * CHUNK
    half = NST // 2
    folded = (lax.broadcasted_iota(jnp.int32, (2 * CHUNK, spread), 1) // half
              == lax.broadcasted_iota(jnp.int32, (2 * CHUNK, spread), 0)).astype(BF)

    @pl.when(pl.program_id(1) == 0)
    def _():
        carry_ref[...] = jnp.zeros_like(carry_ref)

    @pl.when((pl.program_id(1) == 0) & (pl.program_id(0) == 0))
    def _():
        grate_ref[...] = jnp.zeros_like(grate_ref)
        sums_ref[...] = jnp.zeros_like(sums_ref)
        for ref in (dt_ref, u_ref, gy_ref, wide_ref):
            ref[...] = jnp.zeros_like(ref)
        wide_ref[0:NST, :cols] = rate_ref[...] * LOG2E

    scale, shift = stat_ref[0, 0][:, 2:3], stat_ref[0, 0][:, 3:4]
    d, core, z = d_ref[0, 0], core_ref[0, 0], z_ref[0, 0]
    logistic = jax.nn.sigmoid(z)
    gated = core * (z * logistic)
    grad_gated = scale * (d * gain_ref[...] - gated * shift)
    gy_ref[:, :cols] = grad_gated * (z * logistic)
    gz_ref[0, 0] = (grad_gated * core * (logistic * (1.0 + z * (1.0 - logistic)))).astype(BF)
    sums_ref[0:1] += jnp.sum(d * gated * scale, axis=0, keepdims=True)
    sums_ref[1:2] += jnp.sum(gy_ref[:, :cols] * mix_ref[0, 0], axis=0, keepdims=True)
    proj = proj_ref[0, 0]
    turn_chunks(proj, bt_ref, ct_ref)
    pre = dot(proj[:, 2 * NST :].astype(BF), wdt_ref[...]) + dtb_ref[...]
    dt = jax.nn.softplus(pre)
    dt_ref[:, :cols] = dt
    u_ref[:, :cols] = dt * mix_ref[0, 0]
    wide_ref[NST:, :cols] = start_ref[0, 0]
    rate = wide_ref[0:NST]
    hs_ref[0:NST] = wide_ref[NST:].astype(BF)

    def ahead(k, h):
        base = pl.multiple_of(k * CHUNK, CHUNK)
        bt = bt_ref[k]
        for t in range(CHUNK):
            a = jnp.exp2(dt_ref[pl.ds(base + t, 1), :] * rate)
            h = a * h + bt[:, t : t + 1] * u_ref[pl.ds(base + t, 1), :]
            hs_ref[pl.ds(pl.multiple_of((base + t + 1) * NST, NST), NST), :] = h.astype(BF)
        return h

    lax.fori_loop(0, length // CHUNK, ahead, wide_ref[NST:])

    def back(r, state):
        carry, grate = state
        k = length // CHUNK - 1 - r
        base = pl.multiple_of(k * CHUNK, CHUNK)
        ct = ct_ref[k]
        qr_late = None
        for t in reversed(range(CHUNK)):
            at = pl.ds(pl.multiple_of((base + t) * NST, NST), NST)
            dt_row = dt_ref[pl.ds(base + t, 1), :]
            a = jnp.exp2(dt_row * rate)
            g = ct[:, t : t + 1] * gy_ref[pl.ds(base + t, 1), :] + carry
            carry = a * g
            q = carry * hs_ref[at, :].astype(F32)
            grate = grate + q * dt_row
            gs_ref[at, :] = g.astype(BF)
            qr = q * rate
            qr = qr[:half] + qr[half:]
            if t % 2:
                qr_late = qr
            else:
                both = jnp.concatenate([qr, qr_late], axis=0).astype(BF)
                q_ref[pl.ds(pl.multiple_of((base + t) * half, NST), NST), :] = both
        return carry, grate

    carry, grate = lax.fori_loop(
        0, length // CHUNK, back, (carry_ref[...], jnp.zeros(carry_ref.shape, F32))
    )
    carry_ref[...] = carry
    grate_ref[...] += grate[:, :cols]
    brep = dot(proj[:, :NST].astype(BF), tile)
    gy_low = gy_ref[...].astype(BF)
    u_low = u_ref[...].astype(BF)
    gcs, gbs = [], []
    for pair in range(length // CHUNK // 2):
        gdts = dot(folded, q_ref[pair * spread : (pair + 1) * spread]) * LN2
        for k in (2 * pair, 2 * pair + 1):
            rows = slice(k * CHUNK, (k + 1) * CHUNK)
            deep = slice(k * spread, (k + 1) * spread)
            mix, dt_now, gy = mix_ref[0, 0, rows, :], dt_ref[rows, :cols], gy_ref[rows, :cols]
            gs = gs_ref[deep]
            gu = dot((brep[rows] * own).astype(BF), gs)[:, :cols]
            gdt = gdts[(k % 2) * CHUNK : (k % 2 + 1) * CHUNK, :cols] + gu * mix
            gpre = gdt * jax.nn.sigmoid(pre[rows])
            gpre_ref[0, 0, rows, :] = gpre.astype(BF)
            sums_ref[2:3] += jnp.sum(gpre, axis=0, keepdims=True)
            gmix_ref[0, 0, rows, :] = gu * dt_now + skip_ref[...] * gy
            hs = hs_ref[k * spread + NST : (k + 1) * spread + NST]
            gcs.append((ntdot(gy_low[rows], hs) * own).astype(BF))
            gbs.append((ntdot(u_low[rows], gs) * own).astype(BF))
    gc_ref[0, 0] = ntdot(jnp.concatenate(gcs, axis=0), tile)
    gb_ref[0, 0] = ntdot(jnp.concatenate(gbs, axis=0), tile)

def scan_backward(proj, mix, d, core, z, stats, start, wdt, dtb, rate, skip, gain):
    n, seqs, length, cols = mix.shape
    wide = -(-cols // 128) * 128
    at = lambda s, i: (n - 1 - i, s, 0, 0)
    big = lambda w: pl.BlockSpec((1, 1, length, w), at)
    whole = lambda a: pl.BlockSpec(a.shape, lambda s, i: (0, 0))
    shape = lambda w, t: jax.ShapeDtypeStruct((n, seqs, length, w), t)
    return pl.pallas_call(
        scan_bwd_kernel,
        grid=(seqs, n),
        in_specs=[big(proj.shape[3]), big(cols), big(cols), big(cols), big(cols), big(stats.shape[3]),
                  pl.BlockSpec((1, 1, NST, cols), at)] + [whole(a) for a in (wdt, dtb, rate, skip, gain)],
        out_specs=[big(cols), big(cols), big(cols), big(NST), big(NST), whole(rate),
                   pl.BlockSpec((8, cols), lambda s, i: (0, 0))],
        out_shape=[
            shape(cols, BF), shape(cols, F32), shape(cols, BF), shape(NST, F32), shape(NST, F32),
            jax.ShapeDtypeStruct((NST, cols), F32),
            jax.ShapeDtypeStruct((8, cols), F32),
        ],
        scratch_shapes=[
            pltpu.VMEM((NST, wide), F32),
            pltpu.VMEM((length, wide), F32),
            pltpu.VMEM((length, wide), F32),
            pltpu.VMEM((length, wide), F32),
            pltpu.VMEM((2 * NST, wide), F32),
            pltpu.VMEM((length * NST + NST, wide), BF),
            pltpu.VMEM((length * NST, wide), BF),
            pltpu.VMEM((length * NST // 2, wide), BF),
            pltpu.VMEM((length // CHUNK, NST, CHUNK), F32),
            pltpu.VMEM((length // CHUNK, NST, CHUNK), F32),
        ],
        compiler_params=pltpu.CompilerParams(vmem_limit_bytes=GIANT),
    )(proj, mix, d, core, z, stats, start, wdt, dtb, rate, skip, gain)


def pick(ref, blocks, slots, slot):
    value = ref[0:blocks, 0, :, 0:HEAD].reshape(-1, HEAD)
    for other in range(1, slots):
        here = ref[0:blocks, 0, :, other * HEAD : (other + 1) * HEAD].reshape(-1, HEAD)
        value = jnp.where(slot == other, here, value)
    return value


def masked_scores(queries, keys, first, length):
    scores = ntdot(queries, keys)
    rows = first + lax.broadcasted_iota(jnp.int32, (scores.shape[0], 1), 0)
    bound = jnp.minimum(rows, length - 1)
    return jnp.where(lax.broadcasted_iota(jnp.int32, scores.shape, 1) <= bound, scores, NEGATIVE)


def attn_fwd_kernel(seq, slot_ref, len_ref, q_ref, k_ref, v_ref, *refs):
    out_ref, lse_ref = refs[-2:]
    n, _, length, width = q_ref.shape
    heads, slots = width // HEAD, k_ref.shape[3] // HEAD
    group = 2
    seq_length = len_ref[seq]
    for i in range(n // group):
        at = slice(i * group, (i + 1) * group)
        for j in range(heads):
            lanes = slice(j * HEAD, (j + 1) * HEAD)
            blocks = (i + 1) * group
            queries = q_ref[at, 0, :, lanes].reshape(group * length, HEAD) * HEAD ** (-0.5)
            keys = pick(k_ref, blocks, slots, slot_ref[j])
            values = pick(v_ref, blocks, slots, slot_ref[j])
            scores = masked_scores(queries.astype(BF), keys, i * group * length, seq_length)
            top = jnp.max(scores, axis=1, keepdims=True)
            probs = jnp.exp(scores - top)
            total = jnp.sum(probs, axis=1, keepdims=True)
            mixed = dot(probs.astype(BF), values) * (slot_ref[heads + j].astype(F32) / total)
            out_ref[at, 0, :, lanes] = mixed.reshape(group, length, HEAD)
            lse_ref[at, 0, :, j : j + 1] = (top + jnp.log(total)).reshape(group, length, 1)


def attn_forward(seq, slot, lengths, q, k, v, before=()):
    n, seqs, length, width = q.shape
    big = lambda w: pl.BlockSpec((n, 1, length, w), lambda s: (0, seq, 0, 0))
    smem = pl.BlockSpec(memory_space=pltpu.SMEM)
    return pl.pallas_call(
        functools.partial(attn_fwd_kernel, seq),
        grid=(1,),
        in_specs=[smem, smem, big(width), big(k.shape[3]), big(k.shape[3])]
        + [pl.BlockSpec(memory_space=pl.ANY)] * len(before),
        out_specs=[big(width), big(width // HEAD)],
        out_shape=[
            jax.ShapeDtypeStruct(q.shape, F32),
            jax.ShapeDtypeStruct((n, seqs, length, width // HEAD), F32),
        ],
        input_output_aliases={5: 0, 6: 1} if before else {},
        compiler_params=pltpu.CompilerParams(vmem_limit_bytes=GIANT),
    )(slot, lengths, q, k, v, *before)


def attn_bwd_kernel(slot_ref, len_ref, q_ref, k_ref, v_ref, d_ref, att_ref, lse_ref, stat_ref, gain_ref,
                    gq_ref, gk_ref, gv_ref, sums_ref, gk_acc, gv_acc, gh_ref):
    n, _, length, width = q_ref.shape
    heads, slots = width // HEAD, k_ref.shape[3] // HEAD
    group = 2
    seq_length = len_ref[pl.program_id(0)]
    @pl.when(pl.program_id(0) == 0)
    def _():
        sums_ref[...] = jnp.zeros_like(sums_ref)

    for i in range(n):
        scale, shift = stat_ref[i, 0][:, 0:1], stat_ref[i, 0][:, 1:2]
        d, attended = d_ref[i, 0], att_ref[i, 0]
        gh_ref[i] = (scale * (d * gain_ref[...] - attended * shift)).astype(BF)
        sums_ref[0:1] += jnp.sum(d * attended * scale, axis=0, keepdims=True)
    gk_acc[...] = jnp.zeros_like(gk_acc)
    gv_acc[...] = jnp.zeros_like(gv_acc)
    for i in range(n // group):
        at = slice(i * group, (i + 1) * group)
        blocks = (i + 1) * group
        for j in range(heads):
            lanes = slice(j * HEAD, (j + 1) * HEAD)
            slot = slot_ref[j]
            queries = q_ref[at, 0, :, lanes].reshape(group * length, HEAD) * HEAD ** (-0.5)
            queries = queries.astype(BF)
            keys = pick(k_ref, blocks, slots, slot)
            values = pick(v_ref, blocks, slots, slot)
            grad = gh_ref[at, :, lanes].reshape(group * length, HEAD)
            attended = att_ref[at, 0, :, lanes].reshape(group * length, HEAD)
            delta = jnp.sum(grad.astype(F32) * attended, axis=1, keepdims=True)
            lse = lse_ref[at, 0, :, j : j + 1].reshape(group * length, 1)
            scores = masked_scores(queries, keys, i * group * length, seq_length)
            probs = jnp.exp(scores - lse)
            grad_scores = (probs * (ntdot(grad, values) - delta)).astype(BF)
            gq = dot(grad_scores, keys) * HEAD ** (-0.5)
            gq_ref[at, 0, :, lanes] = gq.astype(BF).reshape(group, length, HEAD)
            rows = slice(0, blocks * length)
            gk_acc[slot, rows] += tndot(grad_scores, queries)
            gv_acc[slot, rows] += tndot(probs.astype(BF), grad)
    for other in range(slots):
        lanes = slice(other * HEAD, (other + 1) * HEAD)
        gk_ref[:, 0, :, lanes] = gk_acc[other].astype(BF).reshape(n, length, HEAD)
        gv_ref[:, 0, :, lanes] = gv_acc[other].astype(BF).reshape(n, length, HEAD)


def attn_backward(slot, lengths, q, k, v, d, att, lse, stats, gain):
    n, seqs, length, width = q.shape
    big = lambda w: pl.BlockSpec((n, 1, length, w), lambda s: (0, s, 0, 0))
    whole = lambda r: pl.BlockSpec((r, width), lambda s: (0, 0))
    smem = pl.BlockSpec(memory_space=pltpu.SMEM)
    kw = k.shape[3]
    return pl.pallas_call(
        attn_bwd_kernel,
        grid=(seqs,),
        in_specs=[smem, smem, big(width), big(kw), big(kw), big(width), big(width), big(width // HEAD),
                  big(stats.shape[3]), whole(1)],
        out_specs=[big(width), big(kw), big(kw), whole(8)],
        out_shape=[jax.ShapeDtypeStruct(x.shape, BF) for x in (q, k, v)]
        + [jax.ShapeDtypeStruct((8, width), F32)],
        scratch_shapes=[pltpu.VMEM((kw // HEAD, n * length, HEAD), F32)] * 2 + [pltpu.VMEM((n, length, width), BF)],
        compiler_params=pltpu.CompilerParams(vmem_limit_bytes=GIANT),
    )(slot, lengths, q, k, v, d, att, lse, stats, gain)


def signal_fwd_kernel(rows_ref, wx_ref, taps_ref, bias_ref, xp_ref, x_ref, pre_ref, mix_ref, low_ref, part_ref, xs_ref):
    length = rows_ref.shape[2]

    @pl.when(pl.program_id(1) == 0)
    def _():
        xs_ref[0:8] = jnp.zeros((8, xs_ref.shape[1]), F32)

    x = dot(rows_ref[0, 0], wx_ref[...]).astype(BF)
    x_ref[0, 0] = x
    xs_ref[8:] = x.astype(F32)
    first = 8 - (KCONV - 1)
    pre = bias_ref[...]
    for o in range(KCONV):
        pre = pre + taps_ref[o : o + 1] * xs_ref[first + o : first + o + length]
    xs_ref[0:8] = xs_ref[length : length + 8]
    pre_ref[0, 0] = pre
    mix = pre * jax.nn.sigmoid(pre)
    mix_ref[0, 0] = mix
    low_ref[0, 0] = mix.astype(BF)
    part_ref[0, 0] = ntdot(mix.astype(BF), xp_ref[...])


def signal_forward(rows, wx, taps, bias, xp):
    n, seqs, length, width = rows.shape
    cols = wx.shape[1]
    big = lambda w: pl.BlockSpec((1, 1, length, w), lambda s, i: (i, s, 0, 0))
    whole = lambda a: pl.BlockSpec(a.shape, lambda s, i: (0, 0))
    shape = lambda w, t: jax.ShapeDtypeStruct((n, seqs, length, w), t)
    return pl.pallas_call(
        signal_fwd_kernel,
        grid=(seqs, n),
        in_specs=[big(width), whole(wx), whole(taps), whole(bias), whole(xp)],
        out_specs=[big(cols)] * 4 + [big(xp.shape[0])],
        out_shape=[shape(cols, BF), shape(cols, F32), shape(cols, F32), shape(cols, BF), shape(xp.shape[0], F32)],
        scratch_shapes=[pltpu.VMEM((length + 8, cols), F32)],
        compiler_params=pltpu.CompilerParams(vmem_limit_bytes=GIANT),
    )(rows, wx, taps, bias, xp)


def signal_bwd_kernel(gmix_ref, gproj_ref, xp_ref, pre_ref, x_ref, last_ref, taps_ref, gx_ref, sums_ref, gs_ref, xs_ref):
    length = gmix_ref.shape[2]
    edge = KCONV - 1
    i = pl.program_id(1)

    @pl.when((i == 0) & (pl.program_id(0) == 0))
    def _():
        sums_ref[...] = jnp.zeros_like(sums_ref)

    @pl.when(i == 0)
    def _():
        gs_ref[length:] = jnp.zeros((8, gs_ref.shape[1]), F32)

    grad = gmix_ref[0, 0] + dot(gproj_ref[0, 0], xp_ref[...])
    grad = grad * silu_grad(pre_ref[0, 0])
    gs_ref[:length] = grad
    first_block = (i == pl.num_programs(1) - 1).astype(F32)
    xs_ref[0:16] = last_ref[0, 0].astype(F32) * (1.0 - first_block)
    xs_ref[16:] = x_ref[0, 0].astype(F32)
    total = None
    for o in range(KCONV):
        term = taps_ref[o : o + 1] * gs_ref[edge - o : edge - o + length]
        total = term if total is None else total + term
        at = 16 - edge + o
        sums_ref[o : o + 1] += jnp.sum(grad * xs_ref[at : at + length], axis=0, keepdims=True)
    sums_ref[KCONV : KCONV + 1] += jnp.sum(grad, axis=0, keepdims=True)
    gx_ref[0, 0] = total.astype(BF)
    gs_ref[length:] = gs_ref[0:8]


def signal_backward(gmix, gproj, xp, pre, x, taps):
    n, seqs, length, cols = gmix.shape
    at = lambda s, i: (n - 1 - i, s, 0, 0)
    big = lambda w: pl.BlockSpec((1, 1, length, w), at)
    whole = lambda a: pl.BlockSpec(a.shape, lambda s, i: (0, 0))
    before = lambda s, i: (jnp.maximum(n - 2 - i, 0), s, length // 16 - 1, 0)
    return pl.pallas_call(
        signal_bwd_kernel,
        grid=(seqs, n),
        in_specs=[big(cols), big(xp.shape[0]), whole(xp), big(cols), big(cols),
                  pl.BlockSpec((1, 1, 16, cols), before), whole(taps)],
        out_specs=[big(cols), pl.BlockSpec((8, cols), lambda s, i: (0, 0))],
        out_shape=[jax.ShapeDtypeStruct(gmix.shape, BF), jax.ShapeDtypeStruct((8, cols), F32)],
        scratch_shapes=[pltpu.VMEM((length + 8, cols), F32), pltpu.VMEM((length + 16, cols), F32)],
        compiler_params=pltpu.CompilerParams(vmem_limit_bytes=GIANT),
    )(gmix, gproj, xp, pre, x, x, taps)


def norm_kernel(sq_ref, att_ref, again_ref, core_ref, z_ref, sgain_ref, attn_ref, ssm_ref):
    sq = sq_ref[0]
    r_attn = lax.rsqrt(sq[:, 0:1] / (HEADS * HEAD) + EPSILON)
    r_ssm = lax.rsqrt(sq[:, 1:2] / INNER + EPSILON)
    attn_ref[0] = (att_ref[0] * r_attn * again_ref[...]).astype(BF)
    z = z_ref[0]
    ssm_ref[0] = (core_ref[0] * (z * jax.nn.sigmoid(z)) * r_ssm * sgain_ref[...]).astype(BF)


def norm_both(squares, attended, attn_gain, core, z, ssm_gain):
    n, rows, _ = squares.shape
    block = lambda c: pl.BlockSpec((1, rows, c), lambda i: (i, 0, 0))
    whole = lambda a: pl.BlockSpec(a.shape, lambda i: (0, 0))
    aw, sw = attended.shape[2], core.shape[2]
    return pl.pallas_call(
        norm_kernel,
        grid=(n,),
        in_specs=[block(2), block(aw), whole(attn_gain), block(sw), block(sw), whole(ssm_gain)],
        out_specs=[block(aw), block(sw)],
        out_shape=[jax.ShapeDtypeStruct((n, rows, w), BF) for w in (aw, sw)],
        compiler_params=pltpu.CompilerParams(vmem_limit_bytes=GIANT),
    )(squares, attended, attn_gain, core, z, ssm_gain)


def ffn_bwd_kernel(u_ref, down_ref, gate_ref, up_ref, ggate_ref, gup_ref):
    grad = ntdot(u_ref[0], down_ref[...])
    gate, up = gate_ref[0].astype(F32), up_ref[0].astype(F32)
    logistic = jax.nn.sigmoid(gate)
    ggate_ref[0] = (grad * up * (logistic * (1.0 + gate * (1.0 - logistic)))).astype(BF)
    gup_ref[0] = (grad * (gate * logistic)).astype(BF)


def ffn_backward(upstream, w_down, gate, up):
    n, rows, hidden = gate.shape
    block = lambda c: pl.BlockSpec((1, rows, c), lambda i: (i, 0, 0))
    return pl.pallas_call(
        ffn_bwd_kernel,
        grid=(n,),
        in_specs=[block(upstream.shape[2]), pl.BlockSpec(w_down.shape, lambda i: (0, 0)), block(hidden), block(hidden)],
        out_specs=[block(hidden)] * 2,
        out_shape=[jax.ShapeDtypeStruct(gate.shape, BF)] * 2,
        compiler_params=pltpu.CompilerParams(vmem_limit_bytes=GIANT),
    )(upstream, w_down, gate, up)


def greet(peers, axis="seq"):
    barrier = pltpu.get_barrier_semaphore()
    for peer in peers:
        pl.semaphore_signal(barrier, inc=1, device_id={axis: peer}, device_id_type=MESH)
    pl.semaphore_wait(barrier, len(peers))

def send(src, dst, send_sem, recv_sem, peer, axis="seq"):
    return pltpu.make_async_remote_copy(src_ref=src, dst_ref=dst, send_sem=send_sem, recv_sem=recv_sem,
        device_id={axis: peer}, device_id_type=MESH)

def ag_parts(n, x_ref, o_ref, local_sem, far_send, far_recv, near_send, near_recv):
    me = lax.axis_index("seq")
    core, chip, chips = me % 2, me // 2, n // 2
    sib = me + 1 - 2 * core
    far = [((chip + d) % chips) * 2 + core for d in range(1, chips)]
    mine = pltpu.make_async_copy(x_ref, o_ref.at[me], local_sem)
    out = [
        send(x_ref, o_ref.at[me], far_send.at[d], far_recv.at[d], far[d - 1]) for d in range(1, chips)
    ]
    near = [send(x_ref, o_ref.at[me], near_send.at[0], near_recv.at[0], sib)]

    def begin():
        for c in [mine] + out + near:
            c.start()

    def finish():
        for d in range(1, chips):
            out[d - 1].wait_recv()
            block = ((chip + chips - d) % chips) * 2 + core
            c = send(o_ref.at[block], o_ref.at[block], near_send.at[d], near_recv.at[d], sib)
            c.start()
            near.append(c)
        mine.wait()
        for c in near:
            c.wait()
        for c in out:
            c.wait_send()

    return begin, finish


def ag_kernel(n, x_ref, o_ref, *sems):
    me = lax.axis_index("seq")
    core, chip, chips = me % 2, me // 2, n // 2
    greet([me + 1 - 2 * core] + [((chip + d) % chips) * 2 + core for d in range(1, chips)])
    begin, finish = ag_parts(n, x_ref, o_ref, *sems)
    begin()
    finish()


def all_gather_any(x, n, cid):
    chips = n // 2
    return pl.pallas_call(functools.partial(ag_kernel, n),
        out_shape=jax.ShapeDtypeStruct((n,) + x.shape, x.dtype),
        in_specs=[pl.BlockSpec(memory_space=pl.ANY)],
        out_specs=pl.BlockSpec(memory_space=pl.ANY),
        scratch_shapes=[pltpu.SemaphoreType.DMA] + [pltpu.SemaphoreType.DMA((chips,))] * 4,
        compiler_params=pltpu.CompilerParams(collective_id=cid, has_side_effects=True),
    )(x)

def rs_kernel(n, p_ref, after_ref, o_ref, own, near, sums, got, local_sem, near_send, near_recv, far_send, far_recv):
    me = lax.axis_index("seq")
    core, chip, chips = me % 2, me // 2, n // 2
    sib = me + 1 - 2 * core
    step = lambda d: (chip + d) % chips
    far = [step(d) * 2 + core for d in range(1, chips)]
    greet([sib] + far)
    order = list(range(1, chips)) + [0]
    loads, nears, fars = {}, {}, {}
    for d in order:
        nears[d] = send(p_ref.at[step(d) * 2 + 1 - core], near.at[d], near_send.at[d], near_recv.at[d], sib)
        nears[d].start()
        loads[d] = pltpu.make_async_copy(p_ref.at[step(d) * 2 + core], own.at[d], local_sem.at[d])
        loads[d].start()
    rows = own.shape[1]
    slab = 16
    def each(body):
        def run(i, _):
            body(pl.ds(pl.multiple_of(i * slab, slab), slab))
            return 0
        lax.fori_loop(0, rows // slab, run, 0, unroll=2)
    for d in order:
        loads[d].wait()
        nears[d].wait_recv()
        if d:
            def add(at):
                sums[d - 1, at] = (own[d, at].astype(F32) + near[d, at].astype(F32)).astype(BF)
            each(add)
            fars[d] = send(sums.at[d - 1], got.at[d - 1], far_send.at[d - 1], far_recv.at[d - 1], far[d - 1])
            fars[d].start()
        else:
            def add(at):
                o_ref[at] = own[0, at].astype(F32) + near[0, at].astype(F32)
            each(add)
    for d in range(1, chips):
        fars[d].wait_recv()
        def add(at):
            o_ref[at] = o_ref[at] + got[d - 1, at].astype(F32)
        each(add)
    for d in order:
        nears[d].wait_send()
        if d: fars[d].wait_send()

def reduce_scatter_any(p, after, n, cid):
    chips = n // 2
    blk = p.shape[1:]
    return pl.pallas_call(functools.partial(rs_kernel, n),
        out_shape=jax.ShapeDtypeStruct(blk, F32),
        in_specs=[pl.BlockSpec(memory_space=pl.ANY)] * 2,
        out_specs=pl.BlockSpec(memory_space=pltpu.VMEM),
        scratch_shapes=[pltpu.VMEM((chips,) + blk, p.dtype), pltpu.VMEM((chips,) + blk, p.dtype),
            pltpu.VMEM((chips-1,) + blk, p.dtype), pltpu.VMEM((chips-1,) + blk, p.dtype),
            pltpu.SemaphoreType.DMA((chips,)), pltpu.SemaphoreType.DMA((chips,)), pltpu.SemaphoreType.DMA((chips,)),
            pltpu.SemaphoreType.DMA((chips-1,)), pltpu.SemaphoreType.DMA((chips-1,))],
        compiler_params=pltpu.CompilerParams(collective_id=cid, has_side_effects=True, vmem_limit_bytes=GIANT),
    )(p, after)

def stat_kernel(n, axis, x_ref, o_ref, got, send_sem, recv_sem):
    me = lax.axis_index(axis)
    peers = [(me + d) % n for d in range(1, n)]
    greet(peers, axis)
    copies = []
    for d in range(1, n):
        c = send(x_ref, got.at[d - 1], send_sem.at[d - 1], recv_sem.at[d - 1], peers[d - 1], axis)
        c.start()
        copies.append(c)
    total = x_ref[...]
    for d in range(1, n):
        copies[d - 1].wait_recv()
        total = total + got[d - 1]
    o_ref[...] = total
    for c in copies:
        c.wait_send()


def small_sum(x, n, cid, axis="seq"):
    return pl.pallas_call(
        functools.partial(stat_kernel, n, axis),
        out_shape=jax.ShapeDtypeStruct(x.shape, F32),
        in_specs=[pl.BlockSpec(memory_space=pltpu.VMEM)],
        out_specs=pl.BlockSpec(memory_space=pltpu.VMEM),
        scratch_shapes=[pltpu.VMEM((n - 1,) + x.shape, F32)] + [pltpu.SemaphoreType.DMA((n - 1,))] * 2,
        compiler_params=pltpu.CompilerParams(collective_id=cid, has_side_effects=True, vmem_limit_bytes=GIANT),
    )(x)


def square(me):
    core, x, y = me % 2, (me // 2) % 2, me // 4
    seat = lambda yy, xx, cc: (yy * 2 + xx) * 2 + cc
    return core, (seat(y, x, 1 - core), seat(y, 1 - x, core), seat(1 - y, x, core), seat(1 - y, 1 - x, core))

def ag4_parts(n, x_ref, o_ref, local_sem, far_send, far_recv, near_send, near_recv):
    me = lax.axis_index("seq")
    core, (sib, east, north, across) = square(me)
    half = x_ref.shape[0] // 2
    cut = (pl.ds(0, half), pl.ds(half, half))
    mine = pltpu.make_async_copy(x_ref, o_ref.at[me], local_sem)
    far, near = {}, []
    for slot, h, peer in ((0, 0, east), (2, 1, north), (1, 1, east), (3, 0, north)):
        far[slot] = send(x_ref.at[cut[h]], o_ref.at[me, cut[h]], far_send.at[slot], far_recv.at[slot], peer)
    near.append(send(x_ref, o_ref.at[me], near_send.at[6], near_recv.at[6], sib))

    def begin():
        mine.start()
        for slot in (0, 2, 1, 3):
            far[slot].start()
        near[0].start()

    def pass_on(slot, block, h):
        ref = o_ref.at[block, cut[h]]
        c = send(ref, ref, near_send.at[slot], near_recv.at[slot], sib)
        c.start()
        near.append(c)

    def finish():
        for slot, block, h, relay, to in (
            (0, east, 0, 4, north), (2, north, 1, 5, east), (1, east, 1, None, None), (3, north, 0, None, None)
        ):
            far[slot].wait_recv()
            if relay is not None:
                ref = o_ref.at[block, cut[h]]
                far[relay] = send(ref, ref, far_send.at[relay], far_recv.at[relay], to)
                far[relay].start()
            pass_on(slot, block, h)
        for slot, h in ((4, 0), (5, 1)):
            far[slot].wait_recv()
            pass_on(slot, across, h)
        mine.wait()
        for c in near:
            c.wait()
        for c in far.values():
            c.wait_send()

    return begin, finish


def ag4_kernel(x_ref, o_ref, *sems):
    core, (sib, east, north, across) = square(lax.axis_index("seq"))
    greet([sib, east, north])
    begin, finish = ag4_parts(8, x_ref, o_ref, *sems)
    begin()
    finish()


def all_gather4(x, n, cid):
    return pl.pallas_call(ag4_kernel,
        out_shape=jax.ShapeDtypeStruct((n,) + x.shape, x.dtype),
        in_specs=[pl.BlockSpec(memory_space=pl.ANY)],
        out_specs=pl.BlockSpec(memory_space=pl.ANY),
        scratch_shapes=[pltpu.SemaphoreType.DMA] + [pltpu.SemaphoreType.DMA((6,))] * 2 + [pltpu.SemaphoreType.DMA((7,))] * 2,
        compiler_params=pltpu.CompilerParams(collective_id=cid, has_side_effects=True),
    )(x)

def rs4_kernel(p_ref, after_ref, o_ref, own, near, got, local_sem, near_send, near_recv, far_send, far_recv):
    me = lax.axis_index("seq")
    core, (sib, east, north, across) = square(me)
    greet([sib, east, north])
    rows = own.shape[1]
    half = rows // 2
    cut = (pl.ds(0, half), pl.ds(half, half))
    seats = (across, east, north, me)
    loads, nears, far = [], [], {}
    for i, seat in enumerate(seats):
        other = seat + 1 - 2 * core
        c = send(p_ref.at[other], near.at[i], near_send.at[i], near_recv.at[i], sib)
        c.start(); nears.append(c)
        c = pltpu.make_async_copy(p_ref.at[seat], own.at[i], local_sem.at[i])
        c.start(); loads.append(c)
    slab = 16
    def each(first, count, body):
        def run(i, _):
            body(pl.ds(pl.multiple_of(first + i * slab, slab), slab), pl.ds(pl.multiple_of(i * slab, slab), slab))
            return 0
        lax.fori_loop(0, count // slab, run, 0, unroll=2)
    def fold(i):
        loads[i].wait(); nears[i].wait_recv()
        def add(at, _):
            own[i, at] = (own[i, at].astype(F32) + near[i, at].astype(F32)).astype(own.dtype)
        each(0, rows, add)
    def go(slot, i, h, peer):
        far[slot] = send(own.at[i, cut[h]], got.at[slot], far_send.at[slot], far_recv.at[slot], peer)
        far[slot].start()
    fold(0)
    go(0, 0, 0, east)
    go(1, 0, 1, north)
    fold(1)
    go(2, 1, 0, east)
    fold(2)
    go(3, 2, 1, north)
    def join(i, h, slot):
        far[slot].wait_recv()
        def add(at, src):
            own[i, at] = (own[i, at].astype(F32) + got[slot, src].astype(F32)).astype(own.dtype)
        each(h * half, half, add)
    join(2, 0, 0)
    go(4, 2, 0, north)
    join(1, 1, 1)
    go(5, 1, 1, east)
    loads[3].wait(); nears[3].wait_recv()
    def first(h, slot):
        far[slot].wait_recv()
        def add(at, src):
            o_ref[at] = own[3, at].astype(F32) + near[3, at].astype(F32) + got[slot, src].astype(F32)
        each(h * half, half, add)
    first(0, 2)
    first(1, 3)
    def last(h, slot):
        far[slot].wait_recv()
        def add(at, src):
            o_ref[at] = o_ref[at] + got[slot, src].astype(F32)
        each(h * half, half, add)
    last(0, 4)
    last(1, 5)
    for c in nears: c.wait_send()
    for c in far.values(): c.wait_send()

def reduce_scatter4(p, after, n, cid):
    blk = p.shape[1:]
    return pl.pallas_call(rs4_kernel,
        out_shape=jax.ShapeDtypeStruct(blk, F32),
        in_specs=[pl.BlockSpec(memory_space=pl.ANY)] * 2,
        out_specs=pl.BlockSpec(memory_space=pltpu.VMEM),
        scratch_shapes=[pltpu.VMEM((4,) + blk, p.dtype), pltpu.VMEM((4,) + blk, p.dtype),
            pltpu.VMEM((6, blk[0] // 2) + blk[1:], p.dtype)] + [pltpu.SemaphoreType.DMA((4,))] * 3 + [pltpu.SemaphoreType.DMA((6,))] * 2,
        compiler_params=pltpu.CompilerParams(collective_id=cid, has_side_effects=True, vmem_limit_bytes=GIANT),
    )(p, after)


def start_kernel(n, moves, x_ref, gain_ref, w_ref, in_ref, o_ref, c_ref, first_ref, second_ref,
                 normed_ref, cols_ref, swap_sem, swap_send, swap_recv, *sems):
    me = lax.axis_index("seq")
    others = [(me + d) % n for d in range(1, n)]
    barrier = pltpu.get_barrier_semaphore()
    for peer in others:
        pl.semaphore_signal(barrier, inc=1, device_id={"seq": peer}, device_id_type=MESH)
    x = x_ref[...].astype(F32)
    scale = lax.rsqrt(jnp.mean(x * x, axis=-1, keepdims=True) + EPSILON)
    normed_ref[...] = (x * scale * gain_ref[...]).astype(BF)
    pl.semaphore_wait(barrier, n - 1)
    gather_start, gather_end = (ag4_parts if n == 8 else ag_parts)(n, normed_ref, o_ref, *sems)
    gather_start()
    for i in range(n):
        if sum(size for _, _, size in moves[i]) < cols_ref.shape[2]:
            cols_ref[i] = jnp.zeros(cols_ref.shape[1:], BF)
        for dst, src, size in moves[i]:
            cols_ref[i, :, dst : dst + size] = w_ref[:, src : src + size]
    own = pltpu.make_async_copy(cols_ref.at[me], c_ref.at[me], swap_sem)
    own.start()
    swaps = []
    for d in range(1, n):
        peer = others[d - 1]
        c = send(cols_ref.at[peer], c_ref.at[me], swap_send.at[d - 1], swap_recv.at[d - 1], peer)
        c.start()
        swaps.append(c)
    width = first_ref.shape[2]
    for i in range(n):
        first_ref[i] = in_ref[:, i * width : (i + 1) * width]
        second_ref[i] = in_ref[:, (n + i) * width : (n + i + 1) * width]
    gather_end()
    own.wait()
    for c in swaps:
        c.wait()


def gather_and_exchange(x, gain, w, moves, width, w_in, n, cid):
    far, near = (6, 7) if n == 8 else (n // 2, n // 2)
    anywhere = pl.BlockSpec(memory_space=pl.ANY)
    vmem = pl.BlockSpec(memory_space=pltpu.VMEM)
    dma = pltpu.SemaphoreType.DMA
    cols = jax.ShapeDtypeStruct((n, w.shape[0], width), BF)
    part = jax.ShapeDtypeStruct((n, w_in.shape[0], w_in.shape[1] // (2 * n)), BF)
    return pl.pallas_call(
        functools.partial(start_kernel, n, moves),
        out_shape=[jax.ShapeDtypeStruct((n,) + x.shape, BF), cols, part, part],
        in_specs=[vmem] * 4,
        out_specs=[anywhere] * 2 + [vmem] * 2,
        scratch_shapes=[pltpu.VMEM(x.shape, BF), pltpu.VMEM(cols.shape, BF), dma, dma((n - 1,)), dma((n - 1,)),
                        dma, dma((far,)), dma((far,)), dma((near,)), dma((near,))],
        compiler_params=pltpu.CompilerParams(collective_id=cid, has_side_effects=True, vmem_limit_bytes=GIANT),
    )(x, gain[None], w, w_in)


def all_gather(x, n, cid):
    return (all_gather4 if n == 8 else all_gather_any)(x, n, cid)


def reduce_scatter(p, n, cid, after=None):
    after = jnp.zeros((8, 128), F32) if after is None else after
    return (reduce_scatter4 if n == 8 else reduce_scatter_any)(p, after, n, cid)


def mm_rs4_kernel(turned, *refs):
    terms = len(turned)
    a_refs, b_refs = refs[:terms], refs[terms : 2 * terms]
    after_ref, o_ref, part, near, got, near_send, near_recv, far_send, far_recv = refs[2 * terms :]
    me = lax.axis_index("seq")
    core, (sib, east, north, across) = square(me)
    x, y = (me // 2) % 2, me // 4
    greet([sib, east, north])
    rows = part.shape[2]
    half = rows // 2
    cut = (pl.ds(0, half), pl.ds(half, half))
    slab = 16
    own = part.at[1]

    def near_copy(i):
        return send(part.at[0, i], near.at[i], near_send.at[i], near_recv.at[i], sib)

    hops = ((0, 0, east), (0, 1, north), (1, 0, east), (2, 1, north), (2, 0, north), (1, 1, east))

    def far_copy(slot):
        i, h, peer = hops[slot]
        return send(own.at[i, cut[h]], got.at[slot], far_send.at[slot], far_recv.at[slot], peer)

    def each(first, count, body):
        def run(i, _):
            at = pl.multiple_of(i * slab, slab)
            body(pl.ds(pl.multiple_of(first + at, slab), slab), pl.ds(at, slab))
            return 0

        lax.fori_loop(0, count // slab, run, 0, unroll=2)

    def fold(i):
        near_copy(i).wait_recv()

        def add(at, _):
            own[i, at] = (own[i, at].astype(F32) + near[i, at].astype(F32)).astype(BF)

        each(0, rows, add)

    def step(s, _):
        i, mine = s // 2, s % 2
        yy, xx = (y + (i + 1) % 2) % 2, (x + 1 - i // 2) % 2
        seat = (yy * 2 + xx) * 2 + (core + 1 - mine) % 2
        total = None
        for a, b, t in zip(a_refs, b_refs, turned):
            term = (ntdot if t else dot)(a[seat], b[...])
            total = term if total is None else total + term
        part[mine, i] = total.astype(BF)

        @pl.when(mine == 0)
        def _():
            near_copy(i).start()

        @pl.when(s == 3)
        def _():
            fold(0)
            far_copy(0).start()
            far_copy(1).start()

        @pl.when(s == 5)
        def _():
            fold(1)
            far_copy(2).start()

        @pl.when(s == 6)
        def _():
            fold(2)
            far_copy(3).start()

        return 0

    lax.fori_loop(0, 8, step, 0)

    def join(i, h, slot):
        far_copy(slot).wait_recv()

        def add(at, src):
            own[i, at] = (own[i, at].astype(F32) + got[slot, src].astype(F32)).astype(BF)

        each(h * half, half, add)

    join(2, 0, 0)
    far_copy(4).start()
    join(1, 1, 1)
    far_copy(5).start()
    near_copy(3).wait_recv()

    def first(h, slot):
        far_copy(slot).wait_recv()

        def add(at, src):
            o_ref[at] = own[3, at].astype(F32) + near[3, at].astype(F32) + got[slot, src].astype(F32)

        each(h * half, half, add)

    first(0, 2)
    first(1, 3)

    def last(h, slot):
        far_copy(slot).wait_recv()

        def add(at, src):
            o_ref[at] = o_ref[at] + got[slot, src].astype(F32)

        each(h * half, half, add)

    last(0, 4)
    last(1, 5)
    for i in range(4):
        near_copy(i).wait_send()
    for slot in range(6):
        far_copy(slot).wait_send()


def product_scatter(pairs, n, cid, after=None):
    after = jnp.zeros((8, 128), F32) if after is None else after
    rows = pairs[0][0].shape[0] // n
    cols = pairs[0][1].shape[0 if pairs[0][2] else 1]
    if n != 8:
        total = sum((ntdot if t else dot)(a, b) for a, b, t in pairs)
        return reduce_scatter(total.astype(BF).reshape(n, rows, cols), n, cid, after)
    vmem = pl.BlockSpec(memory_space=pltpu.VMEM)
    dma = pltpu.SemaphoreType.DMA
    return pl.pallas_call(
        functools.partial(mm_rs4_kernel, tuple(t for _, _, t in pairs)),
        out_shape=jax.ShapeDtypeStruct((rows, cols), F32),
        in_specs=[vmem] * (2 * len(pairs)) + [pl.BlockSpec(memory_space=pl.ANY)],
        out_specs=vmem,
        scratch_shapes=[
            pltpu.VMEM((2, 4, rows, cols), BF),
            pltpu.VMEM((4, rows, cols), BF),
            pltpu.VMEM((6, rows // 2, cols), BF),
            dma((4,)), dma((4,)), dma((6,)), dma((6,)),
        ],
        compiler_params=pltpu.CompilerParams(collective_id=cid, has_side_effects=True, vmem_limit_bytes=GIANT),
    )(*(a.reshape(n, rows, a.shape[1]) for a, _, _ in pairs), *(b for _, b, _ in pairs), after)


def chain_kernel(axis, count, cuts, *refs):
    arrays = len(cuts)
    x_refs, after_ref, o_refs = refs[:arrays], refs[arrays], refs[arrays + 1 : 2 * arrays + 1]
    rest = refs[2 * arrays + 1 :]
    up_in, up_out, down_in, down_out = (rest[k * arrays : (k + 1) * arrays] for k in range(4))
    up_send, up_recv, down_send, down_recv = rest[4 * arrays :]
    me = lax.axis_index(axis)
    first, last = me == 0, me == count - 1
    above, below = (me + 1) % count, (me + count - 1) % count
    barrier = pltpu.get_barrier_semaphore()

    @pl.when(me > 0)
    def _():
        pl.semaphore_signal(barrier, inc=1, device_id={axis: below}, device_id_type=MESH)

    @pl.when(me < count - 1)
    def _():
        pl.semaphore_signal(barrier, inc=1, device_id={axis: above}, device_id_type=MESH)

    @pl.when((me > 0) & (me < count - 1))
    def _():
        pl.semaphore_wait(barrier, 2)

    @pl.when(first | last)
    def _():
        pl.semaphore_wait(barrier, 1)

    pieces = [(k, c) for k in range(arrays) for c in range(cuts[k])]
    lane = lambda k: x_refs[k].shape[1] // cuts[k]
    at = lambda k, c: slice(c * lane(k), (c + 1) * lane(k))

    def up(s, k, c):
        return send(up_out[k].at[c], up_in[k].at[c], up_send.at[s], up_recv.at[s], above, axis)

    def down(s, k, c):
        return send(down_out[k].at[c], down_in[k].at[c], down_send.at[s], down_recv.at[s], below, axis)

    for s, (k, c) in enumerate(pieces):
        own = x_refs[k][:, at(k, c)]

        @pl.when(first)
        def _():
            up_out[k][c] = own
            up(s, k, c).start()

        @pl.when(last)
        def _():
            down_out[k][c] = own
            down(s, k, c).start()

    own = lambda s: x_refs[pieces[s][0]][:, at(*pieces[s])].astype(F32)

    def serve_up(s):
        k, c = pieces[s]

        @pl.when(me > 0)
        def _():
            up(s, k, c).wait_recv()

            @pl.when(me < count - 1)
            def _():
                up_out[k][c] = (own(s) + up_in[k][c].astype(F32)).astype(BF)
                up(s, k, c).start()

    def serve_down(s):
        k, c = pieces[s]

        @pl.when(me < count - 1)
        def _():
            down(s, k, c).wait_recv()

            @pl.when(me > 0)
            def _():
                down_out[k][c] = (own(s) + down_in[k][c].astype(F32)).astype(BF)
                down(s, k, c).start()

    def finish(s):
        k, c = pieces[s]
        put = lambda value: o_refs[k].__setitem__((slice(None), at(k, c)), value)

        @pl.when(first)
        def _():
            put(own(s) + down_in[k][c].astype(F32))

        @pl.when(last)
        def _():
            put(own(s) + up_in[k][c].astype(F32))

        @pl.when((me > 0) & (me < count - 1))
        def _():
            put(own(s) + up_in[k][c].astype(F32) + down_in[k][c].astype(F32))

    for s in range(len(pieces) + 1):
        for side, early, late in ((me * 2 < count, serve_up, serve_down), (me * 2 >= count, serve_down, serve_up)):
            @pl.when(side)
            def _():
                if s < len(pieces):
                    early(s)
                if s:
                    late(s - 1)

        if s:
            finish(s - 1)

    for s, (k, c) in enumerate(pieces):
        @pl.when(me < count - 1)
        def _():
            up(s, k, c).wait_send()

        @pl.when(me > 0)
        def _():
            down(s, k, c).wait_send()


def chain_sum(arrays, cuts, count, cid, after, axis="dp"):
    vmem = pl.BlockSpec(memory_space=pltpu.VMEM)
    total = sum(cuts)
    slots = [pltpu.VMEM((c, a.shape[0], a.shape[1] // c), BF) for a, c in zip(arrays, cuts)]
    return pl.pallas_call(
        functools.partial(chain_kernel, axis, count, tuple(cuts)),
        out_shape=[jax.ShapeDtypeStruct(a.shape, F32) for a in arrays],
        in_specs=[vmem] * len(arrays) + [pl.BlockSpec(memory_space=pl.ANY)],
        out_specs=[vmem] * len(arrays),
        scratch_shapes=slots * 4 + [pltpu.SemaphoreType.DMA((total,))] * 4,
        compiler_params=pltpu.CompilerParams(collective_id=cid, has_side_effects=True, vmem_limit_bytes=GIANT),
    )(*arrays, after)


def gather_product4_kernel(body, weights, aligned, x_ref, *refs):
    w_refs, refs = refs[:weights], refs[weights:]
    row_refs, o_ref = refs[:aligned], refs[aligned]
    results, (mine_sem, far_send, far_recv, near_send, near_recv) = refs[aligned + 1 : -5], refs[-5:]
    me = lax.axis_index("seq")
    core, (sib, east, north, across) = square(me)
    x, y = (me // 2) % 2, me // 4
    greet([sib, east, north])
    half = x_ref.shape[0] // 2
    cut = (pl.ds(0, half), pl.ds(half, half))
    hops = (
        (me, 0, east), (me, 1, east), (me, 1, north), (me, 0, north), (east, 0, north), (north, 1, east)
    )
    handed = ((east, 0), (east, 1), (north, 1), (north, 0), (across, 0), (across, 1))

    def far(slot):
        block, h, peer = hops[slot]
        ref = o_ref.at[block, cut[h]]
        return send(x_ref.at[cut[h]] if slot < 4 else ref, ref, far_send.at[slot], far_recv.at[slot], peer)

    def near(slot):
        if slot == 6:
            return send(x_ref, o_ref.at[me], near_send.at[6], near_recv.at[6], sib)
        block, h = handed[slot]
        ref = o_ref.at[block, cut[h]]
        return send(ref, ref, near_send.at[slot], near_recv.at[slot], sib)

    mine = pltpu.make_async_copy(x_ref, o_ref.at[me], mine_sem)
    mine.start()
    for slot in (0, 2, 1, 3):
        far(slot).start()
    near(6).start()

    def arrive(slot, relay=None):
        far(slot).wait_recv()
        if relay is not None:
            far(relay).start()
        near(slot).start()

    def step(s, _):
        @pl.when(s == 0)
        def _():
            mine.wait()

        @pl.when(s == 1)
        def _():
            near(6).wait_recv()

        @pl.when(s == 2)
        def _():
            arrive(0, 4)
            arrive(2, 5)
            arrive(1)

        @pl.when(s == 3)
        def _():
            near(0).wait_recv()
            near(1).wait_recv()

        @pl.when(s == 4)
        def _():
            arrive(3)

        @pl.when(s == 5)
        def _():
            near(2).wait_recv()
            near(3).wait_recv()

        @pl.when(s == 6)
        def _():
            arrive(4)
            arrive(5)

        @pl.when(s == 7)
        def _():
            near(4).wait_recv()
            near(5).wait_recv()

        pair = s // 2
        seat = (((y + pair // 2) % 2) * 2 + (x + pair % 2) % 2) * 2 + (core + s) % 2
        for ref, value in zip(results, body(o_ref[seat], *w_refs, *(ref[seat] for ref in row_refs))):
            ref[seat] = value.astype(ref.dtype)
        return 0

    lax.fori_loop(0, 8, step, 0)
    for slot in range(7):
        near(slot).wait_send()
    for slot in range(6):
        far(slot).wait_send()


def gather_product(body, x, weights, outs, n, cid, by_rows=()):
    rows = x.shape[0]
    if n != 8:
        whole = all_gather(x, n, cid)
        values = body(
            whole.reshape(n * rows, -1), *weights, *(a.reshape(n * rows, a.shape[2]) for a in by_rows)
        )
        return [whole] + [v.astype(t).reshape(n, rows, -1) for v, (_, t) in zip(values, outs)]
    vmem = pl.BlockSpec(memory_space=pltpu.VMEM)
    dma = pltpu.SemaphoreType.DMA
    return pl.pallas_call(
        functools.partial(gather_product4_kernel, body, len(weights), len(by_rows)),
        out_shape=[jax.ShapeDtypeStruct((n,) + x.shape, x.dtype)]
        + [jax.ShapeDtypeStruct((n, rows, c), t) for c, t in outs],
        in_specs=[vmem] * (1 + len(weights) + len(by_rows)),
        out_specs=[vmem] * (1 + len(outs)),
        scratch_shapes=[dma, dma((6,)), dma((6,)), dma((7,)), dma((7,))],
        compiler_params=pltpu.CompilerParams(collective_id=cid, has_side_effects=True, vmem_limit_bytes=GIANT),
    )(x, *weights, *by_rows)


class HeadPlan:
    def __init__(self, n):
        self.n = n
        self.per = -(-HEADS // n)
        group = HEADS // KVH
        self.first_kv, self.slots = [], 1
        for i in range(n):
            low, high = i * self.per, min((i + 1) * self.per, HEADS) - 1
            if low >= HEADS:
                self.first_kv.append(KVH)
            else:
                self.first_kv.append(low // group)
                self.slots = max(self.slots, high // group - low // group + 1)
        self.width = self.per * HEAD
        self.kv_width = self.slots * HEAD

    def head_table(self):
        group = HEADS // KVH
        rows = []
        for i in range(self.n):
            heads = [i * self.per + j for j in range(self.per)]
            rows.append(
                [h // group - self.first_kv[i] if h < HEADS else 0 for h in heads]
                + [int(h < HEADS) for h in heads]
            )
        return jnp.array(rows, jnp.int32)

    def kv_used(self, i):
        group = HEADS // KVH
        heads = range(i * self.per, min((i + 1) * self.per, HEADS))
        return sorted({h // group for h in heads})

    def moves(self):
        lists = []
        for i in range(self.n):
            first = i * self.width
            mine = [(0, first, min(self.width, HEADS * HEAD - first))] if first < HEADS * HEAD else []
            for kind in range(2):
                start = HEADS * HEAD + kind * KVH * HEAD
                for g in self.kv_used(i):
                    slot = g - self.first_kv[i]
                    mine.append((self.width + kind * self.kv_width + slot * HEAD, start + g * HEAD, HEAD))
            lists.append(tuple(mine))
        return tuple(lists)

    def join_columns(self, g):
        q = [g[i, :, : self.width] for i in range(self.n)]
        q = jnp.concatenate(q, axis=1)[:, : HEADS * HEAD].astype(F32)
        kv = []
        for kind in range(2):
            for head in range(KVH):
                total = 0.0
                for i in range(self.n):
                    if head in self.kv_used(i):
                        at = self.width + kind * self.kv_width + (head - self.first_kv[i]) * HEAD
                        total = total + g[i, :, at : at + HEAD].astype(F32)
                kv.append(total)
        return jnp.concatenate([q] + kv, axis=1)


def reblock(rows, have, want, total):
    n, me = lax.axis_size("seq"), lax.axis_index("seq")
    result = jnp.zeros((want,) + rows.shape[1:], rows.dtype)
    pad = jnp.pad(rows, ((want, want), (0, 0)))
    for shift in range(-(n - 1), n):
        pairs = []
        for i in range(n):
            j = i + shift
            if 0 <= j < n:
                low = max(i * have, j * want)
                high = min((i + 1) * have, (j + 1) * want, total)
                if low < high:
                    pairs.append((i, j))
        if not pairs:
            continue
        start = want + (me + shift) * want - me * have
        piece = lax.dynamic_slice_in_dim(pad, jnp.clip(start, 0, have + want), want, 0)
        if shift:
            piece = lax.ppermute(piece, "seq", pairs)
        else:
            ok = jnp.array([(i, i) in pairs for i in range(n)])[me]
            piece = jnp.where(ok, piece, jnp.zeros_like(piece))
        result = result + piece
    return result


def per_device(tokens, lengths, cotangent, w_qkv, w_ao, w_in, w_xp, w_dt, w_so, w_gu, w_down,
               norm_in, norm_attn, norm_ssm, norm_ffn, conv_w, conv_b, dt_bias, a_log, d_skip):
    seqs, slot_len, width = tokens.shape
    n, me, replicas = lax.axis_size("seq"), lax.axis_index("seq"), lax.axis_size("dp")
    local, rows = seqs * slot_len, seqs * slot_len * n
    cols = INNER // n
    plan = HeadPlan(n)
    w_rows, ao_rows = w_qkv.shape[0], w_ao.shape[0]
    pos = me * slot_len + jnp.arange(slot_len, dtype=jnp.int32)
    is_valid = pos[None, :] < lengths[:, None]
    table = plan.head_table()[me]
    tie = lax.optimization_barrier
    flat = lambda v: v.reshape(rows, v.shape[-1])
    gather = lambda v, cid: flat(all_gather(v, n, cid))
    scatter = lambda v, cid, after=None: reduce_scatter(
        v.astype(BF).reshape(n, local, v.shape[-1]), n, cid, after
    )
    later = lambda g, zero: g + zero.astype(g.dtype)
    nothing = lambda *sums: 0.0 * sum(g.reshape(-1)[0].astype(F32) for g in sums)
    mark = lambda zero: jnp.full((8, 128), zero)
    exchange = lambda v: lax.all_to_all(v, "seq", 0, 0, tiled=True)
    blocks = lambda v: v.reshape(n, seqs, slot_len, v.shape[-1])
    mine = lambda v: lax.dynamic_slice_in_dim(v, me * cols, cols, v.ndim - 1)
    over = lambda g: lax.psum(g, "dp")

    def one_step(work):
        shapes = jax.eval_shape(work, 0)
        none = lambda _: jax.tree.map(lambda t: jnp.zeros(t.shape, t.dtype), shapes)
        return lax.cond(lengths[0] > 0, work, none, 0)

    def row_sums(a, b, cid):
        both = jnp.stack([a, b]).reshape(-1, 128)
        return small_sum(both, n, cid).reshape(2, rows)

    wdt = mine(w_dt)
    taps, bias, dtb, skip = mine(conv_w), mine(conv_b), mine(dt_bias), mine(d_skip)
    rate = -jnp.exp(mine(a_log))
    ssm_gain = mine(norm_ssm)
    attn_gain = lax.dynamic_slice_in_dim(
        jnp.pad(norm_attn, (0, n * plan.width - HEADS * HEAD)), me * plan.width, plan.width, 0
    )

    x = tokens.astype(F32).reshape(local, width)
    scale_in = lax.rsqrt(jnp.mean(x * x, axis=-1, keepdims=True) + EPSILON)
    normed, qkv_cols, in_x, in_z = gather_and_exchange(
        tokens.reshape(local, width), norm_in, w_qkv, plan.moves(), plan.width + 2 * plan.kv_width, w_in, n, 1
    )
    normed, qkv_cols = flat(normed), qkv_cols.reshape(n * w_rows, -1)
    qkv = dot(normed, qkv_cols).astype(BF)
    wx, wz = exchange(in_x), exchange(in_z)
    behind = 0.0 * qkv[0, 0].astype(F32)
    ao_all = lax.all_gather(later(w_ao, behind), "seq", axis=0, tiled=True)
    ao_mine = lax.dynamic_slice_in_dim(
        jnp.pad(ao_all, ((0, n * plan.width - HEADS * HEAD), (0, 0))), me * plan.width, plan.width, 0
    )
    upstream = (cotangent.astype(F32) * is_valid[..., None]).reshape(local, width)
    upstream_all = lax.all_gather(later(upstream.astype(BF), behind), "seq", axis=0, tiled=True)
    q = blocks(qkv[:, : plan.width])
    k = blocks(qkv[:, plan.width : plan.width + plan.kv_width])
    v = blocks(qkv[:, plan.width + plan.kv_width :])
    attended, lse = attn_forward(0, table, lengths, q, k, v)
    for seq in range(1, seqs):
        attended, lse = attn_forward(seq, table, lengths, q, k, v, (attended, lse))
    wx = later(wx, nothing(lse)).reshape(n * w_rows, cols)
    wz = wz.reshape(n * w_rows, cols)
    xp = jnp.swapaxes(w_xp, 0, 1)
    xp = jnp.concatenate([xp[DTR:], xp[:DTR]], axis=0)
    x_conv, conv_pre, mixer_in, mixer_low, projected = signal_forward(blocks(normed), wx, taps, bias[None], xp)
    mixer_low = flat(mixer_low)
    projected = blocks(gather(scatter(flat(projected), 15).astype(BF), 16)).astype(F32)
    core, z_gate, ssm_sq, start = scan_forward(
        projected, mixer_in, blocks(normed), wz, wdt, dtb[None], rate, skip[None]
    )
    by_device = lambda m: m.reshape(n, local, m.shape[-1])
    squares = row_sums(jnp.sum(attended * attended, axis=3).reshape(rows), ssm_sq.reshape(rows), 2)
    r_attn = lax.rsqrt(squares[0] / (HEADS * HEAD) + EPSILON)
    r_ssm = lax.rsqrt(squares[1] / INNER + EPSILON)
    attn_low, ssm_low = map(flat, norm_both(
        by_device(squares.T), by_device(attended), attn_gain[None], by_device(core), by_device(z_gate), ssm_gain[None]
    ))
    mixed = product_scatter(((attn_low, ao_mine, False), (ssm_low, w_so, False)), n, 3)
    residual = x + 0.5 * mixed
    r_ffn = lax.rsqrt(jnp.mean(residual * residual, axis=-1, keepdims=True) + EPSILON)
    turned = jnp.transpose(w_gu, (1, 2, 0))
    w_gate, w_up = turned[0], turned[1]
    hidden = w_gate.shape[0]

    def gated_units(rows_in, gate_ref, up_ref):
        gate, up = ntdot(rows_in, gate_ref[...]), ntdot(rows_in, up_ref[...])
        return gate, up, jax.nn.silu(gate) * up

    normed_two, gate, up, activated = gather_product(
        gated_units, (residual * r_ffn * norm_ffn).astype(BF), (w_gate, w_up), ((hidden, BF),) * 3, n, 4
    )
    normed_two, activated = flat(normed_two), flat(activated)

    grad_gate, grad_up = map(flat, ffn_backward(by_device(upstream_all), w_down, gate, up))
    g_down = tndot(activated, upstream_all).astype(BF)
    g_gate, g_up = tndot(grad_gate, normed_two).astype(BF), tndot(grad_up, normed_two).astype(BF)
    g_down, g_gate, g_up = tie((g_down, g_gate, g_up))
    s_down, s_gate, s_up = over((g_down, g_gate, g_up))
    grad_two = product_scatter(
        ((grad_gate, w_gate, False), (grad_up, w_up, False)), n, 5, mark(nothing(g_gate, g_up))
    )

    def norm_pull(grad, values, r, gain):
        dotted = jnp.mean(grad * gain * values, axis=-1, keepdims=True)
        return r * (grad * gain - values * (r * r * dotted)), jnp.sum(grad * values * r, axis=0)

    add, g_norm_ffn = norm_pull(grad_two, residual, r_ffn, norm_ffn)
    grad_residual = upstream + add

    def heads_and_channels(rows_in, ao_ref, so_ref, head_gain, channel_gain, heads_out, core_out, gate_out):
        of_heads = 0.5 * ntdot(rows_in, ao_ref[...])
        of_channels = 0.5 * ntdot(rows_in, so_ref[...])
        gated = core_out * (gate_out * jax.nn.sigmoid(gate_out))
        sums = [
            jnp.sum(of_heads * head_gain[...] * heads_out, axis=1, keepdims=True),
            jnp.sum(of_channels * channel_gain[...] * gated, axis=1, keepdims=True),
        ]
        return of_heads, of_channels, jnp.concatenate(sums, axis=1)

    mix_low, d_attn, d_ssm, inner = gather_product(
        heads_and_channels, grad_residual.astype(BF), (ao_mine, w_so, attn_gain[None], ssm_gain[None]),
        ((plan.width, F32), (cols, F32), (2, F32)), n, 7, (by_device(attended), by_device(core), by_device(z_gate)),
    )
    mix_low, inner = flat(mix_low), inner.reshape(rows, 2)
    inner = row_sums(inner[:, 0], inner[:, 1], 8)
    stats = blocks(jnp.stack([
        r_attn, inner[0] / (HEADS * HEAD) * r_attn * r_attn, r_ssm, inner[1] / INNER * r_ssm * r_ssm
    ], axis=1))

    def mixers_back(_):
        gq, gk, gv, head_sums = attn_backward(
            table, lengths, q, k, v, blocks(d_attn), attended, lse, stats, attn_gain[None]
        )
        gpre, gmix, gz, gb, gc, grate, channel_sums = scan_backward(
            projected, mixer_in, blocks(d_ssm), core, z_gate, stats, start, wdt, dtb[None], rate, skip[None],
            ssm_gain[None],
        )
        grad_qkv, grad_z = flat(jnp.concatenate([gq, gk, gv], axis=3)), flat(gz)
        of_weights = (
            (0.5 * tndot(attn_low, mix_low)).astype(BF),
            (0.5 * tndot(ssm_low, mix_low)).astype(BF),
            tndot(normed, grad_z).astype(BF),
            tndot(normed, grad_qkv).astype(BF),
        )
        return head_sums[0], channel_sums, grad_qkv, grad_z, flat(gpre), gmix, flat(gb), flat(gc), grate, of_weights

    g_norm_attn, channel_sums, grad_qkv, grad_z, grad_step, gmix, gb, gc, grate, of_weights = one_step(mixers_back)
    g_norm_ssm, gskip, g_dt_bias = channel_sums[0], channel_sums[1:2], channel_sums[2]
    g_ao, g_so, g_z, g_qkv = of_weights
    g_ao = reblock(g_ao, plan.width, ao_rows, HEADS * HEAD)
    g_z = exchange(g_z.reshape(n, w_rows, cols))
    g_z = jnp.swapaxes(g_z, 0, 1).reshape(w_rows, INNER)
    g_qkv = exchange(g_qkv.reshape(n, w_rows, -1))
    g_qkv = plan.join_columns(g_qkv).astype(BF)
    after_one = nothing(s_down, s_gate, s_up, grate)
    s_ao, s_so, s_qkv, s_z = over(tuple(later(g, after_one) for g in (g_ao, g_so, g_qkv, g_z)))
    grad_projected = jnp.concatenate([gb, gc, ntdot(grad_step, wdt)], axis=1)
    grad_projected = gather(scatter(grad_projected, 9, mark(after_one)).astype(BF), 10)

    def signal_back(_):
        grad_x, sums = signal_backward(gmix, blocks(grad_projected), xp, conv_pre, x_conv, taps)
        grad_x = flat(grad_x)
        return (
            grad_x,
            sums,
            tndot(normed, grad_x).astype(BF),
            tndot(grad_projected, mixer_low).astype(BF),
            tndot(grad_step, flat(projected)[:, 2 * NST :].astype(BF)).astype(BF),
        )

    grad_x, tap_sums, g_x, g_xp, g_wdt = one_step(signal_back)
    g_conv_w, g_conv_b = tap_sums[:KCONV], tap_sums[KCONV]
    g_x = exchange(g_x.reshape(n, w_rows, cols))
    g_x = jnp.swapaxes(g_x, 0, 1).reshape(w_rows, INNER)
    grad_normed = product_scatter(
        ((grad_x, wx, True), (grad_z, wz, True), (grad_qkv, qkv_cols, True)), n, 11
    )
    block_out = residual + product_scatter(
        ((activated, w_down, False),), n, 6, mark(nothing(grad_normed))
    )
    add_in, g_norm_in = norm_pull(grad_normed, x, scale_in, norm_in)
    grad_tokens = grad_residual + add_in

    s_gu = jnp.transpose(jnp.stack([s_gate, s_up]), (2, 0, 1))
    s_x, s_xp, s_wdt = chain_sum((g_x, g_xp, g_wdt), (5, 1, 1), replicas, 14, mark(nothing(block_out, s_ao, s_so, s_qkv, s_z)))
    s_in = jnp.concatenate([s_x, s_z.astype(F32)], axis=1)
    s_xp = jnp.swapaxes(jnp.concatenate([s_xp[2 * NST :], s_xp[: 2 * NST]], axis=0), 0, 1)
    s_wdt = jnp.swapaxes(s_wdt, 0, 1)

    place = lambda g: lax.dynamic_update_slice_in_dim(
        jnp.zeros((n * plan.width,), F32), g, me * plan.width, 0
    )[: HEADS * HEAD]

    def pad_rows(v):
        v = v.reshape(-1)
        return jnp.pad(v, (0, -v.size % 1024)).reshape(-1, 128)

    shared = jnp.stack([g_norm_in, place(g_norm_attn), g_norm_ffn])
    total = small_sum(pad_rows(shared), n, 12).reshape(-1)[: shared.size].reshape(shared.shape)
    shared = lax.dynamic_slice_in_dim(total, me * w_rows, w_rows, 1)
    owned = jnp.concatenate(
        [g_norm_ssm[None], g_conv_w, g_conv_b[None], g_dt_bias[None], grate * rate, gskip], axis=0
    )
    small = pad_rows(jnp.concatenate([shared.reshape(-1), owned.reshape(-1)]))
    small = small_sum(small, replicas, 13, "dp").reshape(-1)
    s_shared = small[: shared.size].reshape(shared.shape)
    s_owned = small[shared.size : shared.size + owned.size].reshape(owned.shape)
    full = lambda g: g.astype(F32)

    return (
        block_out.astype(BF).reshape(seqs, slot_len, width),
        grad_tokens.reshape(seqs, slot_len, width),
        full(s_qkv),
        full(s_ao),
        full(s_in),
        full(s_xp),
        full(s_wdt),
        full(s_so),
        full(s_gu),
        full(s_down),
        s_shared[0],
        s_shared[1],
        s_owned[0],
        s_shared[2],
        s_owned[1 : 1 + KCONV],
        s_owned[1 + KCONV],
        s_owned[2 + KCONV],
        s_owned[3 + KCONV : 3 + KCONV + NST],
        s_owned[3 + KCONV + NST],
    )


def solution(mesh):
    rows, cols, flat = P("seq", None), P(None, "seq"), P("seq")
    act = P("dp", "seq", None)
    hid = P(None, None, "seq")
    in_specs = (act, P("dp"), act, rows, rows, rows, rows, P(), rows, hid, rows) + (P(),) * 9
    out_specs = (act, act, rows, rows, rows, rows, cols, rows, hid, rows,
                 flat, flat, flat, flat, cols, flat, flat, cols, flat)
    return jax.shard_map(per_device, mesh=mesh, in_specs=in_specs, out_specs=out_specs, check_vma=False)
```

```python
import functools
import math

import jax
import jax.numpy as jnp
from jax import lax
from jax.experimental import pallas as pl
from jax.experimental.pallas import tpu as pltpu
from jax.sharding import PartitionSpec as P

HEADS = 25
HEAD = 64
KVH = 5
INNER = 3200
NST = 16
KCONV = 4
DTR = 100
EPSILON = 1e-05
NEGATIVE = -1e30
CHUNK = 16
LOG2E = math.log2(math.e)
LN2 = math.log(2.0)

BF = jnp.bfloat16
F32 = jnp.float32
NT = (((1,), (1,)), ((), ()))
TN = (((0,), (0,)), ((), ()))
GIANT = 60 * 1024 * 1024
MESH = pl.DeviceIdType.MESH


def ntdot(a, b):
    return lax.dot_general(a, b, NT, preferred_element_type=F32)


def tndot(a, b):
    return lax.dot_general(a, b, TN, preferred_element_type=F32)


def dot(a, b):
    return jnp.dot(a, b, preferred_element_type=F32)


def silu_grad(values):
    logistic = jax.nn.sigmoid(values)
    return logistic * (1.0 + values * (1.0 - logistic))


def chunk_masks():
    spread = NST * CHUNK
    row = lax.broadcasted_iota(jnp.int32, (CHUNK, spread), 0)
    col = lax.broadcasted_iota(jnp.int32, (CHUNK, spread), 1)
    own = (col // NST == row).astype(F32)
    tile = (col % NST == row).astype(BF)
    return own, tile


def turn_chunks(proj, bt_ref, ct_ref):
    turned = jnp.swapaxes(proj[:, : 8 * NST], 0, 1)
    for k in range(proj.shape[0] // CHUNK):
        at = slice(k * CHUNK, (k + 1) * CHUNK)
        bt_ref[k] = turned[:NST, at]
        if ct_ref is not None:
            ct_ref[k] = turned[NST : 2 * NST, at]


def scan_fwd_kernel(proj_ref, mix_ref, rows_ref, wz_ref, wdt_ref, dtb_ref, rate_ref, skip_ref,
                    core_ref, z_ref, sq_ref, start_ref, h_ref, dt_ref, u_ref, wide_ref, hs_ref, bt_ref):
    length, cols = mix_ref.shape[2:]
    own, tile = chunk_masks()

    @pl.when(pl.program_id(1) == 0)
    def _():
        for ref in (h_ref, dt_ref, u_ref, wide_ref):
            ref[...] = jnp.zeros_like(ref)
        wide_ref[:, :cols] = rate_ref[...] * LOG2E

    start_ref[0, 0] = h_ref[:, :cols]
    proj = proj_ref[0, 0].astype(F32)
    turn_chunks(proj, bt_ref, None)
    pre = dot(proj[:, 2 * NST :].astype(BF), wdt_ref[...]) + dtb_ref[...]
    dt = jax.nn.softplus(pre)
    dt_ref[:, :cols] = dt
    u_ref[:, :cols] = dt * mix_ref[0, 0]
    rate = wide_ref[...]
    spread = NST * CHUNK

    def chunk(k, h):
        base = pl.multiple_of(k * CHUNK, CHUNK)
        bt = bt_ref[k]
        for t in range(CHUNK):
            a = jnp.exp2(dt_ref[pl.ds(base + t, 1), :] * rate)
            h = a * h + bt[:, t : t + 1] * u_ref[pl.ds(base + t, 1), :]
            hs_ref[pl.ds(pl.multiple_of((base + t) * NST, NST), NST), :] = h.astype(BF)
        return h

    h_ref[...] = lax.fori_loop(0, length // CHUNK, chunk, h_ref[...])
    z = dot(rows_ref[0, 0], wz_ref[...])
    z_ref[0, 0] = z
    crep = dot(proj[:, NST : 2 * NST].astype(BF), tile)
    for k in range(length // CHUNK):
        at = slice(k * CHUNK, (k + 1) * CHUNK)
        cb = (crep[at] * own).astype(BF)
        core_ref[0, 0, at, :] = (
            dot(cb, hs_ref[k * spread : (k + 1) * spread])[:, :cols] + skip_ref[...] * mix_ref[0, 0, at, :]
        )
    gated = core_ref[0, 0] * (z * jax.nn.sigmoid(z))
    sq_ref[0, 0] = jnp.sum(gated * gated, axis=1, keepdims=True)


def scan_forward(proj, mix, rows, wz, wdt, dtb, rate, skip):
    n, seqs, length, cols = mix.shape
    wide = -(-cols // 128) * 128
    big = lambda w: pl.BlockSpec((1, 1, length, w), lambda s, i: (i, s, 0, 0))
    whole = lambda a: pl.BlockSpec(a.shape, lambda s, i: (0, 0))
    shape = lambda w: jax.ShapeDtypeStruct((n, seqs, length, w), F32)
    return pl.pallas_call(
        scan_fwd_kernel,
        grid=(seqs, n),
        in_specs=[big(proj.shape[3]), big(cols), big(rows.shape[3])] + [whole(a) for a in (wz, wdt, dtb, rate, skip)],
        out_specs=[big(cols), big(cols), big(1), pl.BlockSpec((1, 1, NST, cols), lambda s, i: (i, s, 0, 0))],
        out_shape=[shape(cols), shape(cols), shape(1), jax.ShapeDtypeStruct((n, seqs, NST, cols), F32)],
        scratch_shapes=[
            pltpu.VMEM((NST, wide), F32),
            pltpu.VMEM((length, wide), F32),
            pltpu.VMEM((length, wide), F32),
            pltpu.VMEM((NST, wide), F32),
            pltpu.VMEM((NST * length, wide), BF),
            pltpu.VMEM((length // CHUNK, NST, CHUNK), F32),
        ],
        compiler_params=pltpu.CompilerParams(vmem_limit_bytes=GIANT),
    )(proj, mix, rows, wz, wdt, dtb, rate, skip)


def scan_bwd_kernel(len_ref, proj_ref, mix_ref, d_ref, core_ref, z_ref, stat_ref, start_ref, wdt_ref, dtb_ref, rate_ref, skip_ref,
                    gain_ref, gpre_ref, gmix_ref, gz_ref, gb_ref, gc_ref, grate_ref, sums_ref,
                    carry_ref, dt_ref, u_ref, gy_ref, wide_ref, hs_ref, gs_ref, q_ref, bt_ref, ct_ref):
    length, cols = mix_ref.shape[2:]
    own, tile = chunk_masks()
    spread = NST * CHUNK
    half = NST // 2
    folded = (lax.broadcasted_iota(jnp.int32, (2 * CHUNK, spread), 1) // half
              == lax.broadcasted_iota(jnp.int32, (2 * CHUNK, spread), 0)).astype(BF)

    @pl.when(pl.program_id(1) == 0)
    def _():
        carry_ref[...] = jnp.zeros_like(carry_ref)

    @pl.when((pl.program_id(1) == 0) & (pl.program_id(0) == 0))
    def _():
        grate_ref[...] = jnp.zeros_like(grate_ref)
        sums_ref[...] = jnp.zeros_like(sums_ref)
        for ref in (dt_ref, u_ref, gy_ref, wide_ref):
            ref[...] = jnp.zeros_like(ref)
        wide_ref[0:NST, :cols] = rate_ref[...] * LOG2E

    filled = (pl.num_programs(1) - 1 - pl.program_id(1)) * length < len_ref[pl.program_id(0)]

    @pl.when(jnp.logical_not(filled))
    def _():
        for ref in (gpre_ref, gmix_ref, gz_ref, gb_ref, gc_ref):
            ref[...] = jnp.zeros_like(ref)

    @pl.when(filled)
    def _():
        scale, shift = stat_ref[0, 0][:, 2:3], stat_ref[0, 0][:, 3:4]
        d, core, z = d_ref[0, 0], core_ref[0, 0], z_ref[0, 0]
        logistic = jax.nn.sigmoid(z)
        gated = core * (z * logistic)
        grad_gated = scale * (d * gain_ref[...] - gated * shift)
        gy_ref[:, :cols] = grad_gated * (z * logistic)
        gz_ref[0, 0] = (grad_gated * core * (logistic * (1.0 + z * (1.0 - logistic)))).astype(BF)
        sums_ref[0:1] += jnp.sum(d * gated * scale, axis=0, keepdims=True)
        sums_ref[1:2] += jnp.sum(gy_ref[:, :cols] * mix_ref[0, 0], axis=0, keepdims=True)
        proj = proj_ref[0, 0].astype(F32)
        turn_chunks(proj, bt_ref, ct_ref)
        pre = dot(proj[:, 2 * NST :].astype(BF), wdt_ref[...]) + dtb_ref[...]
        dt = jax.nn.softplus(pre)
        dt_ref[:, :cols] = dt
        u_ref[:, :cols] = dt * mix_ref[0, 0]
        wide_ref[NST:, :cols] = start_ref[0, 0]
        rate = wide_ref[0:NST]
        hs_ref[0:NST] = wide_ref[NST:].astype(BF)

        def ahead(k, h):
            base = pl.multiple_of(k * CHUNK, CHUNK)
            bt = bt_ref[k]
            for t in range(CHUNK):
                a = jnp.exp2(dt_ref[pl.ds(base + t, 1), :] * rate)
                h = a * h + bt[:, t : t + 1] * u_ref[pl.ds(base + t, 1), :]
                hs_ref[pl.ds(pl.multiple_of((base + t + 1) * NST, NST), NST), :] = h.astype(BF)
            return h

        lax.fori_loop(0, length // CHUNK, ahead, wide_ref[NST:])

        def back(r, state):
            carry, grate = state
            k = length // CHUNK - 1 - r
            base = pl.multiple_of(k * CHUNK, CHUNK)
            ct = ct_ref[k]
            qr_late = None
            for t in reversed(range(CHUNK)):
                at = pl.ds(pl.multiple_of((base + t) * NST, NST), NST)
                dt_row = dt_ref[pl.ds(base + t, 1), :]
                a = jnp.exp2(dt_row * rate)
                g = ct[:, t : t + 1] * gy_ref[pl.ds(base + t, 1), :] + carry
                carry = a * g
                q = carry * hs_ref[at, :].astype(F32)
                grate = grate + q * dt_row
                gs_ref[at, :] = g.astype(BF)
                qr = q * rate
                qr = qr[:half] + qr[half:]
                if t % 2:
                    qr_late = qr
                else:
                    both = jnp.concatenate([qr, qr_late], axis=0).astype(BF)
                    q_ref[pl.ds(pl.multiple_of((base + t) * half, NST), NST), :] = both
            return carry, grate

        carry, grate = lax.fori_loop(
            0, length // CHUNK, back, (carry_ref[...], jnp.zeros(carry_ref.shape, F32))
        )
        carry_ref[...] = carry
        grate_ref[...] += grate[:, :cols]
        brep = dot(proj[:, :NST].astype(BF), tile)
        gy_low = gy_ref[...].astype(BF)
        u_low = u_ref[...].astype(BF)
        gcs, gbs = [], []
        for pair in range(length // CHUNK // 2):
            gdts = dot(folded, q_ref[pair * spread : (pair + 1) * spread]) * LN2
            for k in (2 * pair, 2 * pair + 1):
                rows = slice(k * CHUNK, (k + 1) * CHUNK)
                deep = slice(k * spread, (k + 1) * spread)
                mix, dt_now, gy = mix_ref[0, 0, rows, :], dt_ref[rows, :cols], gy_ref[rows, :cols]
                gs = gs_ref[deep]
                gu = dot((brep[rows] * own).astype(BF), gs)[:, :cols]
                gdt = gdts[(k % 2) * CHUNK : (k % 2 + 1) * CHUNK, :cols] + gu * mix
                gpre = gdt * jax.nn.sigmoid(pre[rows])
                gpre_ref[0, 0, rows, :] = gpre.astype(BF)
                sums_ref[2:3] += jnp.sum(gpre, axis=0, keepdims=True)
                gmix_ref[0, 0, rows, :] = gu * dt_now + skip_ref[...] * gy
                hs = hs_ref[k * spread + NST : (k + 1) * spread + NST]
                gcs.append((ntdot(gy_low[rows], hs) * own).astype(BF))
                gbs.append((ntdot(u_low[rows], gs) * own).astype(BF))
        gc_ref[0, 0] = ntdot(jnp.concatenate(gcs, axis=0), tile)
        gb_ref[0, 0] = ntdot(jnp.concatenate(gbs, axis=0), tile)


def scan_backward(lengths, proj, mix, d, core, z, stats, start, wdt, dtb, rate, skip, gain):
    n, seqs, length, cols = mix.shape
    wide = -(-cols // 128) * 128
    at = lambda s, i: (n - 1 - i, s, 0, 0)
    big = lambda w: pl.BlockSpec((1, 1, length, w), at)
    whole = lambda a: pl.BlockSpec(a.shape, lambda s, i: (0, 0))
    shape = lambda w, t: jax.ShapeDtypeStruct((n, seqs, length, w), t)
    return pl.pallas_call(
        scan_bwd_kernel,
        grid=(seqs, n),
        in_specs=[pl.BlockSpec(memory_space=pltpu.SMEM),
                  big(proj.shape[3]), big(cols), big(cols), big(cols), big(cols), big(stats.shape[3]),
                  pl.BlockSpec((1, 1, NST, cols), at)] + [whole(a) for a in (wdt, dtb, rate, skip, gain)],
        out_specs=[big(cols), big(cols), big(cols), big(NST), big(NST), whole(rate),
                   pl.BlockSpec((8, cols), lambda s, i: (0, 0))],
        out_shape=[
            shape(cols, BF), shape(cols, F32), shape(cols, BF), shape(NST, F32), shape(NST, F32),
            jax.ShapeDtypeStruct((NST, cols), F32),
            jax.ShapeDtypeStruct((8, cols), F32),
        ],
        scratch_shapes=[
            pltpu.VMEM((NST, wide), F32),
            pltpu.VMEM((length, wide), F32),
            pltpu.VMEM((length, wide), F32),
            pltpu.VMEM((length, wide), F32),
            pltpu.VMEM((2 * NST, wide), F32),
            pltpu.VMEM((length * NST + NST, wide), BF),
            pltpu.VMEM((length * NST, wide), BF),
            pltpu.VMEM((length * NST // 2, wide), BF),
            pltpu.VMEM((length // CHUNK, NST, CHUNK), F32),
            pltpu.VMEM((length // CHUNK, NST, CHUNK), F32),
        ],
        compiler_params=pltpu.CompilerParams(vmem_limit_bytes=GIANT),
    )(lengths, proj, mix, d, core, z, stats, start, wdt, dtb, rate, skip, gain)


def pick(ref, blocks, slots, slot):
    value = ref[0:blocks, 0, :, 0:HEAD].reshape(-1, HEAD)
    for other in range(1, slots):
        here = ref[0:blocks, 0, :, other * HEAD : (other + 1) * HEAD].reshape(-1, HEAD)
        value = jnp.where(slot == other, here, value)
    return value


def masked_scores(queries, keys, first, length):
    scores = ntdot(queries, keys)
    rows = first + lax.broadcasted_iota(jnp.int32, (scores.shape[0], 1), 0)
    bound = jnp.minimum(rows, length - 1)
    return jnp.where(lax.broadcasted_iota(jnp.int32, scores.shape, 1) <= bound, scores, NEGATIVE)


def attn_fwd_kernel(seq, slot_ref, len_ref, rows_ref, w_ref, *refs):
    out_ref, lse_ref, q_ref, k_ref, v_ref = refs[-5:]
    n, _, length, width = q_ref.shape
    heads, slots = width // HEAD, k_ref.shape[3] // HEAD
    group = 2
    seq_length = len_ref[seq]
    kv_width = k_ref.shape[3]

    def project(i, _):
        y = dot(rows_ref[i, 0], w_ref[...]).astype(BF)
        q_ref[i, 0] = y[:, :width]
        k_ref[i, 0] = y[:, width : width + kv_width]
        v_ref[i, 0] = y[:, width + kv_width :]
        return 0

    lax.fori_loop(0, n, project, 0)
    for i in range(n // group):
        at = slice(i * group, (i + 1) * group)
        for j in range(heads):
            lanes = slice(j * HEAD, (j + 1) * HEAD)
            blocks = (i + 1) * group
            queries = q_ref[at, 0, :, lanes].reshape(group * length, HEAD) * HEAD ** (-0.5)
            keys = pick(k_ref, blocks, slots, slot_ref[j])
            values = pick(v_ref, blocks, slots, slot_ref[j])
            scores = masked_scores(queries.astype(BF), keys, i * group * length, seq_length)
            top = jnp.max(scores, axis=1, keepdims=True)
            probs = jnp.exp(scores - top)
            total = jnp.sum(probs, axis=1, keepdims=True)
            mixed = dot(probs.astype(BF), values) * (slot_ref[heads + j].astype(F32) / total)
            out_ref[at, 0, :, lanes] = mixed.reshape(group, length, HEAD)
            lse_ref[at, 0, :, j : j + 1] = (top + jnp.log(total)).reshape(group, length, 1)


def attn_forward(seq, slot, lengths, rows, w, width, before=()):
    n, seqs, length, depth = rows.shape
    kv_width = (w.shape[1] - width) // 2
    big = lambda w: pl.BlockSpec((n, 1, length, w), lambda s: (0, seq, 0, 0))
    smem = pl.BlockSpec(memory_space=pltpu.SMEM)
    outs = ((width, F32), (width // HEAD, F32), (width, BF), (kv_width, BF), (kv_width, BF))
    return pl.pallas_call(
        functools.partial(attn_fwd_kernel, seq),
        grid=(1,),
        in_specs=[smem, smem, big(depth), pl.BlockSpec(w.shape, lambda s: (0, 0))]
        + [pl.BlockSpec(memory_space=pl.ANY)] * len(before),
        out_specs=[big(c) for c, _ in outs],
        out_shape=[jax.ShapeDtypeStruct((n, seqs, length, c), t) for c, t in outs],
        input_output_aliases={4 + i: i for i in range(len(before))},
        compiler_params=pltpu.CompilerParams(vmem_limit_bytes=GIANT),
    )(slot, lengths, rows, w, *before)


def attn_bwd_kernel(slot_ref, len_ref, q_ref, k_ref, v_ref, d_ref, att_ref, lse_ref, stat_ref, gain_ref,
                    gq_ref, gk_ref, gv_ref, sums_ref, gk_acc, gv_acc, gh_ref):
    n, _, length, width = q_ref.shape
    heads, slots = width // HEAD, k_ref.shape[3] // HEAD
    group = 2
    seq_length = len_ref[pl.program_id(0)]
    @pl.when(pl.program_id(0) == 0)
    def _():
        sums_ref[...] = jnp.zeros_like(sums_ref)

    for i in range(n):
        scale, shift = stat_ref[i, 0][:, 0:1], stat_ref[i, 0][:, 1:2]
        d, attended = d_ref[i, 0], att_ref[i, 0]
        gh_ref[i] = (scale * (d * gain_ref[...] - attended * shift)).astype(BF)
        sums_ref[0:1] += jnp.sum(d * attended * scale, axis=0, keepdims=True)
    gk_acc[...] = jnp.zeros_like(gk_acc)
    gv_acc[...] = jnp.zeros_like(gv_acc)
    def block(i):
        at = slice(i * group, (i + 1) * group)
        blocks = (i + 1) * group
        for j in range(heads):
            lanes = slice(j * HEAD, (j + 1) * HEAD)
            slot = slot_ref[j]
            queries = q_ref[at, 0, :, lanes].reshape(group * length, HEAD) * HEAD ** (-0.5)
            queries = queries.astype(BF)
            keys = pick(k_ref, blocks, slots, slot)
            values = pick(v_ref, blocks, slots, slot)
            grad = gh_ref[at, :, lanes].reshape(group * length, HEAD)
            attended = att_ref[at, 0, :, lanes].reshape(group * length, HEAD)
            delta = jnp.sum(grad.astype(F32) * attended, axis=1, keepdims=True)
            lse = lse_ref[at, 0, :, j : j + 1].reshape(group * length, 1)
            scores = masked_scores(queries, keys, i * group * length, seq_length)
            probs = jnp.exp(scores - lse)
            grad_scores = (probs * (ntdot(grad, values) - delta)).astype(BF)
            gq = dot(grad_scores, keys) * HEAD ** (-0.5)
            gq_ref[at, 0, :, lanes] = gq.astype(BF).reshape(group, length, HEAD)
            rows = slice(0, blocks * length)
            gk_acc[slot, rows] += tndot(grad_scores, queries)
            gv_acc[slot, rows] += tndot(probs.astype(BF), grad)

    for i in range(n // group):
        pl.when(i * group * length < seq_length)(functools.partial(block, i))

        @pl.when(i * group * length >= seq_length)
        def _():
            gq_ref[i * group : (i + 1) * group] = jnp.zeros((group,) + gq_ref.shape[1:], BF)

    for other in range(slots):
        lanes = slice(other * HEAD, (other + 1) * HEAD)
        gk_ref[:, 0, :, lanes] = gk_acc[other].astype(BF).reshape(n, length, HEAD)
        gv_ref[:, 0, :, lanes] = gv_acc[other].astype(BF).reshape(n, length, HEAD)


def attn_backward(slot, lengths, q, k, v, d, att, lse, stats, gain):
    n, seqs, length, width = q.shape
    big = lambda w: pl.BlockSpec((n, 1, length, w), lambda s: (0, s, 0, 0))
    whole = lambda r: pl.BlockSpec((r, width), lambda s: (0, 0))
    smem = pl.BlockSpec(memory_space=pltpu.SMEM)
    kw = k.shape[3]
    return pl.pallas_call(
        attn_bwd_kernel,
        grid=(seqs,),
        in_specs=[smem, smem, big(width), big(kw), big(kw), big(width), big(width), big(width // HEAD),
                  big(stats.shape[3]), whole(1)],
        out_specs=[big(width), big(kw), big(kw), whole(8)],
        out_shape=[jax.ShapeDtypeStruct(x.shape, BF) for x in (q, k, v)]
        + [jax.ShapeDtypeStruct((8, width), F32)],
        scratch_shapes=[pltpu.VMEM((kw // HEAD, n * length, HEAD), F32)] * 2 + [pltpu.VMEM((n, length, width), BF)],
        compiler_params=pltpu.CompilerParams(vmem_limit_bytes=GIANT),
    )(slot, lengths, q, k, v, d, att, lse, stats, gain)


def signal_fwd_kernel(rows_ref, wx_ref, taps_ref, bias_ref, xp_ref, x_ref, pre_ref, mix_ref, low_ref, part_ref, xs_ref):
    length = rows_ref.shape[2]

    @pl.when(pl.program_id(1) == 0)
    def _():
        xs_ref[0:8] = jnp.zeros((8, xs_ref.shape[1]), F32)

    x = dot(rows_ref[0, 0], wx_ref[...]).astype(BF)
    x_ref[0, 0] = x
    xs_ref[8:] = x.astype(F32)
    first = 8 - (KCONV - 1)
    pre = bias_ref[...]
    for o in range(KCONV):
        pre = pre + taps_ref[o : o + 1] * xs_ref[first + o : first + o + length]
    xs_ref[0:8] = xs_ref[length : length + 8]
    pre_ref[0, 0] = pre
    mix = pre * jax.nn.sigmoid(pre)
    mix_ref[0, 0] = mix
    low_ref[0, 0] = mix.astype(BF)
    part_ref[0, 0] = ntdot(mix.astype(BF), xp_ref[...]).astype(BF)


def signal_forward(rows, wx, taps, bias, xp):
    n, seqs, length, width = rows.shape
    cols = wx.shape[1]
    big = lambda w: pl.BlockSpec((1, 1, length, w), lambda s, i: (i, s, 0, 0))
    whole = lambda a: pl.BlockSpec(a.shape, lambda s, i: (0, 0))
    shape = lambda w, t: jax.ShapeDtypeStruct((n, seqs, length, w), t)
    return pl.pallas_call(
        signal_fwd_kernel,
        grid=(seqs, n),
        in_specs=[big(width), whole(wx), whole(taps), whole(bias), whole(xp)],
        out_specs=[big(cols)] * 4 + [big(xp.shape[0])],
        out_shape=[shape(cols, BF), shape(cols, F32), shape(cols, F32), shape(cols, BF), shape(xp.shape[0], BF)],
        scratch_shapes=[pltpu.VMEM((length + 8, cols), F32)],
        compiler_params=pltpu.CompilerParams(vmem_limit_bytes=GIANT),
    )(rows, wx, taps, bias, xp)


def signal_bwd_kernel(gmix_ref, gproj_ref, xp_ref, pre_ref, x_ref, last_ref, taps_ref, gx_ref, sums_ref, gs_ref, xs_ref):
    length = gmix_ref.shape[2]
    edge = KCONV - 1
    i = pl.program_id(1)

    @pl.when((i == 0) & (pl.program_id(0) == 0))
    def _():
        sums_ref[...] = jnp.zeros_like(sums_ref)

    @pl.when(i == 0)
    def _():
        gs_ref[length:] = jnp.zeros((8, gs_ref.shape[1]), F32)

    grad = gmix_ref[0, 0] + dot(gproj_ref[0, 0], xp_ref[...])
    grad = grad * silu_grad(pre_ref[0, 0])
    gs_ref[:length] = grad
    first_block = (i == pl.num_programs(1) - 1).astype(F32)
    xs_ref[0:16] = last_ref[0, 0].astype(F32) * (1.0 - first_block)
    xs_ref[16:] = x_ref[0, 0].astype(F32)
    total = None
    for o in range(KCONV):
        term = taps_ref[o : o + 1] * gs_ref[edge - o : edge - o + length]
        total = term if total is None else total + term
        at = 16 - edge + o
        sums_ref[o : o + 1] += jnp.sum(grad * xs_ref[at : at + length], axis=0, keepdims=True)
    sums_ref[KCONV : KCONV + 1] += jnp.sum(grad, axis=0, keepdims=True)
    gx_ref[0, 0] = total.astype(BF)
    gs_ref[length:] = gs_ref[0:8]


def signal_backward(gmix, gproj, xp, pre, x, taps):
    n, seqs, length, cols = gmix.shape
    at = lambda s, i: (n - 1 - i, s, 0, 0)
    big = lambda w: pl.BlockSpec((1, 1, length, w), at)
    whole = lambda a: pl.BlockSpec(a.shape, lambda s, i: (0, 0))
    before = lambda s, i: (jnp.maximum(n - 2 - i, 0), s, length // 16 - 1, 0)
    return pl.pallas_call(
        signal_bwd_kernel,
        grid=(seqs, n),
        in_specs=[big(cols), big(xp.shape[0]), whole(xp), big(cols), big(cols),
                  pl.BlockSpec((1, 1, 16, cols), before), whole(taps)],
        out_specs=[big(cols), pl.BlockSpec((8, cols), lambda s, i: (0, 0))],
        out_shape=[jax.ShapeDtypeStruct(gmix.shape, BF), jax.ShapeDtypeStruct((8, cols), F32)],
        scratch_shapes=[pltpu.VMEM((length + 8, cols), F32), pltpu.VMEM((length + 16, cols), F32)],
        compiler_params=pltpu.CompilerParams(vmem_limit_bytes=GIANT),
    )(gmix, gproj, xp, pre, x, x, taps)


def norm_kernel(sq_ref, att_ref, again_ref, core_ref, z_ref, sgain_ref, attn_ref, ssm_ref):
    sq = sq_ref[0]
    r_attn = lax.rsqrt(sq[:, 0:1] / (HEADS * HEAD) + EPSILON)
    r_ssm = lax.rsqrt(sq[:, 1:2] / INNER + EPSILON)
    attn_ref[0] = (att_ref[0] * r_attn * again_ref[...]).astype(BF)
    z = z_ref[0]
    ssm_ref[0] = (core_ref[0] * (z * jax.nn.sigmoid(z)) * r_ssm * sgain_ref[...]).astype(BF)


def norm_both(squares, attended, attn_gain, core, z, ssm_gain):
    n, rows, _ = squares.shape
    block = lambda c: pl.BlockSpec((1, rows, c), lambda i: (i, 0, 0))
    whole = lambda a: pl.BlockSpec(a.shape, lambda i: (0, 0))
    aw, sw = attended.shape[2], core.shape[2]
    return pl.pallas_call(
        norm_kernel,
        grid=(n,),
        in_specs=[block(2), block(aw), whole(attn_gain), block(sw), block(sw), whole(ssm_gain)],
        out_specs=[block(aw), block(sw)],
        out_shape=[jax.ShapeDtypeStruct((n, rows, w), BF) for w in (aw, sw)],
        compiler_params=pltpu.CompilerParams(vmem_limit_bytes=GIANT),
    )(squares, attended, attn_gain, core, z, ssm_gain)


def ffn_bwd_kernel(u_ref, down_ref, gate_ref, up_ref, ggate_ref, gup_ref):
    grad = ntdot(u_ref[0], down_ref[...])
    gate, up = gate_ref[0].astype(F32), up_ref[0].astype(F32)
    logistic = jax.nn.sigmoid(gate)
    ggate_ref[0] = (grad * up * (logistic * (1.0 + gate * (1.0 - logistic)))).astype(BF)
    gup_ref[0] = (grad * (gate * logistic)).astype(BF)


def ffn_backward(upstream, w_down, gate, up):
    n, rows, hidden = gate.shape
    block = lambda c: pl.BlockSpec((1, rows, c), lambda i: (i, 0, 0))
    return pl.pallas_call(
        ffn_bwd_kernel,
        grid=(n,),
        in_specs=[block(upstream.shape[2]), pl.BlockSpec(w_down.shape, lambda i: (0, 0)), block(hidden), block(hidden)],
        out_specs=[block(hidden)] * 2,
        out_shape=[jax.ShapeDtypeStruct(gate.shape, BF)] * 2,
        compiler_params=pltpu.CompilerParams(vmem_limit_bytes=GIANT),
    )(upstream, w_down, gate, up)


def greet(peers, axis="seq"):
    barrier = pltpu.get_barrier_semaphore()
    for peer in peers:
        pl.semaphore_signal(barrier, inc=1, device_id={axis: peer}, device_id_type=MESH)
    pl.semaphore_wait(barrier, len(peers))

def send(src, dst, send_sem, recv_sem, peer, axis="seq"):
    return pltpu.make_async_remote_copy(src_ref=src, dst_ref=dst, send_sem=send_sem, recv_sem=recv_sem,
        device_id={axis: peer}, device_id_type=MESH)

def ag_parts(n, x_ref, o_ref, local_sem, far_send, far_recv, near_send, near_recv):
    me = lax.axis_index("seq")
    core, chip, chips = me % 2, me // 2, n // 2
    sib = me + 1 - 2 * core
    far = [((chip + d) % chips) * 2 + core for d in range(1, chips)]
    mine = pltpu.make_async_copy(x_ref, o_ref.at[me], local_sem)
    out = [
        send(x_ref, o_ref.at[me], far_send.at[d], far_recv.at[d], far[d - 1]) for d in range(1, chips)
    ]
    near = [send(x_ref, o_ref.at[me], near_send.at[0], near_recv.at[0], sib)]

    def begin():
        for c in [mine] + out + near:
            c.start()

    def finish():
        for d in range(1, chips):
            out[d - 1].wait_recv()
            block = ((chip + chips - d) % chips) * 2 + core
            c = send(o_ref.at[block], o_ref.at[block], near_send.at[d], near_recv.at[d], sib)
            c.start()
            near.append(c)
        mine.wait()
        for c in near:
            c.wait()
        for c in out:
            c.wait_send()

    return begin, finish


def ag_kernel(n, x_ref, o_ref, *sems):
    me = lax.axis_index("seq")
    core, chip, chips = me % 2, me // 2, n // 2
    greet([me + 1 - 2 * core] + [((chip + d) % chips) * 2 + core for d in range(1, chips)])
    begin, finish = ag_parts(n, x_ref, o_ref, *sems)
    begin()
    finish()


def all_gather_any(x, n, cid):
    chips = n // 2
    return pl.pallas_call(functools.partial(ag_kernel, n),
        out_shape=jax.ShapeDtypeStruct((n,) + x.shape, x.dtype),
        in_specs=[pl.BlockSpec(memory_space=pl.ANY)],
        out_specs=pl.BlockSpec(memory_space=pl.ANY),
        scratch_shapes=[pltpu.SemaphoreType.DMA] + [pltpu.SemaphoreType.DMA((chips,))] * 4,
        compiler_params=pltpu.CompilerParams(collective_id=cid, has_side_effects=True),
    )(x)

def rs_kernel(n, p_ref, after_ref, o_ref, own, near, sums, got, local_sem, near_send, near_recv, far_send, far_recv):
    me = lax.axis_index("seq")
    core, chip, chips = me % 2, me // 2, n // 2
    sib = me + 1 - 2 * core
    step = lambda d: (chip + d) % chips
    far = [step(d) * 2 + core for d in range(1, chips)]
    greet([sib] + far)
    order = list(range(1, chips)) + [0]
    loads, nears, fars = {}, {}, {}
    for d in order:
        nears[d] = send(p_ref.at[step(d) * 2 + 1 - core], near.at[d], near_send.at[d], near_recv.at[d], sib)
        nears[d].start()
        loads[d] = pltpu.make_async_copy(p_ref.at[step(d) * 2 + core], own.at[d], local_sem.at[d])
        loads[d].start()
    rows = own.shape[1]
    slab = 16
    def each(body):
        def run(i, _):
            body(pl.ds(pl.multiple_of(i * slab, slab), slab))
            return 0
        lax.fori_loop(0, rows // slab, run, 0, unroll=2)
    for d in order:
        loads[d].wait()
        nears[d].wait_recv()
        if d:
            def add(at):
                sums[d - 1, at] = (own[d, at].astype(F32) + near[d, at].astype(F32)).astype(BF)
            each(add)
            fars[d] = send(sums.at[d - 1], got.at[d - 1], far_send.at[d - 1], far_recv.at[d - 1], far[d - 1])
            fars[d].start()
        else:
            def add(at):
                o_ref[at] = own[0, at].astype(F32) + near[0, at].astype(F32)
            each(add)
    for d in range(1, chips):
        fars[d].wait_recv()
        def add(at):
            o_ref[at] = o_ref[at] + got[d - 1, at].astype(F32)
        each(add)
    for d in order:
        nears[d].wait_send()
        if d: fars[d].wait_send()

def reduce_scatter_any(p, after, n, cid):
    chips = n // 2
    blk = p.shape[1:]
    return pl.pallas_call(functools.partial(rs_kernel, n),
        out_shape=jax.ShapeDtypeStruct(blk, F32),
        in_specs=[pl.BlockSpec(memory_space=pl.ANY)] * 2,
        out_specs=pl.BlockSpec(memory_space=pltpu.VMEM),
        scratch_shapes=[pltpu.VMEM((chips,) + blk, p.dtype), pltpu.VMEM((chips,) + blk, p.dtype),
            pltpu.VMEM((chips-1,) + blk, p.dtype), pltpu.VMEM((chips-1,) + blk, p.dtype),
            pltpu.SemaphoreType.DMA((chips,)), pltpu.SemaphoreType.DMA((chips,)), pltpu.SemaphoreType.DMA((chips,)),
            pltpu.SemaphoreType.DMA((chips-1,)), pltpu.SemaphoreType.DMA((chips-1,))],
        compiler_params=pltpu.CompilerParams(collective_id=cid, has_side_effects=True, vmem_limit_bytes=GIANT),
    )(p, after)

def stat_kernel(n, axis, x_ref, o_ref, got, send_sem, recv_sem):
    me = lax.axis_index(axis)
    peers = [(me + d) % n for d in range(1, n)]
    greet(peers, axis)
    copies = []
    for d in range(1, n):
        c = send(x_ref, got.at[d - 1], send_sem.at[d - 1], recv_sem.at[d - 1], peers[d - 1], axis)
        c.start()
        copies.append(c)
    total = x_ref[...]
    for d in range(1, n):
        copies[d - 1].wait_recv()
        total = total + got[d - 1]
    o_ref[...] = total
    for c in copies:
        c.wait_send()


def small_sum(x, n, cid, axis="seq"):
    return pl.pallas_call(
        functools.partial(stat_kernel, n, axis),
        out_shape=jax.ShapeDtypeStruct(x.shape, F32),
        in_specs=[pl.BlockSpec(memory_space=pltpu.VMEM)],
        out_specs=pl.BlockSpec(memory_space=pltpu.VMEM),
        scratch_shapes=[pltpu.VMEM((n - 1,) + x.shape, F32)] + [pltpu.SemaphoreType.DMA((n - 1,))] * 2,
        compiler_params=pltpu.CompilerParams(collective_id=cid, has_side_effects=True, vmem_limit_bytes=GIANT),
    )(x)


def square(me):
    core, x, y = me % 2, (me // 2) % 2, me // 4
    seat = lambda yy, xx, cc: (yy * 2 + xx) * 2 + cc
    return core, (seat(y, x, 1 - core), seat(y, 1 - x, core), seat(1 - y, x, core), seat(1 - y, 1 - x, core))

def ag4_parts(n, x_ref, o_ref, local_sem, far_send, far_recv, near_send, near_recv):
    me = lax.axis_index("seq")
    core, (sib, east, north, across) = square(me)
    half = x_ref.shape[0] // 2
    cut = (pl.ds(0, half), pl.ds(half, half))
    mine = pltpu.make_async_copy(x_ref, o_ref.at[me], local_sem)
    far, near = {}, []
    for slot, h, peer in ((0, 0, east), (2, 1, north), (1, 1, east), (3, 0, north)):
        far[slot] = send(x_ref.at[cut[h]], o_ref.at[me, cut[h]], far_send.at[slot], far_recv.at[slot], peer)
    near.append(send(x_ref, o_ref.at[me], near_send.at[6], near_recv.at[6], sib))

    def begin():
        mine.start()
        for slot in (0, 2, 1, 3):
            far[slot].start()
        near[0].start()

    def pass_on(slot, block, h):
        ref = o_ref.at[block, cut[h]]
        c = send(ref, ref, near_send.at[slot], near_recv.at[slot], sib)
        c.start()
        near.append(c)

    def finish():
        for slot, block, h, relay, to in (
            (0, east, 0, 4, north), (2, north, 1, 5, east), (1, east, 1, None, None), (3, north, 0, None, None)
        ):
            far[slot].wait_recv()
            if relay is not None:
                ref = o_ref.at[block, cut[h]]
                far[relay] = send(ref, ref, far_send.at[relay], far_recv.at[relay], to)
                far[relay].start()
            pass_on(slot, block, h)
        for slot, h in ((4, 0), (5, 1)):
            far[slot].wait_recv()
            pass_on(slot, across, h)
        mine.wait()
        for c in near:
            c.wait()
        for c in far.values():
            c.wait_send()

    return begin, finish


def ag4_kernel(x_ref, o_ref, *sems):
    core, (sib, east, north, across) = square(lax.axis_index("seq"))
    greet([sib, east, north])
    begin, finish = ag4_parts(8, x_ref, o_ref, *sems)
    begin()
    finish()


def all_gather4(x, n, cid):
    return pl.pallas_call(ag4_kernel,
        out_shape=jax.ShapeDtypeStruct((n,) + x.shape, x.dtype),
        in_specs=[pl.BlockSpec(memory_space=pl.ANY)],
        out_specs=pl.BlockSpec(memory_space=pl.ANY),
        scratch_shapes=[pltpu.SemaphoreType.DMA] + [pltpu.SemaphoreType.DMA((6,))] * 2 + [pltpu.SemaphoreType.DMA((7,))] * 2,
        compiler_params=pltpu.CompilerParams(collective_id=cid, has_side_effects=True),
    )(x)

def rs4_kernel(p_ref, after_ref, o_ref, own, near, got, local_sem, near_send, near_recv, far_send, far_recv):
    me = lax.axis_index("seq")
    core, (sib, east, north, across) = square(me)
    greet([sib, east, north])
    rows = own.shape[1]
    half = rows // 2
    cut = (pl.ds(0, half), pl.ds(half, half))
    seats = (across, east, north, me)
    loads, nears, far = [], [], {}
    for i, seat in enumerate(seats):
        other = seat + 1 - 2 * core
        c = send(p_ref.at[other], near.at[i], near_send.at[i], near_recv.at[i], sib)
        c.start(); nears.append(c)
        c = pltpu.make_async_copy(p_ref.at[seat], own.at[i], local_sem.at[i])
        c.start(); loads.append(c)
    slab = 16
    def each(first, count, body):
        def run(i, _):
            body(pl.ds(pl.multiple_of(first + i * slab, slab), slab), pl.ds(pl.multiple_of(i * slab, slab), slab))
            return 0
        lax.fori_loop(0, count // slab, run, 0, unroll=2)
    def fold(i):
        loads[i].wait(); nears[i].wait_recv()
        def add(at, _):
            own[i, at] = (own[i, at].astype(F32) + near[i, at].astype(F32)).astype(own.dtype)
        each(0, rows, add)
    def go(slot, i, h, peer):
        far[slot] = send(own.at[i, cut[h]], got.at[slot], far_send.at[slot], far_recv.at[slot], peer)
        far[slot].start()
    fold(0)
    go(0, 0, 0, east)
    go(1, 0, 1, north)
    fold(1)
    go(2, 1, 0, east)
    fold(2)
    go(3, 2, 1, north)
    def join(i, h, slot):
        far[slot].wait_recv()
        def add(at, src):
            own[i, at] = (own[i, at].astype(F32) + got[slot, src].astype(F32)).astype(own.dtype)
        each(h * half, half, add)
    join(2, 0, 0)
    go(4, 2, 0, north)
    join(1, 1, 1)
    go(5, 1, 1, east)
    loads[3].wait(); nears[3].wait_recv()
    def first(h, slot):
        far[slot].wait_recv()
        def add(at, src):
            o_ref[at] = own[3, at].astype(F32) + near[3, at].astype(F32) + got[slot, src].astype(F32)
        each(h * half, half, add)
    first(0, 2)
    first(1, 3)
    def last(h, slot):
        far[slot].wait_recv()
        def add(at, src):
            o_ref[at] = o_ref[at] + got[slot, src].astype(F32)
        each(h * half, half, add)
    last(0, 4)
    last(1, 5)
    for c in nears: c.wait_send()
    for c in far.values(): c.wait_send()

def reduce_scatter4(p, after, n, cid):
    blk = p.shape[1:]
    return pl.pallas_call(rs4_kernel,
        out_shape=jax.ShapeDtypeStruct(blk, F32),
        in_specs=[pl.BlockSpec(memory_space=pl.ANY)] * 2,
        out_specs=pl.BlockSpec(memory_space=pltpu.VMEM),
        scratch_shapes=[pltpu.VMEM((4,) + blk, p.dtype), pltpu.VMEM((4,) + blk, p.dtype),
            pltpu.VMEM((6, blk[0] // 2) + blk[1:], p.dtype)] + [pltpu.SemaphoreType.DMA((4,))] * 3 + [pltpu.SemaphoreType.DMA((6,))] * 2,
        compiler_params=pltpu.CompilerParams(collective_id=cid, has_side_effects=True, vmem_limit_bytes=GIANT),
    )(p, after)


def start_kernel(n, moves, x_ref, gain_ref, w_ref, in_ref, o_ref, c_ref, first_ref, second_ref,
                 normed_ref, cols_ref, swap_sem, swap_send, swap_recv, *sems):
    me = lax.axis_index("seq")
    others = [(me + d) % n for d in range(1, n)]
    barrier = pltpu.get_barrier_semaphore()
    for peer in others:
        pl.semaphore_signal(barrier, inc=1, device_id={"seq": peer}, device_id_type=MESH)
    x = x_ref[...].astype(F32)
    scale = lax.rsqrt(jnp.mean(x * x, axis=-1, keepdims=True) + EPSILON)
    normed_ref[...] = (x * scale * gain_ref[...]).astype(BF)
    pl.semaphore_wait(barrier, n - 1)
    gather_start, gather_end = (ag4_parts if n == 8 else ag_parts)(n, normed_ref, o_ref, *sems)
    gather_start()
    for i in range(n):
        if sum(size for _, _, size in moves[i]) < cols_ref.shape[2]:
            cols_ref[i] = jnp.zeros(cols_ref.shape[1:], BF)
        for dst, src, size in moves[i]:
            cols_ref[i, :, dst : dst + size] = w_ref[:, src : src + size]
    own = pltpu.make_async_copy(cols_ref.at[me], c_ref.at[me], swap_sem)
    own.start()
    swaps = []
    for d in range(1, n):
        peer = others[d - 1]
        c = send(cols_ref.at[peer], c_ref.at[me], swap_send.at[d - 1], swap_recv.at[d - 1], peer)
        c.start()
        swaps.append(c)
    width = first_ref.shape[2]
    for i in range(n):
        first_ref[i] = in_ref[:, i * width : (i + 1) * width]
        second_ref[i] = in_ref[:, (n + i) * width : (n + i + 1) * width]
    gather_end()
    own.wait()
    for c in swaps:
        c.wait()


def gather_and_exchange(x, gain, w, moves, width, w_in, n, cid):
    far, near = (6, 7) if n == 8 else (n // 2, n // 2)
    anywhere = pl.BlockSpec(memory_space=pl.ANY)
    vmem = pl.BlockSpec(memory_space=pltpu.VMEM)
    dma = pltpu.SemaphoreType.DMA
    cols = jax.ShapeDtypeStruct((n, w.shape[0], width), BF)
    part = jax.ShapeDtypeStruct((n, w_in.shape[0], w_in.shape[1] // (2 * n)), BF)
    return pl.pallas_call(
        functools.partial(start_kernel, n, moves),
        out_shape=[jax.ShapeDtypeStruct((n,) + x.shape, BF), cols, part, part],
        in_specs=[vmem] * 4,
        out_specs=[anywhere] * 2 + [vmem] * 2,
        scratch_shapes=[pltpu.VMEM(x.shape, BF), pltpu.VMEM(cols.shape, BF), dma, dma((n - 1,)), dma((n - 1,)),
                        dma, dma((far,)), dma((far,)), dma((near,)), dma((near,))],
        compiler_params=pltpu.CompilerParams(collective_id=cid, has_side_effects=True, vmem_limit_bytes=GIANT),
    )(x, gain[None], w, w_in)


def all_gather(x, n, cid):
    return (all_gather4 if n == 8 else all_gather_any)(x, n, cid)


def reduce_scatter(p, n, cid, after=None):
    after = jnp.zeros((8, 128), F32) if after is None else after
    return (reduce_scatter4 if n == 8 else reduce_scatter_any)(p, after, n, cid)


def mm_rs4_kernel(turned, *refs):
    terms = len(turned)
    a_refs, b_refs = refs[:terms], refs[terms : 2 * terms]
    after_ref, o_ref, part, near, got, near_send, near_recv, far_send, far_recv = refs[2 * terms :]
    me = lax.axis_index("seq")
    core, (sib, east, north, across) = square(me)
    x, y = (me // 2) % 2, me // 4
    greet([sib, east, north])
    rows = part.shape[2]
    half = rows // 2
    cut = (pl.ds(0, half), pl.ds(half, half))
    slab = 16
    own = part.at[1]

    def near_copy(i):
        return send(part.at[0, i], near.at[i], near_send.at[i], near_recv.at[i], sib)

    hops = ((0, 0, east), (0, 1, north), (1, 0, east), (2, 1, north), (2, 0, north), (1, 1, east))

    def far_copy(slot):
        i, h, peer = hops[slot]
        return send(own.at[i, cut[h]], got.at[slot], far_send.at[slot], far_recv.at[slot], peer)

    def each(first, count, body):
        def run(i, _):
            at = pl.multiple_of(i * slab, slab)
            body(pl.ds(pl.multiple_of(first + at, slab), slab), pl.ds(at, slab))
            return 0

        lax.fori_loop(0, count // slab, run, 0, unroll=2)

    def fold(i):
        near_copy(i).wait_recv()

        def add(at, _):
            own[i, at] = (own[i, at].astype(F32) + near[i, at].astype(F32)).astype(BF)

        each(0, rows, add)

    def step(s, _):
        i, mine = s // 2, s % 2
        yy, xx = (y + (i + 1) % 2) % 2, (x + 1 - i // 2) % 2
        seat = (yy * 2 + xx) * 2 + (core + 1 - mine) % 2
        total = None
        for a, b, t in zip(a_refs, b_refs, turned):
            term = (ntdot if t else dot)(a[seat], b[...])
            total = term if total is None else total + term
        part[mine, i] = total.astype(BF)

        @pl.when(mine == 0)
        def _():
            near_copy(i).start()

        @pl.when(s == 3)
        def _():
            fold(0)
            far_copy(0).start()
            far_copy(1).start()

        @pl.when(s == 5)
        def _():
            fold(1)
            far_copy(2).start()

        @pl.when(s == 6)
        def _():
            fold(2)
            far_copy(3).start()

        return 0

    lax.fori_loop(0, 8, step, 0)

    def join(i, h, slot):
        far_copy(slot).wait_recv()

        def add(at, src):
            own[i, at] = (own[i, at].astype(F32) + got[slot, src].astype(F32)).astype(BF)

        each(h * half, half, add)

    join(2, 0, 0)
    far_copy(4).start()
    join(1, 1, 1)
    far_copy(5).start()
    near_copy(3).wait_recv()

    def first(h, slot):
        far_copy(slot).wait_recv()

        def add(at, src):
            o_ref[at] = own[3, at].astype(F32) + near[3, at].astype(F32) + got[slot, src].astype(F32)

        each(h * half, half, add)

    first(0, 2)
    first(1, 3)

    def last(h, slot):
        far_copy(slot).wait_recv()

        def add(at, src):
            o_ref[at] = o_ref[at] + got[slot, src].astype(F32)

        each(h * half, half, add)

    last(0, 4)
    last(1, 5)
    for i in range(4):
        near_copy(i).wait_send()
    for slot in range(6):
        far_copy(slot).wait_send()


def product_scatter(pairs, n, cid, after=None):
    after = jnp.zeros((8, 128), F32) if after is None else after
    rows = pairs[0][0].shape[0] // n
    cols = pairs[0][1].shape[0 if pairs[0][2] else 1]
    if n != 8:
        total = sum((ntdot if t else dot)(a, b) for a, b, t in pairs)
        return reduce_scatter(total.astype(BF).reshape(n, rows, cols), n, cid, after)
    vmem = pl.BlockSpec(memory_space=pltpu.VMEM)
    dma = pltpu.SemaphoreType.DMA
    return pl.pallas_call(
        functools.partial(mm_rs4_kernel, tuple(t for _, _, t in pairs)),
        out_shape=jax.ShapeDtypeStruct((rows, cols), F32),
        in_specs=[vmem] * (2 * len(pairs)) + [pl.BlockSpec(memory_space=pl.ANY)],
        out_specs=vmem,
        scratch_shapes=[
            pltpu.VMEM((2, 4, rows, cols), BF),
            pltpu.VMEM((4, rows, cols), BF),
            pltpu.VMEM((6, rows // 2, cols), BF),
            dma((4,)), dma((4,)), dma((6,)), dma((6,)),
        ],
        compiler_params=pltpu.CompilerParams(collective_id=cid, has_side_effects=True, vmem_limit_bytes=GIANT),
    )(*(a.reshape(n, rows, a.shape[1]) for a, _, _ in pairs), *(b for _, b, _ in pairs), after)


def chain_kernel(axis, count, cuts, *refs):
    arrays = len(cuts)
    x_refs, after_ref, o_refs = refs[:arrays], refs[arrays], refs[arrays + 1 : 2 * arrays + 1]
    rest = refs[2 * arrays + 1 :]
    up_in, up_out, down_in, down_out = (rest[k * arrays : (k + 1) * arrays] for k in range(4))
    up_send, up_recv, down_send, down_recv = rest[4 * arrays :]
    me = lax.axis_index(axis)
    first, last = me == 0, me == count - 1
    above, below = (me + 1) % count, (me + count - 1) % count
    barrier = pltpu.get_barrier_semaphore()

    @pl.when(me > 0)
    def _():
        pl.semaphore_signal(barrier, inc=1, device_id={axis: below}, device_id_type=MESH)

    @pl.when(me < count - 1)
    def _():
        pl.semaphore_signal(barrier, inc=1, device_id={axis: above}, device_id_type=MESH)

    @pl.when((me > 0) & (me < count - 1))
    def _():
        pl.semaphore_wait(barrier, 2)

    @pl.when(first | last)
    def _():
        pl.semaphore_wait(barrier, 1)

    pieces = [(k, c) for k in range(arrays) for c in range(cuts[k])]
    lane = lambda k: x_refs[k].shape[1] // cuts[k]
    at = lambda k, c: slice(c * lane(k), (c + 1) * lane(k))

    def up(s, k, c):
        return send(up_out[k].at[c], up_in[k].at[c], up_send.at[s], up_recv.at[s], above, axis)

    def down(s, k, c):
        return send(down_out[k].at[c], down_in[k].at[c], down_send.at[s], down_recv.at[s], below, axis)

    for s, (k, c) in enumerate(pieces):
        own = x_refs[k][:, at(k, c)]

        @pl.when(first)
        def _():
            up_out[k][c] = own
            up(s, k, c).start()

        @pl.when(last)
        def _():
            down_out[k][c] = own
            down(s, k, c).start()

    own = lambda s: x_refs[pieces[s][0]][:, at(*pieces[s])].astype(F32)

    def serve_up(s):
        k, c = pieces[s]

        @pl.when(me > 0)
        def _():
            up(s, k, c).wait_recv()

            @pl.when(me < count - 1)
            def _():
                up_out[k][c] = (own(s) + up_in[k][c].astype(F32)).astype(BF)
                up(s, k, c).start()

    def serve_down(s):
        k, c = pieces[s]

        @pl.when(me < count - 1)
        def _():
            down(s, k, c).wait_recv()

            @pl.when(me > 0)
            def _():
                down_out[k][c] = (own(s) + down_in[k][c].astype(F32)).astype(BF)
                down(s, k, c).start()

    def finish(s):
        k, c = pieces[s]
        put = lambda value: o_refs[k].__setitem__((slice(None), at(k, c)), value)

        @pl.when(first)
        def _():
            put(own(s) + down_in[k][c].astype(F32))

        @pl.when(last)
        def _():
            put(own(s) + up_in[k][c].astype(F32))

        @pl.when((me > 0) & (me < count - 1))
        def _():
            put(own(s) + up_in[k][c].astype(F32) + down_in[k][c].astype(F32))

    for s in range(len(pieces) + 1):
        for side, early, late in ((me * 2 < count, serve_up, serve_down), (me * 2 >= count, serve_down, serve_up)):
            @pl.when(side)
            def _():
                if s < len(pieces):
                    early(s)
                if s:
                    late(s - 1)

        if s:
            finish(s - 1)

    for s, (k, c) in enumerate(pieces):
        @pl.when(me < count - 1)
        def _():
            up(s, k, c).wait_send()

        @pl.when(me > 0)
        def _():
            down(s, k, c).wait_send()


def chain_sum(arrays, cuts, count, cid, after, axis="dp"):
    vmem = pl.BlockSpec(memory_space=pltpu.VMEM)
    total = sum(cuts)
    slots = [pltpu.VMEM((c, a.shape[0], a.shape[1] // c), BF) for a, c in zip(arrays, cuts)]
    return pl.pallas_call(
        functools.partial(chain_kernel, axis, count, tuple(cuts)),
        out_shape=[jax.ShapeDtypeStruct(a.shape, F32) for a in arrays],
        in_specs=[vmem] * len(arrays) + [pl.BlockSpec(memory_space=pl.ANY)],
        out_specs=[vmem] * len(arrays),
        scratch_shapes=slots * 4 + [pltpu.SemaphoreType.DMA((total,))] * 4,
        compiler_params=pltpu.CompilerParams(collective_id=cid, has_side_effects=True, vmem_limit_bytes=GIANT),
    )(*arrays, after)


def gather_product4_kernel(body, weights, aligned, x_ref, *refs):
    w_refs, refs = refs[:weights], refs[weights:]
    row_refs, o_ref = refs[:aligned], refs[aligned]
    results, (mine_sem, far_send, far_recv, near_send, near_recv) = refs[aligned + 1 : -5], refs[-5:]
    me = lax.axis_index("seq")
    core, (sib, east, north, across) = square(me)
    x, y = (me // 2) % 2, me // 4
    greet([sib, east, north])
    half = x_ref.shape[0] // 2
    cut = (pl.ds(0, half), pl.ds(half, half))
    hops = (
        (me, 0, east), (me, 1, east), (me, 1, north), (me, 0, north), (east, 0, north), (north, 1, east)
    )
    handed = ((east, 0), (east, 1), (north, 1), (north, 0), (across, 0), (across, 1))

    def far(slot):
        block, h, peer = hops[slot]
        ref = o_ref.at[block, cut[h]]
        return send(x_ref.at[cut[h]] if slot < 4 else ref, ref, far_send.at[slot], far_recv.at[slot], peer)

    def near(slot):
        if slot == 6:
            return send(x_ref, o_ref.at[me], near_send.at[6], near_recv.at[6], sib)
        block, h = handed[slot]
        ref = o_ref.at[block, cut[h]]
        return send(ref, ref, near_send.at[slot], near_recv.at[slot], sib)

    mine = pltpu.make_async_copy(x_ref, o_ref.at[me], mine_sem)
    mine.start()
    for slot in (0, 2, 1, 3):
        far(slot).start()
    near(6).start()

    def arrive(slot, relay=None):
        far(slot).wait_recv()
        if relay is not None:
            far(relay).start()
        near(slot).start()

    def step(s, _):
        @pl.when(s == 0)
        def _():
            mine.wait()

        @pl.when(s == 1)
        def _():
            near(6).wait_recv()

        @pl.when(s == 2)
        def _():
            arrive(0, 4)
            arrive(2, 5)
            arrive(1)

        @pl.when(s == 3)
        def _():
            near(0).wait_recv()
            near(1).wait_recv()

        @pl.when(s == 4)
        def _():
            arrive(3)

        @pl.when(s == 5)
        def _():
            near(2).wait_recv()
            near(3).wait_recv()

        @pl.when(s == 6)
        def _():
            arrive(4)
            arrive(5)

        @pl.when(s == 7)
        def _():
            near(4).wait_recv()
            near(5).wait_recv()

        pair = s // 2
        seat = (((y + pair // 2) % 2) * 2 + (x + pair % 2) % 2) * 2 + (core + s) % 2
        for ref, value in zip(results, body(o_ref[seat], *w_refs, *(ref[seat] for ref in row_refs))):
            ref[seat] = value.astype(ref.dtype)
        return 0

    lax.fori_loop(0, 8, step, 0)
    for slot in range(7):
        near(slot).wait_send()
    for slot in range(6):
        far(slot).wait_send()


def gather_product(body, x, weights, outs, n, cid, by_rows=()):
    rows = x.shape[0]
    if n != 8:
        whole = all_gather(x, n, cid)
        values = body(
            whole.reshape(n * rows, -1), *weights, *(a.reshape(n * rows, a.shape[2]) for a in by_rows)
        )
        return [whole] + [v.astype(t).reshape(n, rows, -1) for v, (_, t) in zip(values, outs)]
    vmem = pl.BlockSpec(memory_space=pltpu.VMEM)
    dma = pltpu.SemaphoreType.DMA
    return pl.pallas_call(
        functools.partial(gather_product4_kernel, body, len(weights), len(by_rows)),
        out_shape=[jax.ShapeDtypeStruct((n,) + x.shape, x.dtype)]
        + [jax.ShapeDtypeStruct((n, rows, c), t) for c, t in outs],
        in_specs=[vmem] * (1 + len(weights) + len(by_rows)),
        out_specs=[vmem] * (1 + len(outs)),
        scratch_shapes=[dma, dma((6,)), dma((6,)), dma((7,)), dma((7,))],
        compiler_params=pltpu.CompilerParams(collective_id=cid, has_side_effects=True, vmem_limit_bytes=GIANT),
    )(x, *weights, *by_rows)


class HeadPlan:
    def __init__(self, n):
        self.n = n
        self.per = -(-HEADS // n)
        group = HEADS // KVH
        self.first_kv, self.slots = [], 1
        for i in range(n):
            low, high = i * self.per, min((i + 1) * self.per, HEADS) - 1
            if low >= HEADS:
                self.first_kv.append(KVH)
            else:
                self.first_kv.append(low // group)
                self.slots = max(self.slots, high // group - low // group + 1)
        self.width = self.per * HEAD
        self.kv_width = self.slots * HEAD

    def head_table(self):
        group = HEADS // KVH
        rows = []
        for i in range(self.n):
            heads = [i * self.per + j for j in range(self.per)]
            rows.append(
                [h // group - self.first_kv[i] if h < HEADS else 0 for h in heads]
                + [int(h < HEADS) for h in heads]
            )
        return jnp.array(rows, jnp.int32)

    def kv_used(self, i):
        group = HEADS // KVH
        heads = range(i * self.per, min((i + 1) * self.per, HEADS))
        return sorted({h // group for h in heads})

    def moves(self):
        lists = []
        for i in range(self.n):
            first = i * self.width
            mine = [(0, first, min(self.width, HEADS * HEAD - first))] if first < HEADS * HEAD else []
            for kind in range(2):
                start = HEADS * HEAD + kind * KVH * HEAD
                for g in self.kv_used(i):
                    slot = g - self.first_kv[i]
                    mine.append((self.width + kind * self.kv_width + slot * HEAD, start + g * HEAD, HEAD))
            lists.append(tuple(mine))
        return tuple(lists)

    def join_columns(self, g):
        q = [g[i, :, : self.width] for i in range(self.n)]
        q = jnp.concatenate(q, axis=1)[:, : HEADS * HEAD].astype(F32)
        kv = []
        for kind in range(2):
            for head in range(KVH):
                total = 0.0
                for i in range(self.n):
                    if head in self.kv_used(i):
                        at = self.width + kind * self.kv_width + (head - self.first_kv[i]) * HEAD
                        total = total + g[i, :, at : at + HEAD].astype(F32)
                kv.append(total)
        return jnp.concatenate([q] + kv, axis=1)


def reblock(rows, have, want, total):
    n, me = lax.axis_size("seq"), lax.axis_index("seq")
    result = jnp.zeros((want,) + rows.shape[1:], rows.dtype)
    pad = jnp.pad(rows, ((want, want), (0, 0)))
    for shift in range(-(n - 1), n):
        pairs = []
        for i in range(n):
            j = i + shift
            if 0 <= j < n:
                low = max(i * have, j * want)
                high = min((i + 1) * have, (j + 1) * want, total)
                if low < high:
                    pairs.append((i, j))
        if not pairs:
            continue
        start = want + (me + shift) * want - me * have
        piece = lax.dynamic_slice_in_dim(pad, jnp.clip(start, 0, have + want), want, 0)
        if shift:
            piece = lax.ppermute(piece, "seq", pairs)
        else:
            ok = jnp.array([(i, i) in pairs for i in range(n)])[me]
            piece = jnp.where(ok, piece, jnp.zeros_like(piece))
        result = result + piece
    return result


def per_device(tokens, lengths, cotangent, w_qkv, w_ao, w_in, w_xp, w_dt, w_so, w_gu, w_down,
               norm_in, norm_attn, norm_ssm, norm_ffn, conv_w, conv_b, dt_bias, a_log, d_skip):
    seqs, slot_len, width = tokens.shape
    n, me, replicas = lax.axis_size("seq"), lax.axis_index("seq"), lax.axis_size("dp")
    local, rows = seqs * slot_len, seqs * slot_len * n
    cols = INNER // n
    plan = HeadPlan(n)
    w_rows, ao_rows = w_qkv.shape[0], w_ao.shape[0]
    pos = me * slot_len + jnp.arange(slot_len, dtype=jnp.int32)
    is_valid = pos[None, :] < lengths[:, None]
    table = plan.head_table()[me]
    tie = lax.optimization_barrier
    flat = lambda v: v.reshape(rows, v.shape[-1])
    gather = lambda v, cid: flat(all_gather(v, n, cid))
    scatter = lambda v, cid, after=None: reduce_scatter(
        v.astype(BF).reshape(n, local, v.shape[-1]), n, cid, after
    )
    later = lambda g, zero: g + zero.astype(g.dtype)
    nothing = lambda *sums: 0.0 * sum(g.reshape(-1)[0].astype(F32) for g in sums)
    mark = lambda zero: jnp.full((8, 128), zero)
    exchange = lambda v: lax.all_to_all(v, "seq", 0, 0, tiled=True)
    blocks = lambda v: v.reshape(n, seqs, slot_len, v.shape[-1])
    mine = lambda v: lax.dynamic_slice_in_dim(v, me * cols, cols, v.ndim - 1)
    over = lambda g: lax.psum(g, "dp")

    def one_step(work):
        shapes = jax.eval_shape(work, 0)
        none = lambda _: jax.tree.map(lambda t: jnp.zeros(t.shape, t.dtype), shapes)
        return lax.cond(lengths[0] > 0, work, none, 0)

    def row_sums(a, b, cid):
        both = jnp.stack([a, b]).reshape(-1, 128)
        return small_sum(both, n, cid).reshape(2, rows)

    wdt = mine(w_dt)
    taps, bias, dtb, skip = mine(conv_w), mine(conv_b), mine(dt_bias), mine(d_skip)
    rate = -jnp.exp(mine(a_log))
    ssm_gain = mine(norm_ssm)
    attn_gain = lax.dynamic_slice_in_dim(
        jnp.pad(norm_attn, (0, n * plan.width - HEADS * HEAD)), me * plan.width, plan.width, 0
    )

    x = tokens.astype(F32).reshape(local, width)
    scale_in = lax.rsqrt(jnp.mean(x * x, axis=-1, keepdims=True) + EPSILON)
    normed, qkv_cols, in_x, in_z = gather_and_exchange(
        tokens.reshape(local, width), norm_in, w_qkv, plan.moves(), plan.width + 2 * plan.kv_width, w_in, n, 1
    )
    normed, qkv_cols = flat(normed), qkv_cols.reshape(n * w_rows, -1)
    wx, wz = exchange(in_x), exchange(in_z)
    heads = attn_forward(0, table, lengths, blocks(normed), qkv_cols, plan.width)
    behind = nothing(heads[1])
    for seq in range(1, seqs):
        heads = attn_forward(seq, table, lengths, blocks(normed), qkv_cols, plan.width, heads)
    attended, lse, q, k, v = heads
    ao_all = lax.all_gather(later(w_ao, behind), "seq", axis=0, tiled=True)
    ao_mine = lax.dynamic_slice_in_dim(
        jnp.pad(ao_all, ((0, n * plan.width - HEADS * HEAD), (0, 0))), me * plan.width, plan.width, 0
    )
    upstream = (cotangent.astype(F32) * is_valid[..., None]).reshape(local, width)
    upstream_all = lax.all_gather(later(upstream.astype(BF), behind), "seq", axis=0, tiled=True)
    wx = later(wx, nothing(lse)).reshape(n * w_rows, cols)
    wz = wz.reshape(n * w_rows, cols)
    xp = jnp.swapaxes(w_xp, 0, 1)
    xp = jnp.concatenate([xp[DTR:], xp[:DTR]], axis=0)
    x_conv, conv_pre, mixer_in, mixer_low, projected = signal_forward(blocks(normed), wx, taps, bias[None], xp)
    mixer_low = flat(mixer_low)
    projected = blocks(gather(scatter(flat(projected), 15).astype(BF), 16))
    core, z_gate, ssm_sq, start = scan_forward(
        projected, mixer_in, blocks(normed), wz, wdt, dtb[None], rate, skip[None]
    )
    by_device = lambda m: m.reshape(n, local, m.shape[-1])
    squares = row_sums(jnp.sum(attended * attended, axis=3).reshape(rows), ssm_sq.reshape(rows), 2)
    r_attn = lax.rsqrt(squares[0] / (HEADS * HEAD) + EPSILON)
    r_ssm = lax.rsqrt(squares[1] / INNER + EPSILON)
    attn_low, ssm_low = map(flat, norm_both(
        by_device(squares.T), by_device(attended), attn_gain[None], by_device(core), by_device(z_gate), ssm_gain[None]
    ))
    mixed = product_scatter(((attn_low, ao_mine, False), (ssm_low, w_so, False)), n, 3)
    residual = x + 0.5 * mixed
    r_ffn = lax.rsqrt(jnp.mean(residual * residual, axis=-1, keepdims=True) + EPSILON)
    turned = jnp.transpose(w_gu, (1, 2, 0))
    w_gate, w_up = turned[0], turned[1]
    hidden = w_gate.shape[0]

    def gated_units(rows_in, gate_ref, up_ref):
        gate, up = ntdot(rows_in, gate_ref[...]), ntdot(rows_in, up_ref[...])
        return gate, up, jax.nn.silu(gate) * up

    normed_two, gate, up, activated = gather_product(
        gated_units, (residual * r_ffn * norm_ffn).astype(BF), (w_gate, w_up), ((hidden, BF),) * 3, n, 4
    )
    normed_two, activated = flat(normed_two), flat(activated)

    grad_gate, grad_up = map(flat, ffn_backward(by_device(upstream_all), w_down, gate, up))
    g_down = tndot(activated, upstream_all).astype(BF)
    g_gate, g_up = tndot(grad_gate, normed_two).astype(BF), tndot(grad_up, normed_two).astype(BF)
    g_down, g_gate, g_up = tie((g_down, g_gate, g_up))
    s_down, s_gate, s_up = over((g_down, g_gate, g_up))
    grad_two = product_scatter(
        ((grad_gate, w_gate, False), (grad_up, w_up, False)), n, 5, mark(nothing(g_gate, g_up))
    )

    def norm_pull(grad, values, r, gain):
        dotted = jnp.mean(grad * gain * values, axis=-1, keepdims=True)
        return r * (grad * gain - values * (r * r * dotted)), jnp.sum(grad * values * r, axis=0)

    add, g_norm_ffn = norm_pull(grad_two, residual, r_ffn, norm_ffn)
    grad_residual = upstream + add

    def heads_and_channels(rows_in, ao_ref, so_ref, head_gain, channel_gain, heads_out, core_out, gate_out):
        of_heads = 0.5 * ntdot(rows_in, ao_ref[...])
        of_channels = 0.5 * ntdot(rows_in, so_ref[...])
        gated = core_out * (gate_out * jax.nn.sigmoid(gate_out))
        sums = [
            jnp.sum(of_heads * head_gain[...] * heads_out, axis=1, keepdims=True),
            jnp.sum(of_channels * channel_gain[...] * gated, axis=1, keepdims=True),
        ]
        return of_heads, of_channels, jnp.concatenate(sums, axis=1)

    mix_low, d_attn, d_ssm, inner = gather_product(
        heads_and_channels, grad_residual.astype(BF), (ao_mine, w_so, attn_gain[None], ssm_gain[None]),
        ((plan.width, F32), (cols, F32), (2, F32)), n, 7, (by_device(attended), by_device(core), by_device(z_gate)),
    )
    mix_low, inner = flat(mix_low), inner.reshape(rows, 2)
    inner = row_sums(inner[:, 0], inner[:, 1], 8)
    stats = blocks(jnp.stack([
        r_attn, inner[0] / (HEADS * HEAD) * r_attn * r_attn, r_ssm, inner[1] / INNER * r_ssm * r_ssm
    ], axis=1))

    def mixers_back(_):
        gq, gk, gv, head_sums = attn_backward(
            table, lengths, q, k, v, blocks(d_attn), attended, lse, stats, attn_gain[None]
        )
        gpre, gmix, gz, gb, gc, grate, channel_sums = scan_backward(
            lengths, projected, mixer_in, blocks(d_ssm), core, z_gate, stats, start, wdt, dtb[None], rate, skip[None],
            ssm_gain[None],
        )
        grad_qkv, grad_z = flat(jnp.concatenate([gq, gk, gv], axis=3)), flat(gz)
        of_weights = (
            (0.5 * tndot(attn_low, mix_low)).astype(BF),
            (0.5 * tndot(ssm_low, mix_low)).astype(BF),
            tndot(normed, grad_z).astype(BF),
            tndot(normed, grad_qkv).astype(BF),
        )
        return head_sums[0], channel_sums, grad_qkv, grad_z, flat(gpre), gmix, flat(gb), flat(gc), grate, of_weights

    g_norm_attn, channel_sums, grad_qkv, grad_z, grad_step, gmix, gb, gc, grate, of_weights = one_step(mixers_back)
    g_norm_ssm, gskip, g_dt_bias = channel_sums[0], channel_sums[1:2], channel_sums[2]
    g_ao, g_so, g_z, g_qkv = of_weights
    g_ao = reblock(g_ao, plan.width, ao_rows, HEADS * HEAD)
    g_z = exchange(g_z.reshape(n, w_rows, cols))
    g_z = jnp.swapaxes(g_z, 0, 1).reshape(w_rows, INNER)
    g_qkv = exchange(g_qkv.reshape(n, w_rows, -1))
    g_qkv = plan.join_columns(g_qkv).astype(BF)
    first_sums = nothing(s_down, s_gate, s_up)
    grad_projected = jnp.concatenate([gb, gc, ntdot(grad_step, wdt)], axis=1)
    grad_projected = gather(scatter(grad_projected, 9, mark(first_sums)).astype(BF), 10)
    after_one = first_sums + nothing(grad_projected)
    s_ao, s_so, s_qkv, s_z = over(tuple(later(g, after_one) for g in (g_ao, g_so, g_qkv, g_z)))

    def signal_back(_):
        grad_x, sums = signal_backward(gmix, blocks(grad_projected), xp, conv_pre, x_conv, taps)
        grad_x = flat(grad_x)
        return (
            grad_x,
            sums,
            tndot(normed, grad_x).astype(BF),
            tndot(grad_projected, mixer_low).astype(BF),
            tndot(grad_step, flat(projected)[:, 2 * NST :]).astype(BF),
        )

    grad_x, tap_sums, g_x, g_xp, g_wdt = one_step(signal_back)
    g_conv_w, g_conv_b = tap_sums[:KCONV], tap_sums[KCONV]
    g_x = exchange(g_x.reshape(n, w_rows, cols))
    g_x = jnp.swapaxes(g_x, 0, 1).reshape(w_rows, INNER)
    grad_normed = product_scatter(
        ((grad_x, wx, True), (grad_z, wz, True), (grad_qkv, qkv_cols, True)), n, 11
    )
    block_out = residual + product_scatter(
        ((activated, w_down, False),), n, 6, mark(nothing(grad_normed))
    )
    add_in, g_norm_in = norm_pull(grad_normed, x, scale_in, norm_in)
    grad_tokens = grad_residual + add_in

    s_gu = jnp.transpose(jnp.stack([s_gate, s_up]), (2, 0, 1))
    s_x, s_xp, s_wdt = chain_sum((g_x, g_xp, g_wdt), (5, 1, 1), replicas, 14, mark(nothing(block_out, s_ao, s_so, s_qkv, s_z)))
    s_in = jnp.concatenate([s_x, s_z.astype(F32)], axis=1)
    s_xp = jnp.swapaxes(jnp.concatenate([s_xp[2 * NST :], s_xp[: 2 * NST]], axis=0), 0, 1)
    s_wdt = jnp.swapaxes(s_wdt, 0, 1)

    place = lambda g: lax.dynamic_update_slice_in_dim(
        jnp.zeros((n * plan.width,), F32), g, me * plan.width, 0
    )[: HEADS * HEAD]

    def pad_rows(v):
        v = v.reshape(-1)
        return jnp.pad(v, (0, -v.size % 1024)).reshape(-1, 128)

    shared = jnp.stack([g_norm_in, place(g_norm_attn), g_norm_ffn])
    total = small_sum(pad_rows(shared), n, 12).reshape(-1)[: shared.size].reshape(shared.shape)
    shared = lax.dynamic_slice_in_dim(total, me * w_rows, w_rows, 1)
    owned = jnp.concatenate(
        [g_norm_ssm[None], g_conv_w, g_conv_b[None], g_dt_bias[None], grate * rate, gskip], axis=0
    )
    small = pad_rows(jnp.concatenate([shared.reshape(-1), owned.reshape(-1)]))
    small = small_sum(small, replicas, 13, "dp").reshape(-1)
    s_shared = small[: shared.size].reshape(shared.shape)
    s_owned = small[shared.size : shared.size + owned.size].reshape(owned.shape)
    full = lambda g: g.astype(F32)

    return (
        block_out.astype(BF).reshape(seqs, slot_len, width),
        grad_tokens.reshape(seqs, slot_len, width),
        full(s_qkv),
        full(s_ao),
        full(s_in),
        full(s_xp),
        full(s_wdt),
        full(s_so),
        full(s_gu),
        full(s_down),
        s_shared[0],
        s_shared[1],
        s_owned[0],
        s_shared[2],
        s_owned[1 : 1 + KCONV],
        s_owned[1 + KCONV],
        s_owned[2 + KCONV],
        s_owned[3 + KCONV : 3 + KCONV + NST],
        s_owned[3 + KCONV + NST],
    )


def solution(mesh):
    rows, cols, flat = P("seq", None), P(None, "seq"), P("seq")
    act = P("dp", "seq", None)
    hid = P(None, None, "seq")
    in_specs = (act, P("dp"), act, rows, rows, rows, rows, P(), rows, hid, rows) + (P(),) * 9
    out_specs = (act, act, rows, rows, rows, rows, cols, rows, hid, rows,
                 flat, flat, flat, flat, cols, flat, flat, cols, flat)
    return jax.shard_map(per_device, mesh=mesh, in_specs=in_specs, out_specs=out_specs, check_vma=False)
```

```python
import functools
import math

import jax
import jax.numpy as jnp
from jax import lax
from jax.experimental import pallas as pl
from jax.experimental.pallas import tpu as pltpu
from jax.sharding import PartitionSpec as P

HEADS = 25
HEAD = 64
KVH = 5
INNER = 3200
NST = 16
KCONV = 4
DTR = 100
EPSILON = 1e-05
NEGATIVE = -1e30
CHUNK = 16
LOG2E = math.log2(math.e)
LN2 = math.log(2.0)

BF = jnp.bfloat16
F32 = jnp.float32
NT = (((1,), (1,)), ((), ()))
TN = (((0,), (0,)), ((), ()))
GIANT = 60 * 1024 * 1024
MESH = pl.DeviceIdType.MESH


def ntdot(a, b):
    return lax.dot_general(a, b, NT, preferred_element_type=F32)


def tndot(a, b):
    return lax.dot_general(a, b, TN, preferred_element_type=F32)


def dot(a, b):
    return jnp.dot(a, b, preferred_element_type=F32)


def silu_grad(values):
    logistic = jax.nn.sigmoid(values)
    return logistic * (1.0 + values * (1.0 - logistic))


def chunk_masks():
    spread = NST * CHUNK
    row = lax.broadcasted_iota(jnp.int32, (CHUNK, spread), 0)
    col = lax.broadcasted_iota(jnp.int32, (CHUNK, spread), 1)
    own = (col // NST == row).astype(F32)
    tile = (col % NST == row).astype(BF)
    return own, tile


def turn_chunks(proj, bt_ref, ct_ref):
    turned = jnp.swapaxes(proj[:, : 8 * NST], 0, 1)
    for k in range(proj.shape[0] // CHUNK):
        at = slice(k * CHUNK, (k + 1) * CHUNK)
        bt_ref[k] = turned[:NST, at]
        if ct_ref is not None:
            ct_ref[k] = turned[NST : 2 * NST, at]


def scan_fwd_kernel(proj_ref, mix_ref, rows_ref, wz_ref, wdt_ref, dtb_ref, rate_ref, skip_ref,
                    core_ref, z_ref, sq_ref, start_ref, h_ref, dt_ref, u_ref, wide_ref, hs_ref, bt_ref):
    length, cols = mix_ref.shape[2:]
    own, tile = chunk_masks()

    @pl.when(pl.program_id(1) == 0)
    def _():
        for ref in (h_ref, dt_ref, u_ref, wide_ref):
            ref[...] = jnp.zeros_like(ref)
        wide_ref[:, :cols] = rate_ref[...] * LOG2E

    start_ref[0, 0] = h_ref[:, :cols]
    proj = proj_ref[0, 0].astype(F32)
    turn_chunks(proj, bt_ref, None)
    pre = dot(proj[:, 2 * NST :].astype(BF), wdt_ref[...]) + dtb_ref[...]
    dt = jax.nn.softplus(pre)
    dt_ref[:, :cols] = dt
    u_ref[:, :cols] = dt * mix_ref[0, 0]
    rate = wide_ref[...]
    spread = NST * CHUNK

    def chunk(k, h):
        base = pl.multiple_of(k * CHUNK, CHUNK)
        bt = bt_ref[k]
        for t in range(CHUNK):
            a = jnp.exp2(dt_ref[pl.ds(base + t, 1), :] * rate)
            h = a * h + bt[:, t : t + 1] * u_ref[pl.ds(base + t, 1), :]
            hs_ref[pl.ds(pl.multiple_of((base + t) * NST, NST), NST), :] = h.astype(BF)
        return h

    h_ref[...] = lax.fori_loop(0, length // CHUNK, chunk, h_ref[...])
    z = dot(rows_ref[0, 0], wz_ref[...])
    z_ref[0, 0] = z
    crep = dot(proj[:, NST : 2 * NST].astype(BF), tile)
    for k in range(length // CHUNK):
        at = slice(k * CHUNK, (k + 1) * CHUNK)
        cb = (crep[at] * own).astype(BF)
        core_ref[0, 0, at, :] = (
            dot(cb, hs_ref[k * spread : (k + 1) * spread])[:, :cols] + skip_ref[...] * mix_ref[0, 0, at, :]
        )
    gated = core_ref[0, 0] * (z * jax.nn.sigmoid(z))
    sq_ref[0, 0] = jnp.sum(gated * gated, axis=1, keepdims=True)


def scan_forward(proj, mix, rows, wz, wdt, dtb, rate, skip):
    n, seqs, length, cols = mix.shape
    wide = -(-cols // 128) * 128
    big = lambda w: pl.BlockSpec((1, 1, length, w), lambda s, i: (i, s, 0, 0))
    whole = lambda a: pl.BlockSpec(a.shape, lambda s, i: (0, 0))
    shape = lambda w: jax.ShapeDtypeStruct((n, seqs, length, w), F32)
    return pl.pallas_call(
        scan_fwd_kernel,
        grid=(seqs, n),
        in_specs=[big(proj.shape[3]), big(cols), big(rows.shape[3])] + [whole(a) for a in (wz, wdt, dtb, rate, skip)],
        out_specs=[big(cols), big(cols), big(1), pl.BlockSpec((1, 1, NST, cols), lambda s, i: (i, s, 0, 0))],
        out_shape=[shape(cols), shape(cols), shape(1), jax.ShapeDtypeStruct((n, seqs, NST, cols), F32)],
        scratch_shapes=[
            pltpu.VMEM((NST, wide), F32),
            pltpu.VMEM((length, wide), F32),
            pltpu.VMEM((length, wide), F32),
            pltpu.VMEM((NST, wide), F32),
            pltpu.VMEM((NST * length, wide), BF),
            pltpu.VMEM((length // CHUNK, NST, CHUNK), F32),
        ],
        compiler_params=pltpu.CompilerParams(vmem_limit_bytes=GIANT),
    )(proj, mix, rows, wz, wdt, dtb, rate, skip)


def scan_bwd_kernel(len_ref, proj_ref, mix_ref, d_ref, core_ref, z_ref, stat_ref, start_ref, wdt_ref, dtb_ref, rate_ref, skip_ref,
                    gain_ref, gpre_ref, gmix_ref, gz_ref, gb_ref, gc_ref, grate_ref, sums_ref,
                    carry_ref, dt_ref, u_ref, gy_ref, wide_ref, hs_ref, gs_ref, q_ref, bt_ref, ct_ref):
    length, cols = mix_ref.shape[2:]
    own, tile = chunk_masks()
    spread = NST * CHUNK
    half = NST // 2
    folded = (lax.broadcasted_iota(jnp.int32, (2 * CHUNK, spread), 1) // half
              == lax.broadcasted_iota(jnp.int32, (2 * CHUNK, spread), 0)).astype(BF)

    @pl.when(pl.program_id(1) == 0)
    def _():
        carry_ref[...] = jnp.zeros_like(carry_ref)

    @pl.when((pl.program_id(1) == 0) & (pl.program_id(0) == 0))
    def _():
        grate_ref[...] = jnp.zeros_like(grate_ref)
        sums_ref[...] = jnp.zeros_like(sums_ref)
        for ref in (dt_ref, u_ref, gy_ref, wide_ref):
            ref[...] = jnp.zeros_like(ref)
        wide_ref[0:NST, :cols] = rate_ref[...] * LOG2E

    filled = (pl.num_programs(1) - 1 - pl.program_id(1)) * length < len_ref[pl.program_id(0)]

    @pl.when(jnp.logical_not(filled))
    def _():
        for ref in (gpre_ref, gmix_ref, gz_ref, gb_ref, gc_ref):
            ref[...] = jnp.zeros_like(ref)

    @pl.when(filled)
    def _():
        scale, shift = stat_ref[0, 0][:, 2:3], stat_ref[0, 0][:, 3:4]
        d, core, z = d_ref[0, 0], core_ref[0, 0], z_ref[0, 0]
        logistic = jax.nn.sigmoid(z)
        gated = core * (z * logistic)
        grad_gated = scale * (d * gain_ref[...] - gated * shift)
        gy_ref[:, :cols] = grad_gated * (z * logistic)
        gz_ref[0, 0] = (grad_gated * core * (logistic * (1.0 + z * (1.0 - logistic)))).astype(BF)
        sums_ref[0:1] += jnp.sum(d * gated * scale, axis=0, keepdims=True)
        sums_ref[1:2] += jnp.sum(gy_ref[:, :cols] * mix_ref[0, 0], axis=0, keepdims=True)
        proj = proj_ref[0, 0].astype(F32)
        turn_chunks(proj, bt_ref, ct_ref)
        pre = dot(proj[:, 2 * NST :].astype(BF), wdt_ref[...]) + dtb_ref[...]
        dt = jax.nn.softplus(pre)
        dt_ref[:, :cols] = dt
        u_ref[:, :cols] = dt * mix_ref[0, 0]
        wide_ref[NST:, :cols] = start_ref[0, 0]
        rate = wide_ref[0:NST]
        hs_ref[0:NST] = wide_ref[NST:].astype(BF)

        def ahead(k, h):
            base = pl.multiple_of(k * CHUNK, CHUNK)
            bt = bt_ref[k]
            for t in range(CHUNK):
                a = jnp.exp2(dt_ref[pl.ds(base + t, 1), :] * rate)
                h = a * h + bt[:, t : t + 1] * u_ref[pl.ds(base + t, 1), :]
                hs_ref[pl.ds(pl.multiple_of((base + t + 1) * NST, NST), NST), :] = h.astype(BF)
            return h

        lax.fori_loop(0, length // CHUNK, ahead, wide_ref[NST:])

        def back(r, state):
            carry, grate = state
            k = length // CHUNK - 1 - r
            base = pl.multiple_of(k * CHUNK, CHUNK)
            ct = ct_ref[k]
            qr_late = None
            for t in reversed(range(CHUNK)):
                at = pl.ds(pl.multiple_of((base + t) * NST, NST), NST)
                dt_row = dt_ref[pl.ds(base + t, 1), :]
                a = jnp.exp2(dt_row * rate)
                g = ct[:, t : t + 1] * gy_ref[pl.ds(base + t, 1), :] + carry
                carry = a * g
                q = carry * hs_ref[at, :].astype(F32)
                grate = grate + q * dt_row
                gs_ref[at, :] = g.astype(BF)
                qr = q * rate
                qr = qr[:half] + qr[half:]
                if t % 2:
                    qr_late = qr
                else:
                    both = jnp.concatenate([qr, qr_late], axis=0).astype(BF)
                    q_ref[pl.ds(pl.multiple_of((base + t) * half, NST), NST), :] = both
            return carry, grate

        carry, grate = lax.fori_loop(
            0, length // CHUNK, back, (carry_ref[...], jnp.zeros(carry_ref.shape, F32))
        )
        carry_ref[...] = carry
        grate_ref[...] += grate[:, :cols]
        brep = dot(proj[:, :NST].astype(BF), tile)
        gy_low = gy_ref[...].astype(BF)
        u_low = u_ref[...].astype(BF)
        gcs, gbs = [], []
        for pair in range(length // CHUNK // 2):
            gdts = dot(folded, q_ref[pair * spread : (pair + 1) * spread]) * LN2
            for k in (2 * pair, 2 * pair + 1):
                rows = slice(k * CHUNK, (k + 1) * CHUNK)
                deep = slice(k * spread, (k + 1) * spread)
                mix, dt_now, gy = mix_ref[0, 0, rows, :], dt_ref[rows, :cols], gy_ref[rows, :cols]
                gs = gs_ref[deep]
                gu = dot((brep[rows] * own).astype(BF), gs)[:, :cols]
                gdt = gdts[(k % 2) * CHUNK : (k % 2 + 1) * CHUNK, :cols] + gu * mix
                gpre = gdt * jax.nn.sigmoid(pre[rows])
                gpre_ref[0, 0, rows, :] = gpre.astype(BF)
                sums_ref[2:3] += jnp.sum(gpre, axis=0, keepdims=True)
                gmix_ref[0, 0, rows, :] = gu * dt_now + skip_ref[...] * gy
                hs = hs_ref[k * spread + NST : (k + 1) * spread + NST]
                gcs.append((ntdot(gy_low[rows], hs) * own).astype(BF))
                gbs.append((ntdot(u_low[rows], gs) * own).astype(BF))
        gc_ref[0, 0] = ntdot(jnp.concatenate(gcs, axis=0), tile)
        gb_ref[0, 0] = ntdot(jnp.concatenate(gbs, axis=0), tile)


def scan_backward(lengths, proj, mix, d, core, z, stats, start, wdt, dtb, rate, skip, gain):
    n, seqs, length, cols = mix.shape
    wide = -(-cols // 128) * 128
    at = lambda s, i: (n - 1 - i, s, 0, 0)
    big = lambda w: pl.BlockSpec((1, 1, length, w), at)
    whole = lambda a: pl.BlockSpec(a.shape, lambda s, i: (0, 0))
    shape = lambda w, t: jax.ShapeDtypeStruct((n, seqs, length, w), t)
    return pl.pallas_call(
        scan_bwd_kernel,
        grid=(seqs, n),
        in_specs=[pl.BlockSpec(memory_space=pltpu.SMEM),
                  big(proj.shape[3]), big(cols), big(cols), big(cols), big(cols), big(stats.shape[3]),
                  pl.BlockSpec((1, 1, NST, cols), at)] + [whole(a) for a in (wdt, dtb, rate, skip, gain)],
        out_specs=[big(cols), big(cols), big(cols), big(NST), big(NST), whole(rate),
                   pl.BlockSpec((8, cols), lambda s, i: (0, 0))],
        out_shape=[
            shape(cols, BF), shape(cols, F32), shape(cols, BF), shape(NST, F32), shape(NST, F32),
            jax.ShapeDtypeStruct((NST, cols), F32),
            jax.ShapeDtypeStruct((8, cols), F32),
        ],
        scratch_shapes=[
            pltpu.VMEM((NST, wide), F32),
            pltpu.VMEM((length, wide), F32),
            pltpu.VMEM((length, wide), F32),
            pltpu.VMEM((length, wide), F32),
            pltpu.VMEM((2 * NST, wide), F32),
            pltpu.VMEM((length * NST + NST, wide), BF),
            pltpu.VMEM((length * NST, wide), BF),
            pltpu.VMEM((length * NST // 2, wide), BF),
            pltpu.VMEM((length // CHUNK, NST, CHUNK), F32),
            pltpu.VMEM((length // CHUNK, NST, CHUNK), F32),
        ],
        compiler_params=pltpu.CompilerParams(vmem_limit_bytes=GIANT),
    )(lengths, proj, mix, d, core, z, stats, start, wdt, dtb, rate, skip, gain)


def pick(ref, blocks, slots, slot):
    value = ref[0:blocks, 0, :, 0:HEAD].reshape(-1, HEAD)
    for other in range(1, slots):
        here = ref[0:blocks, 0, :, other * HEAD : (other + 1) * HEAD].reshape(-1, HEAD)
        value = jnp.where(slot == other, here, value)
    return value


def masked_scores(queries, keys, first, length):
    scores = ntdot(queries, keys)
    rows = first + lax.broadcasted_iota(jnp.int32, (scores.shape[0], 1), 0)
    bound = jnp.minimum(rows, length - 1)
    return jnp.where(lax.broadcasted_iota(jnp.int32, scores.shape, 1) <= bound, scores, NEGATIVE)


def attn_fwd_kernel(seq, slot_ref, len_ref, rows_ref, w_ref, *refs):
    out_ref, lse_ref, q_ref, k_ref, v_ref = refs[-5:]
    n, _, length, width = q_ref.shape
    heads, slots = width // HEAD, k_ref.shape[3] // HEAD
    group = 2
    seq_length = len_ref[seq]
    kv_width = k_ref.shape[3]

    def project(i, _):
        y = dot(rows_ref[i, 0], w_ref[...]).astype(BF)
        q_ref[i, 0] = y[:, :width]
        k_ref[i, 0] = y[:, width : width + kv_width]
        v_ref[i, 0] = y[:, width + kv_width :]
        return 0

    lax.fori_loop(0, n, project, 0)
    for i in range(n // group):
        at = slice(i * group, (i + 1) * group)
        for j in range(heads):
            lanes = slice(j * HEAD, (j + 1) * HEAD)
            blocks = (i + 1) * group
            queries = q_ref[at, 0, :, lanes].reshape(group * length, HEAD) * HEAD ** (-0.5)
            keys = pick(k_ref, blocks, slots, slot_ref[j])
            values = pick(v_ref, blocks, slots, slot_ref[j])
            scores = masked_scores(queries.astype(BF), keys, i * group * length, seq_length)
            top = jnp.max(scores, axis=1, keepdims=True)
            probs = jnp.exp(scores - top)
            total = jnp.sum(probs, axis=1, keepdims=True)
            mixed = dot(probs.astype(BF), values) * (slot_ref[heads + j].astype(F32) / total)
            out_ref[at, 0, :, lanes] = mixed.reshape(group, length, HEAD)
            lse_ref[at, 0, :, j : j + 1] = (top + jnp.log(total)).reshape(group, length, 1)


def attn_forward(seq, slot, lengths, rows, w, width, before=()):
    n, seqs, length, depth = rows.shape
    kv_width = (w.shape[1] - width) // 2
    big = lambda w: pl.BlockSpec((n, 1, length, w), lambda s: (0, seq, 0, 0))
    smem = pl.BlockSpec(memory_space=pltpu.SMEM)
    outs = ((width, F32), (width // HEAD, F32), (width, BF), (kv_width, BF), (kv_width, BF))
    return pl.pallas_call(
        functools.partial(attn_fwd_kernel, seq),
        grid=(1,),
        in_specs=[smem, smem, big(depth), pl.BlockSpec(w.shape, lambda s: (0, 0))]
        + [pl.BlockSpec(memory_space=pl.ANY)] * len(before),
        out_specs=[big(c) for c, _ in outs],
        out_shape=[jax.ShapeDtypeStruct((n, seqs, length, c), t) for c, t in outs],
        input_output_aliases={4 + i: i for i in range(len(before))},
        compiler_params=pltpu.CompilerParams(vmem_limit_bytes=GIANT),
        cost_estimate=pl.CostEstimate(
            flops=2 * n * length * w.shape[1] * depth + 16 * (n * length) ** 2 * width,
            bytes_accessed=2 * n * length * (depth + 6 * width),
            transcendentals=(n * length) ** 2 * (width // HEAD),
        ),
    )(slot, lengths, rows, w, *before)


def attn_bwd_kernel(slot_ref, len_ref, q_ref, k_ref, v_ref, d_ref, att_ref, lse_ref, stat_ref, gain_ref,
                    gq_ref, gk_ref, gv_ref, sums_ref, gk_acc, gv_acc, gh_ref):
    n, _, length, width = q_ref.shape
    heads, slots = width // HEAD, k_ref.shape[3] // HEAD
    group = 2
    seq_length = len_ref[pl.program_id(0)]
    @pl.when(pl.program_id(0) == 0)
    def _():
        sums_ref[...] = jnp.zeros_like(sums_ref)

    for i in range(n):
        scale, shift = stat_ref[i, 0][:, 0:1], stat_ref[i, 0][:, 1:2]
        d, attended = d_ref[i, 0], att_ref[i, 0]
        gh_ref[i] = (scale * (d * gain_ref[...] - attended * shift)).astype(BF)
        sums_ref[0:1] += jnp.sum(d * attended * scale, axis=0, keepdims=True)
    gk_acc[...] = jnp.zeros_like(gk_acc)
    gv_acc[...] = jnp.zeros_like(gv_acc)
    def block(i):
        at = slice(i * group, (i + 1) * group)
        blocks = (i + 1) * group
        for j in range(heads):
            lanes = slice(j * HEAD, (j + 1) * HEAD)
            slot = slot_ref[j]
            queries = q_ref[at, 0, :, lanes].reshape(group * length, HEAD) * HEAD ** (-0.5)
            queries = queries.astype(BF)
            keys = pick(k_ref, blocks, slots, slot)
            values = pick(v_ref, blocks, slots, slot)
            grad = gh_ref[at, :, lanes].reshape(group * length, HEAD)
            attended = att_ref[at, 0, :, lanes].reshape(group * length, HEAD)
            delta = jnp.sum(grad.astype(F32) * attended, axis=1, keepdims=True)
            lse = lse_ref[at, 0, :, j : j + 1].reshape(group * length, 1)
            scores = masked_scores(queries, keys, i * group * length, seq_length)
            probs = jnp.exp(scores - lse)
            grad_scores = (probs * (ntdot(grad, values) - delta)).astype(BF)
            gq = dot(grad_scores, keys) * HEAD ** (-0.5)
            gq_ref[at, 0, :, lanes] = gq.astype(BF).reshape(group, length, HEAD)
            rows = slice(0, blocks * length)
            gk_acc[slot, rows] += tndot(grad_scores, queries)
            gv_acc[slot, rows] += tndot(probs.astype(BF), grad)

    for i in range(n // group):
        pl.when(i * group * length < seq_length)(functools.partial(block, i))

        @pl.when(i * group * length >= seq_length)
        def _():
            gq_ref[i * group : (i + 1) * group] = jnp.zeros((group,) + gq_ref.shape[1:], BF)

    for other in range(slots):
        lanes = slice(other * HEAD, (other + 1) * HEAD)
        gk_ref[:, 0, :, lanes] = gk_acc[other].astype(BF).reshape(n, length, HEAD)
        gv_ref[:, 0, :, lanes] = gv_acc[other].astype(BF).reshape(n, length, HEAD)


def attn_backward(slot, lengths, q, k, v, d, att, lse, stats, gain):
    n, seqs, length, width = q.shape
    big = lambda w: pl.BlockSpec((n, 1, length, w), lambda s: (0, s, 0, 0))
    whole = lambda r: pl.BlockSpec((r, width), lambda s: (0, 0))
    smem = pl.BlockSpec(memory_space=pltpu.SMEM)
    kw = k.shape[3]
    return pl.pallas_call(
        attn_bwd_kernel,
        grid=(seqs,),
        in_specs=[smem, smem, big(width), big(kw), big(kw), big(width), big(width), big(width // HEAD),
                  big(stats.shape[3]), whole(1)],
        out_specs=[big(width), big(kw), big(kw), whole(8)],
        out_shape=[jax.ShapeDtypeStruct(x.shape, BF) for x in (q, k, v)]
        + [jax.ShapeDtypeStruct((8, width), F32)],
        scratch_shapes=[pltpu.VMEM((kw // HEAD, n * length, HEAD), F32)] * 2 + [pltpu.VMEM((n, length, width), BF)],
        compiler_params=pltpu.CompilerParams(vmem_limit_bytes=GIANT),
    )(slot, lengths, q, k, v, d, att, lse, stats, gain)


def signal_fwd_kernel(rows_ref, wx_ref, taps_ref, bias_ref, xp_ref, x_ref, pre_ref, mix_ref, low_ref, part_ref, xs_ref):
    length = rows_ref.shape[2]

    @pl.when(pl.program_id(1) == 0)
    def _():
        xs_ref[0:8] = jnp.zeros((8, xs_ref.shape[1]), F32)

    x = dot(rows_ref[0, 0], wx_ref[...]).astype(BF)
    x_ref[0, 0] = x
    xs_ref[8:] = x.astype(F32)
    first = 8 - (KCONV - 1)
    pre = bias_ref[...]
    for o in range(KCONV):
        pre = pre + taps_ref[o : o + 1] * xs_ref[first + o : first + o + length]
    xs_ref[0:8] = xs_ref[length : length + 8]
    pre_ref[0, 0] = pre
    mix = pre * jax.nn.sigmoid(pre)
    mix_ref[0, 0] = mix
    low_ref[0, 0] = mix.astype(BF)
    part_ref[0, 0] = ntdot(mix.astype(BF), xp_ref[...]).astype(BF)


def signal_forward(rows, wx, taps, bias, xp):
    n, seqs, length, width = rows.shape
    cols = wx.shape[1]
    big = lambda w: pl.BlockSpec((1, 1, length, w), lambda s, i: (i, s, 0, 0))
    whole = lambda a: pl.BlockSpec(a.shape, lambda s, i: (0, 0))
    shape = lambda w, t: jax.ShapeDtypeStruct((n, seqs, length, w), t)
    return pl.pallas_call(
        signal_fwd_kernel,
        grid=(seqs, n),
        in_specs=[big(width), whole(wx), whole(taps), whole(bias), whole(xp)],
        out_specs=[big(cols)] * 4 + [big(xp.shape[0])],
        out_shape=[shape(cols, BF), shape(cols, F32), shape(cols, F32), shape(cols, BF), shape(xp.shape[0], BF)],
        scratch_shapes=[pltpu.VMEM((length + 8, cols), F32)],
        compiler_params=pltpu.CompilerParams(vmem_limit_bytes=GIANT),
    )(rows, wx, taps, bias, xp)


def signal_bwd_kernel(gmix_ref, gproj_ref, xp_ref, pre_ref, x_ref, last_ref, taps_ref, gx_ref, sums_ref, gs_ref, xs_ref):
    length = gmix_ref.shape[2]
    edge = KCONV - 1
    i = pl.program_id(1)

    @pl.when((i == 0) & (pl.program_id(0) == 0))
    def _():
        sums_ref[...] = jnp.zeros_like(sums_ref)

    @pl.when(i == 0)
    def _():
        gs_ref[length:] = jnp.zeros((8, gs_ref.shape[1]), F32)

    grad = gmix_ref[0, 0] + dot(gproj_ref[0, 0], xp_ref[...])
    grad = grad * silu_grad(pre_ref[0, 0])
    gs_ref[:length] = grad
    first_block = (i == pl.num_programs(1) - 1).astype(F32)
    xs_ref[0:16] = last_ref[0, 0].astype(F32) * (1.0 - first_block)
    xs_ref[16:] = x_ref[0, 0].astype(F32)
    total = None
    for o in range(KCONV):
        term = taps_ref[o : o + 1] * gs_ref[edge - o : edge - o + length]
        total = term if total is None else total + term
        at = 16 - edge + o
        sums_ref[o : o + 1] += jnp.sum(grad * xs_ref[at : at + length], axis=0, keepdims=True)
    sums_ref[KCONV : KCONV + 1] += jnp.sum(grad, axis=0, keepdims=True)
    gx_ref[0, 0] = total.astype(BF)
    gs_ref[length:] = gs_ref[0:8]


def signal_backward(gmix, gproj, xp, pre, x, taps):
    n, seqs, length, cols = gmix.shape
    at = lambda s, i: (n - 1 - i, s, 0, 0)
    big = lambda w: pl.BlockSpec((1, 1, length, w), at)
    whole = lambda a: pl.BlockSpec(a.shape, lambda s, i: (0, 0))
    before = lambda s, i: (jnp.maximum(n - 2 - i, 0), s, length // 16 - 1, 0)
    return pl.pallas_call(
        signal_bwd_kernel,
        grid=(seqs, n),
        in_specs=[big(cols), big(xp.shape[0]), whole(xp), big(cols), big(cols),
                  pl.BlockSpec((1, 1, 16, cols), before), whole(taps)],
        out_specs=[big(cols), pl.BlockSpec((8, cols), lambda s, i: (0, 0))],
        out_shape=[jax.ShapeDtypeStruct(gmix.shape, BF), jax.ShapeDtypeStruct((8, cols), F32)],
        scratch_shapes=[pltpu.VMEM((length + 8, cols), F32), pltpu.VMEM((length + 16, cols), F32)],
        compiler_params=pltpu.CompilerParams(vmem_limit_bytes=GIANT),
    )(gmix, gproj, xp, pre, x, x, taps)


def norm_kernel(sq_ref, att_ref, again_ref, core_ref, z_ref, sgain_ref, attn_ref, ssm_ref):
    sq = sq_ref[0]
    r_attn = lax.rsqrt(sq[:, 0:1] / (HEADS * HEAD) + EPSILON)
    r_ssm = lax.rsqrt(sq[:, 1:2] / INNER + EPSILON)
    attn_ref[0] = (att_ref[0] * r_attn * again_ref[...]).astype(BF)
    z = z_ref[0]
    ssm_ref[0] = (core_ref[0] * (z * jax.nn.sigmoid(z)) * r_ssm * sgain_ref[...]).astype(BF)


def norm_both(squares, attended, attn_gain, core, z, ssm_gain):
    n, rows, _ = squares.shape
    block = lambda c: pl.BlockSpec((1, rows, c), lambda i: (i, 0, 0))
    whole = lambda a: pl.BlockSpec(a.shape, lambda i: (0, 0))
    aw, sw = attended.shape[2], core.shape[2]
    return pl.pallas_call(
        norm_kernel,
        grid=(n,),
        in_specs=[block(2), block(aw), whole(attn_gain), block(sw), block(sw), whole(ssm_gain)],
        out_specs=[block(aw), block(sw)],
        out_shape=[jax.ShapeDtypeStruct((n, rows, w), BF) for w in (aw, sw)],
        compiler_params=pltpu.CompilerParams(vmem_limit_bytes=GIANT),
    )(squares, attended, attn_gain, core, z, ssm_gain)


def ffn_bwd_kernel(u_ref, down_ref, gate_ref, up_ref, ggate_ref, gup_ref):
    grad = ntdot(u_ref[0], down_ref[...])
    gate, up = gate_ref[0].astype(F32), up_ref[0].astype(F32)
    logistic = jax.nn.sigmoid(gate)
    ggate_ref[0] = (grad * up * (logistic * (1.0 + gate * (1.0 - logistic)))).astype(BF)
    gup_ref[0] = (grad * (gate * logistic)).astype(BF)


def ffn_backward(upstream, w_down, gate, up):
    n, rows, hidden = gate.shape
    block = lambda c: pl.BlockSpec((1, rows, c), lambda i: (i, 0, 0))
    return pl.pallas_call(
        ffn_bwd_kernel,
        grid=(n,),
        in_specs=[block(upstream.shape[2]), pl.BlockSpec(w_down.shape, lambda i: (0, 0)), block(hidden), block(hidden)],
        out_specs=[block(hidden)] * 2,
        out_shape=[jax.ShapeDtypeStruct(gate.shape, BF)] * 2,
        compiler_params=pltpu.CompilerParams(vmem_limit_bytes=GIANT),
    )(upstream, w_down, gate, up)


def greet(peers, axis="seq"):
    barrier = pltpu.get_barrier_semaphore()
    for peer in peers:
        pl.semaphore_signal(barrier, inc=1, device_id={axis: peer}, device_id_type=MESH)
    pl.semaphore_wait(barrier, len(peers))

def send(src, dst, send_sem, recv_sem, peer, axis="seq"):
    return pltpu.make_async_remote_copy(src_ref=src, dst_ref=dst, send_sem=send_sem, recv_sem=recv_sem,
        device_id={axis: peer}, device_id_type=MESH)

def ag_parts(n, x_ref, o_ref, local_sem, far_send, far_recv, near_send, near_recv):
    me = lax.axis_index("seq")
    core, chip, chips = me % 2, me // 2, n // 2
    sib = me + 1 - 2 * core
    far = [((chip + d) % chips) * 2 + core for d in range(1, chips)]
    mine = pltpu.make_async_copy(x_ref, o_ref.at[me], local_sem)
    out = [
        send(x_ref, o_ref.at[me], far_send.at[d], far_recv.at[d], far[d - 1]) for d in range(1, chips)
    ]
    near = [send(x_ref, o_ref.at[me], near_send.at[0], near_recv.at[0], sib)]

    def begin():
        for c in [mine] + out + near:
            c.start()

    def finish():
        for d in range(1, chips):
            out[d - 1].wait_recv()
            block = ((chip + chips - d) % chips) * 2 + core
            c = send(o_ref.at[block], o_ref.at[block], near_send.at[d], near_recv.at[d], sib)
            c.start()
            near.append(c)
        mine.wait()
        for c in near:
            c.wait()
        for c in out:
            c.wait_send()

    return begin, finish


def ag_kernel(n, x_ref, o_ref, *sems):
    me = lax.axis_index("seq")
    core, chip, chips = me % 2, me // 2, n // 2
    greet([me + 1 - 2 * core] + [((chip + d) % chips) * 2 + core for d in range(1, chips)])
    begin, finish = ag_parts(n, x_ref, o_ref, *sems)
    begin()
    finish()


def all_gather_any(x, n, cid):
    chips = n // 2
    return pl.pallas_call(functools.partial(ag_kernel, n),
        out_shape=jax.ShapeDtypeStruct((n,) + x.shape, x.dtype),
        in_specs=[pl.BlockSpec(memory_space=pl.ANY)],
        out_specs=pl.BlockSpec(memory_space=pl.ANY),
        scratch_shapes=[pltpu.SemaphoreType.DMA] + [pltpu.SemaphoreType.DMA((chips,))] * 4,
        compiler_params=pltpu.CompilerParams(collective_id=cid, has_side_effects=True),
    )(x)

def rs_kernel(n, p_ref, after_ref, o_ref, own, near, sums, got, local_sem, near_send, near_recv, far_send, far_recv):
    me = lax.axis_index("seq")
    core, chip, chips = me % 2, me // 2, n // 2
    sib = me + 1 - 2 * core
    step = lambda d: (chip + d) % chips
    far = [step(d) * 2 + core for d in range(1, chips)]
    greet([sib] + far)
    order = list(range(1, chips)) + [0]
    loads, nears, fars = {}, {}, {}
    for d in order:
        nears[d] = send(p_ref.at[step(d) * 2 + 1 - core], near.at[d], near_send.at[d], near_recv.at[d], sib)
        nears[d].start()
        loads[d] = pltpu.make_async_copy(p_ref.at[step(d) * 2 + core], own.at[d], local_sem.at[d])
        loads[d].start()
    rows = own.shape[1]
    slab = 16
    def each(body):
        def run(i, _):
            body(pl.ds(pl.multiple_of(i * slab, slab), slab))
            return 0
        lax.fori_loop(0, rows // slab, run, 0, unroll=2)
    for d in order:
        loads[d].wait()
        nears[d].wait_recv()
        if d:
            def add(at):
                sums[d - 1, at] = (own[d, at].astype(F32) + near[d, at].astype(F32)).astype(BF)
            each(add)
            fars[d] = send(sums.at[d - 1], got.at[d - 1], far_send.at[d - 1], far_recv.at[d - 1], far[d - 1])
            fars[d].start()
        else:
            def add(at):
                o_ref[at] = own[0, at].astype(F32) + near[0, at].astype(F32)
            each(add)
    for d in range(1, chips):
        fars[d].wait_recv()
        def add(at):
            o_ref[at] = o_ref[at] + got[d - 1, at].astype(F32)
        each(add)
    for d in order:
        nears[d].wait_send()
        if d: fars[d].wait_send()

def reduce_scatter_any(p, after, n, cid):
    chips = n // 2
    blk = p.shape[1:]
    return pl.pallas_call(functools.partial(rs_kernel, n),
        out_shape=jax.ShapeDtypeStruct(blk, F32),
        in_specs=[pl.BlockSpec(memory_space=pl.ANY)] * 2,
        out_specs=pl.BlockSpec(memory_space=pltpu.VMEM),
        scratch_shapes=[pltpu.VMEM((chips,) + blk, p.dtype), pltpu.VMEM((chips,) + blk, p.dtype),
            pltpu.VMEM((chips-1,) + blk, p.dtype), pltpu.VMEM((chips-1,) + blk, p.dtype),
            pltpu.SemaphoreType.DMA((chips,)), pltpu.SemaphoreType.DMA((chips,)), pltpu.SemaphoreType.DMA((chips,)),
            pltpu.SemaphoreType.DMA((chips-1,)), pltpu.SemaphoreType.DMA((chips-1,))],
        compiler_params=pltpu.CompilerParams(collective_id=cid, has_side_effects=True, vmem_limit_bytes=GIANT),
    )(p, after)

def stat_kernel(n, axis, x_ref, o_ref, got, send_sem, recv_sem):
    me = lax.axis_index(axis)
    peers = [(me + d) % n for d in range(1, n)]
    greet(peers, axis)
    copies = []
    for d in range(1, n):
        c = send(x_ref, got.at[d - 1], send_sem.at[d - 1], recv_sem.at[d - 1], peers[d - 1], axis)
        c.start()
        copies.append(c)
    total = x_ref[...]
    for d in range(1, n):
        copies[d - 1].wait_recv()
        total = total + got[d - 1]
    o_ref[...] = total
    for c in copies:
        c.wait_send()


def small_sum(x, n, cid, axis="seq"):
    return pl.pallas_call(
        functools.partial(stat_kernel, n, axis),
        out_shape=jax.ShapeDtypeStruct(x.shape, F32),
        in_specs=[pl.BlockSpec(memory_space=pltpu.VMEM)],
        out_specs=pl.BlockSpec(memory_space=pltpu.VMEM),
        scratch_shapes=[pltpu.VMEM((n - 1,) + x.shape, F32)] + [pltpu.SemaphoreType.DMA((n - 1,))] * 2,
        compiler_params=pltpu.CompilerParams(collective_id=cid, has_side_effects=True, vmem_limit_bytes=GIANT),
    )(x)


def square(me):
    core, x, y = me % 2, (me // 2) % 2, me // 4
    seat = lambda yy, xx, cc: (yy * 2 + xx) * 2 + cc
    return core, (seat(y, x, 1 - core), seat(y, 1 - x, core), seat(1 - y, x, core), seat(1 - y, 1 - x, core))

def ag4_parts(n, x_ref, o_ref, local_sem, far_send, far_recv, near_send, near_recv):
    me = lax.axis_index("seq")
    core, (sib, east, north, across) = square(me)
    half = x_ref.shape[0] // 2
    cut = (pl.ds(0, half), pl.ds(half, half))
    mine = pltpu.make_async_copy(x_ref, o_ref.at[me], local_sem)
    far, near = {}, []
    for slot, h, peer in ((0, 0, east), (2, 1, north), (1, 1, east), (3, 0, north)):
        far[slot] = send(x_ref.at[cut[h]], o_ref.at[me, cut[h]], far_send.at[slot], far_recv.at[slot], peer)
    near.append(send(x_ref, o_ref.at[me], near_send.at[6], near_recv.at[6], sib))

    def begin():
        mine.start()
        for slot in (0, 2, 1, 3):
            far[slot].start()
        near[0].start()

    def pass_on(slot, block, h):
        ref = o_ref.at[block, cut[h]]
        c = send(ref, ref, near_send.at[slot], near_recv.at[slot], sib)
        c.start()
        near.append(c)

    def finish():
        for slot, block, h, relay, to in (
            (0, east, 0, 4, north), (2, north, 1, 5, east), (1, east, 1, None, None), (3, north, 0, None, None)
        ):
            far[slot].wait_recv()
            if relay is not None:
                ref = o_ref.at[block, cut[h]]
                far[relay] = send(ref, ref, far_send.at[relay], far_recv.at[relay], to)
                far[relay].start()
            pass_on(slot, block, h)
        for slot, h in ((4, 0), (5, 1)):
            far[slot].wait_recv()
            pass_on(slot, across, h)
        mine.wait()
        for c in near:
            c.wait()
        for c in far.values():
            c.wait_send()

    return begin, finish


def ag4_kernel(x_ref, o_ref, *sems):
    core, (sib, east, north, across) = square(lax.axis_index("seq"))
    greet([sib, east, north])
    begin, finish = ag4_parts(8, x_ref, o_ref, *sems)
    begin()
    finish()


def all_gather4(x, n, cid):
    return pl.pallas_call(ag4_kernel,
        out_shape=jax.ShapeDtypeStruct((n,) + x.shape, x.dtype),
        in_specs=[pl.BlockSpec(memory_space=pl.ANY)],
        out_specs=pl.BlockSpec(memory_space=pl.ANY),
        scratch_shapes=[pltpu.SemaphoreType.DMA] + [pltpu.SemaphoreType.DMA((6,))] * 2 + [pltpu.SemaphoreType.DMA((7,))] * 2,
        compiler_params=pltpu.CompilerParams(collective_id=cid, has_side_effects=True),
    )(x)

def rs4_kernel(p_ref, after_ref, o_ref, own, near, got, local_sem, near_send, near_recv, far_send, far_recv):
    me = lax.axis_index("seq")
    core, (sib, east, north, across) = square(me)
    greet([sib, east, north])
    rows = own.shape[1]
    half = rows // 2
    cut = (pl.ds(0, half), pl.ds(half, half))
    seats = (across, east, north, me)
    loads, nears, far = [], [], {}
    for i, seat in enumerate(seats):
        other = seat + 1 - 2 * core
        c = send(p_ref.at[other], near.at[i], near_send.at[i], near_recv.at[i], sib)
        c.start(); nears.append(c)
        c = pltpu.make_async_copy(p_ref.at[seat], own.at[i], local_sem.at[i])
        c.start(); loads.append(c)
    slab = 16
    def each(first, count, body):
        def run(i, _):
            body(pl.ds(pl.multiple_of(first + i * slab, slab), slab), pl.ds(pl.multiple_of(i * slab, slab), slab))
            return 0
        lax.fori_loop(0, count // slab, run, 0, unroll=2)
    def fold(i):
        loads[i].wait(); nears[i].wait_recv()
        def add(at, _):
            own[i, at] = (own[i, at].astype(F32) + near[i, at].astype(F32)).astype(own.dtype)
        each(0, rows, add)
    def go(slot, i, h, peer):
        far[slot] = send(own.at[i, cut[h]], got.at[slot], far_send.at[slot], far_recv.at[slot], peer)
        far[slot].start()
    fold(0)
    go(0, 0, 0, east)
    go(1, 0, 1, north)
    fold(1)
    go(2, 1, 0, east)
    fold(2)
    go(3, 2, 1, north)
    def join(i, h, slot):
        far[slot].wait_recv()
        def add(at, src):
            own[i, at] = (own[i, at].astype(F32) + got[slot, src].astype(F32)).astype(own.dtype)
        each(h * half, half, add)
    join(2, 0, 0)
    go(4, 2, 0, north)
    join(1, 1, 1)
    go(5, 1, 1, east)
    loads[3].wait(); nears[3].wait_recv()
    def first(h, slot):
        far[slot].wait_recv()
        def add(at, src):
            o_ref[at] = own[3, at].astype(F32) + near[3, at].astype(F32) + got[slot, src].astype(F32)
        each(h * half, half, add)
    first(0, 2)
    first(1, 3)
    def last(h, slot):
        far[slot].wait_recv()
        def add(at, src):
            o_ref[at] = o_ref[at] + got[slot, src].astype(F32)
        each(h * half, half, add)
    last(0, 4)
    last(1, 5)
    for c in nears: c.wait_send()
    for c in far.values(): c.wait_send()

def reduce_scatter4(p, after, n, cid):
    blk = p.shape[1:]
    return pl.pallas_call(rs4_kernel,
        out_shape=jax.ShapeDtypeStruct(blk, F32),
        in_specs=[pl.BlockSpec(memory_space=pl.ANY)] * 2,
        out_specs=pl.BlockSpec(memory_space=pltpu.VMEM),
        scratch_shapes=[pltpu.VMEM((4,) + blk, p.dtype), pltpu.VMEM((4,) + blk, p.dtype),
            pltpu.VMEM((6, blk[0] // 2) + blk[1:], p.dtype)] + [pltpu.SemaphoreType.DMA((4,))] * 3 + [pltpu.SemaphoreType.DMA((6,))] * 2,
        compiler_params=pltpu.CompilerParams(collective_id=cid, has_side_effects=True, vmem_limit_bytes=GIANT),
    )(p, after)


def start_kernel(n, moves, x_ref, gain_ref, w_ref, in_ref, o_ref, c_ref, first_ref, second_ref,
                 normed_ref, cols_ref, swap_sem, swap_send, swap_recv, *sems):
    me = lax.axis_index("seq")
    others = [(me + d) % n for d in range(1, n)]
    barrier = pltpu.get_barrier_semaphore()
    for peer in others:
        pl.semaphore_signal(barrier, inc=1, device_id={"seq": peer}, device_id_type=MESH)
    x = x_ref[...].astype(F32)
    scale = lax.rsqrt(jnp.mean(x * x, axis=-1, keepdims=True) + EPSILON)
    normed_ref[...] = (x * scale * gain_ref[...]).astype(BF)
    pl.semaphore_wait(barrier, n - 1)
    gather_start, gather_end = (ag4_parts if n == 8 else ag_parts)(n, normed_ref, o_ref, *sems)
    gather_start()
    for i in range(n):
        if sum(size for _, _, size in moves[i]) < cols_ref.shape[2]:
            cols_ref[i] = jnp.zeros(cols_ref.shape[1:], BF)
        for dst, src, size in moves[i]:
            cols_ref[i, :, dst : dst + size] = w_ref[:, src : src + size]
    own = pltpu.make_async_copy(cols_ref.at[me], c_ref.at[me], swap_sem)
    own.start()
    swaps = []
    for d in range(1, n):
        peer = others[d - 1]
        c = send(cols_ref.at[peer], c_ref.at[me], swap_send.at[d - 1], swap_recv.at[d - 1], peer)
        c.start()
        swaps.append(c)
    width = first_ref.shape[2]
    for i in range(n):
        first_ref[i] = in_ref[:, i * width : (i + 1) * width]
        second_ref[i] = in_ref[:, (n + i) * width : (n + i + 1) * width]
    gather_end()
    own.wait()
    for c in swaps:
        c.wait()


def gather_and_exchange(x, gain, w, moves, width, w_in, n, cid):
    far, near = (6, 7) if n == 8 else (n // 2, n // 2)
    anywhere = pl.BlockSpec(memory_space=pl.ANY)
    vmem = pl.BlockSpec(memory_space=pltpu.VMEM)
    dma = pltpu.SemaphoreType.DMA
    cols = jax.ShapeDtypeStruct((n, w.shape[0], width), BF)
    part = jax.ShapeDtypeStruct((n, w_in.shape[0], w_in.shape[1] // (2 * n)), BF)
    return pl.pallas_call(
        functools.partial(start_kernel, n, moves),
        out_shape=[jax.ShapeDtypeStruct((n,) + x.shape, BF), cols, part, part],
        in_specs=[vmem] * 4,
        out_specs=[anywhere] * 2 + [vmem] * 2,
        scratch_shapes=[pltpu.VMEM(x.shape, BF), pltpu.VMEM(cols.shape, BF), dma, dma((n - 1,)), dma((n - 1,)),
                        dma, dma((far,)), dma((far,)), dma((near,)), dma((near,))],
        compiler_params=pltpu.CompilerParams(collective_id=cid, has_side_effects=True, vmem_limit_bytes=GIANT),
    )(x, gain[None], w, w_in)


def sum4_kernel(p_ref, after_ref, o_ref, total, low, *rest):
    rs4_kernel(p_ref, after_ref, total, *rest[:8])
    low[...] = total[...].astype(BF)
    begin, finish = ag4_parts(8, low, o_ref, *rest[8:])
    begin()
    finish()


def all_sum(p, n, cid, after=None):
    after = jnp.zeros((8, 128), F32) if after is None else after
    if n != 8:
        return all_gather(reduce_scatter(p, n, cid, after).astype(BF), n, cid + 1)
    blk = p.shape[1:]
    dma = pltpu.SemaphoreType.DMA
    return pl.pallas_call(
        sum4_kernel,
        out_shape=jax.ShapeDtypeStruct(p.shape, BF),
        in_specs=[pl.BlockSpec(memory_space=pl.ANY)] * 2,
        out_specs=pl.BlockSpec(memory_space=pl.ANY),
        scratch_shapes=[
            pltpu.VMEM(blk, F32), pltpu.VMEM(blk, BF),
            pltpu.VMEM((4,) + blk, BF), pltpu.VMEM((4,) + blk, BF), pltpu.VMEM((6, blk[0] // 2) + blk[1:], BF),
            dma((4,)), dma((4,)), dma((4,)), dma((6,)), dma((6,)),
            dma, dma((6,)), dma((6,)), dma((7,)), dma((7,)),
        ],
        compiler_params=pltpu.CompilerParams(collective_id=cid, has_side_effects=True, vmem_limit_bytes=GIANT),
    )(p, after)


def all_gather(x, n, cid):
    return (all_gather4 if n == 8 else all_gather_any)(x, n, cid)


def reduce_scatter(p, n, cid, after=None):
    after = jnp.zeros((8, 128), F32) if after is None else after
    return (reduce_scatter4 if n == 8 else reduce_scatter_any)(p, after, n, cid)


def mm_rs4_kernel(turned, seconds, firsts, *refs):
    terms = len(turned)
    count = max(seconds) + 1
    a_refs, b_refs = refs[:terms], refs[terms : terms + count]
    after_ref, o_ref, part, near, got, near_send, near_recv, far_send, far_recv = refs[terms + count :]
    me = lax.axis_index("seq")
    core, (sib, east, north, across) = square(me)
    x, y = (me // 2) % 2, me // 4
    greet([sib, east, north])
    rows = part.shape[2]
    half = rows // 2
    cut = (pl.ds(0, half), pl.ds(half, half))
    slab = 16
    own = part.at[1]

    def near_copy(i):
        return send(part.at[0, i], near.at[i], near_send.at[i], near_recv.at[i], sib)

    hops = ((0, 0, east), (0, 1, north), (1, 0, east), (2, 1, north), (2, 0, north), (1, 1, east))

    def far_copy(slot):
        i, h, peer = hops[slot]
        return send(own.at[i, cut[h]], got.at[slot], far_send.at[slot], far_recv.at[slot], peer)

    def each(first, count, body):
        def run(i, _):
            at = pl.multiple_of(i * slab, slab)
            body(pl.ds(pl.multiple_of(first + at, slab), slab), pl.ds(at, slab))
            return 0

        lax.fori_loop(0, count // slab, run, 0, unroll=2)

    def fold(i):
        near_copy(i).wait_recv()

        def add(at, _):
            own[i, at] = (own[i, at].astype(F32) + near[i, at].astype(F32)).astype(BF)

        each(0, rows, add)

    def step(s, _):
        i, mine = s // 2, s % 2
        yy, xx = (y + (i + 1) % 2) % 2, (x + 1 - i // 2) % 2
        seat = (yy * 2 + xx) * 2 + (core + 1 - mine) % 2
        total = None
        for a, t, at, first in zip(a_refs, turned, seconds, firsts):
            b = b_refs[at]
            term = ntdot(a[seat], b[...]) if t else dot(a[seat], b[first : first + a.shape[2]])
            total = term if total is None else total + term
        part[mine, i] = total.astype(BF)

        @pl.when(mine == 0)
        def _():
            near_copy(i).start()

        @pl.when(s == 2)
        def _():
            fold(0)
            far_copy(0).start()
            far_copy(1).start()

        @pl.when(s == 4)
        def _():
            fold(1)
            far_copy(2).start()

        @pl.when(s == 6)
        def _():
            fold(2)
            far_copy(3).start()

        return 0

    lax.fori_loop(0, 8, step, 0)

    def join(i, h, slot):
        far_copy(slot).wait_recv()

        def add(at, src):
            own[i, at] = (own[i, at].astype(F32) + got[slot, src].astype(F32)).astype(BF)

        each(h * half, half, add)

    join(2, 0, 0)
    far_copy(4).start()
    join(1, 1, 1)
    far_copy(5).start()
    near_copy(3).wait_recv()

    def first(h, slot):
        far_copy(slot).wait_recv()

        def add(at, src):
            o_ref[at] = own[3, at].astype(F32) + near[3, at].astype(F32) + got[slot, src].astype(F32)

        each(h * half, half, add)

    first(0, 2)
    first(1, 3)

    def last(h, slot):
        far_copy(slot).wait_recv()

        def add(at, src):
            o_ref[at] = o_ref[at] + got[slot, src].astype(F32)

        each(h * half, half, add)

    last(0, 4)
    last(1, 5)
    for i in range(4):
        near_copy(i).wait_send()
    for slot in range(6):
        far_copy(slot).wait_send()


def product_scatter(pairs, n, cid, after=None):
    after = jnp.zeros((8, 128), F32) if after is None else after
    rows = pairs[0][0].shape[0] // n
    cols = pairs[0][1].shape[0 if pairs[0][2] else 1]
    bs, seconds, firsts, used = [], [], [], []
    for a, b, t in pairs:
        if not any(b is other for other in bs):
            bs.append(b)
            used.append(0)
        at = [b is other for other in bs].index(True)
        seconds.append(at)
        firsts.append(used[at])
        used[at] += a.shape[1]
    if n != 8:
        total = sum(
            ntdot(a, b) if t else dot(a, b[first : first + a.shape[1]])
            for (a, b, t), first in zip(pairs, firsts)
        )
        return reduce_scatter(total.astype(BF).reshape(n, rows, cols), n, cid, after)
    vmem = pl.BlockSpec(memory_space=pltpu.VMEM)
    dma = pltpu.SemaphoreType.DMA
    return pl.pallas_call(
        functools.partial(mm_rs4_kernel, tuple(t for _, _, t in pairs), tuple(seconds), tuple(firsts)),
        out_shape=jax.ShapeDtypeStruct((rows, cols), F32),
        in_specs=[vmem] * (len(pairs) + len(bs)) + [pl.BlockSpec(memory_space=pl.ANY)],
        out_specs=vmem,
        scratch_shapes=[
            pltpu.VMEM((2, 4, rows, cols), BF),
            pltpu.VMEM((4, rows, cols), BF),
            pltpu.VMEM((6, rows // 2, cols), BF),
            dma((4,)), dma((4,)), dma((6,)), dma((6,)),
        ],
        compiler_params=pltpu.CompilerParams(collective_id=cid, has_side_effects=True, vmem_limit_bytes=GIANT),
    )(*(a.reshape(n, rows, a.shape[1]) for a, _, _ in pairs), *bs, after)


def chain_kernel(axis, count, cuts, *refs):
    arrays = len(cuts)
    x_refs, after_ref, o_refs = refs[:arrays], refs[arrays], refs[arrays + 1 : 2 * arrays + 1]
    rest = refs[2 * arrays + 1 :]
    up_in, up_out, down_in, down_out = (rest[k * arrays : (k + 1) * arrays] for k in range(4))
    up_send, up_recv, down_send, down_recv = rest[4 * arrays :]
    me = lax.axis_index(axis)
    first, last = me == 0, me == count - 1
    above, below = (me + 1) % count, (me + count - 1) % count
    barrier = pltpu.get_barrier_semaphore()

    @pl.when(me > 0)
    def _():
        pl.semaphore_signal(barrier, inc=1, device_id={axis: below}, device_id_type=MESH)

    @pl.when(me < count - 1)
    def _():
        pl.semaphore_signal(barrier, inc=1, device_id={axis: above}, device_id_type=MESH)

    @pl.when((me > 0) & (me < count - 1))
    def _():
        pl.semaphore_wait(barrier, 2)

    @pl.when(first | last)
    def _():
        pl.semaphore_wait(barrier, 1)

    pieces = [(k, c) for k in range(arrays) for c in range(cuts[k])]
    lane = lambda k: x_refs[k].shape[1] // cuts[k]
    at = lambda k, c: slice(c * lane(k), (c + 1) * lane(k))

    def up(s, k, c):
        return send(up_out[k].at[c], up_in[k].at[c], up_send.at[s], up_recv.at[s], above, axis)

    def down(s, k, c):
        return send(down_out[k].at[c], down_in[k].at[c], down_send.at[s], down_recv.at[s], below, axis)

    for s, (k, c) in enumerate(pieces):
        own = x_refs[k][:, at(k, c)]

        @pl.when(first)
        def _():
            up_out[k][c] = own
            up(s, k, c).start()

        @pl.when(last)
        def _():
            down_out[k][c] = own
            down(s, k, c).start()

    own = lambda s: x_refs[pieces[s][0]][:, at(*pieces[s])].astype(F32)

    def serve_up(s):
        k, c = pieces[s]

        @pl.when(me > 0)
        def _():
            up(s, k, c).wait_recv()

            @pl.when(me < count - 1)
            def _():
                up_out[k][c] = (own(s) + up_in[k][c].astype(F32)).astype(BF)
                up(s, k, c).start()

    def serve_down(s):
        k, c = pieces[s]

        @pl.when(me < count - 1)
        def _():
            down(s, k, c).wait_recv()

            @pl.when(me > 0)
            def _():
                down_out[k][c] = (own(s) + down_in[k][c].astype(F32)).astype(BF)
                down(s, k, c).start()

    def finish(s):
        k, c = pieces[s]
        put = lambda value: o_refs[k].__setitem__((slice(None), at(k, c)), value)

        @pl.when(first)
        def _():
            put(own(s) + down_in[k][c].astype(F32))

        @pl.when(last)
        def _():
            put(own(s) + up_in[k][c].astype(F32))

        @pl.when((me > 0) & (me < count - 1))
        def _():
            put(own(s) + up_in[k][c].astype(F32) + down_in[k][c].astype(F32))

    for s in range(len(pieces) + 1):
        for side, early, late in ((me * 2 < count, serve_up, serve_down), (me * 2 >= count, serve_down, serve_up)):
            @pl.when(side)
            def _():
                if s < len(pieces):
                    early(s)
                if s:
                    late(s - 1)

        if s:
            finish(s - 1)

    for s, (k, c) in enumerate(pieces):
        @pl.when(me < count - 1)
        def _():
            up(s, k, c).wait_send()

        @pl.when(me > 0)
        def _():
            down(s, k, c).wait_send()


def chain_sum(arrays, cuts, count, cid, after, axis="dp"):
    vmem = pl.BlockSpec(memory_space=pltpu.VMEM)
    total = sum(cuts)
    slots = [pltpu.VMEM((c, a.shape[0], a.shape[1] // c), BF) for a, c in zip(arrays, cuts)]
    return pl.pallas_call(
        functools.partial(chain_kernel, axis, count, tuple(cuts)),
        out_shape=[jax.ShapeDtypeStruct(a.shape, F32) for a in arrays],
        in_specs=[vmem] * len(arrays) + [pl.BlockSpec(memory_space=pl.ANY)],
        out_specs=[vmem] * len(arrays),
        scratch_shapes=slots * 4 + [pltpu.SemaphoreType.DMA((total,))] * 4,
        compiler_params=pltpu.CompilerParams(collective_id=cid, has_side_effects=True, vmem_limit_bytes=GIANT),
    )(*arrays, after)


def gather_product4_kernel(body, weights, aligned, x_ref, *refs):
    w_refs, refs = refs[:weights], refs[weights:]
    row_refs, o_ref = refs[:aligned], refs[aligned]
    results, (mine_sem, far_send, far_recv, near_send, near_recv) = refs[aligned + 1 : -5], refs[-5:]
    me = lax.axis_index("seq")
    core, (sib, east, north, across) = square(me)
    x, y = (me // 2) % 2, me // 4
    greet([sib, east, north])
    half = x_ref.shape[0] // 2
    cut = (pl.ds(0, half), pl.ds(half, half))
    hops = (
        (me, 0, east), (me, 1, east), (me, 1, north), (me, 0, north), (east, 0, north), (north, 1, east)
    )
    handed = ((east, 0), (east, 1), (north, 1), (north, 0), (across, 0), (across, 1))

    def far(slot):
        block, h, peer = hops[slot]
        ref = o_ref.at[block, cut[h]]
        return send(x_ref.at[cut[h]] if slot < 4 else ref, ref, far_send.at[slot], far_recv.at[slot], peer)

    def near(slot):
        if slot == 6:
            return send(x_ref, o_ref.at[me], near_send.at[6], near_recv.at[6], sib)
        block, h = handed[slot]
        ref = o_ref.at[block, cut[h]]
        return send(ref, ref, near_send.at[slot], near_recv.at[slot], sib)

    mine = pltpu.make_async_copy(x_ref, o_ref.at[me], mine_sem)
    mine.start()
    for slot in (0, 2, 1, 3):
        far(slot).start()
    near(6).start()

    def arrive(slot, relay=None):
        far(slot).wait_recv()
        if relay is not None:
            far(relay).start()
        near(slot).start()

    def step(s, _):
        @pl.when(s == 0)
        def _():
            mine.wait()

        @pl.when(s == 1)
        def _():
            near(6).wait_recv()

        @pl.when(s == 2)
        def _():
            arrive(0, 4)
            arrive(2, 5)
            arrive(1)

        @pl.when(s == 3)
        def _():
            near(0).wait_recv()
            near(1).wait_recv()

        @pl.when(s == 4)
        def _():
            arrive(3)

        @pl.when(s == 5)
        def _():
            near(2).wait_recv()
            near(3).wait_recv()

        @pl.when(s == 6)
        def _():
            arrive(4)
            arrive(5)

        @pl.when(s == 7)
        def _():
            near(4).wait_recv()
            near(5).wait_recv()

        pair = s // 2
        seat = (((y + pair // 2) % 2) * 2 + (x + pair % 2) % 2) * 2 + (core + s) % 2
        for ref, value in zip(results, body(o_ref[seat], *w_refs, *(ref[seat] for ref in row_refs))):
            ref[seat] = value.astype(ref.dtype)
        return 0

    lax.fori_loop(0, 8, step, 0)
    for slot in range(7):
        near(slot).wait_send()
    for slot in range(6):
        far(slot).wait_send()


def gather_product(body, x, weights, outs, n, cid, by_rows=()):
    rows = x.shape[0]
    if n != 8:
        whole = all_gather(x, n, cid)
        values = body(
            whole.reshape(n * rows, -1), *weights, *(a.reshape(n * rows, a.shape[2]) for a in by_rows)
        )
        return [whole] + [v.astype(t).reshape(n, rows, -1) for v, (_, t) in zip(values, outs)]
    vmem = pl.BlockSpec(memory_space=pltpu.VMEM)
    dma = pltpu.SemaphoreType.DMA
    return pl.pallas_call(
        functools.partial(gather_product4_kernel, body, len(weights), len(by_rows)),
        out_shape=[jax.ShapeDtypeStruct((n,) + x.shape, x.dtype)]
        + [jax.ShapeDtypeStruct((n, rows, c), t) for c, t in outs],
        in_specs=[vmem] * (1 + len(weights) + len(by_rows)),
        out_specs=[vmem] * (1 + len(outs)),
        scratch_shapes=[dma, dma((6,)), dma((6,)), dma((7,)), dma((7,))],
        compiler_params=pltpu.CompilerParams(collective_id=cid, has_side_effects=True, vmem_limit_bytes=GIANT),
    )(x, *weights, *by_rows)


class HeadPlan:
    def __init__(self, n):
        self.n = n
        self.per = -(-HEADS // n)
        group = HEADS // KVH
        self.first_kv, self.slots = [], 1
        for i in range(n):
            low, high = i * self.per, min((i + 1) * self.per, HEADS) - 1
            if low >= HEADS:
                self.first_kv.append(KVH)
            else:
                self.first_kv.append(low // group)
                self.slots = max(self.slots, high // group - low // group + 1)
        self.width = self.per * HEAD
        self.kv_width = self.slots * HEAD

    def head_table(self):
        group = HEADS // KVH
        rows = []
        for i in range(self.n):
            heads = [i * self.per + j for j in range(self.per)]
            rows.append(
                [h // group - self.first_kv[i] if h < HEADS else 0 for h in heads]
                + [int(h < HEADS) for h in heads]
            )
        return jnp.array(rows, jnp.int32)

    def kv_used(self, i):
        group = HEADS // KVH
        heads = range(i * self.per, min((i + 1) * self.per, HEADS))
        return sorted({h // group for h in heads})

    def moves(self):
        lists = []
        for i in range(self.n):
            first = i * self.width
            mine = [(0, first, min(self.width, HEADS * HEAD - first))] if first < HEADS * HEAD else []
            for kind in range(2):
                start = HEADS * HEAD + kind * KVH * HEAD
                for g in self.kv_used(i):
                    slot = g - self.first_kv[i]
                    mine.append((self.width + kind * self.kv_width + slot * HEAD, start + g * HEAD, HEAD))
            lists.append(tuple(mine))
        return tuple(lists)

    def join_columns(self, g):
        q = [g[i, :, : self.width] for i in range(self.n)]
        q = jnp.concatenate(q, axis=1)[:, : HEADS * HEAD].astype(F32)
        kv = []
        for kind in range(2):
            for head in range(KVH):
                total = 0.0
                for i in range(self.n):
                    if head in self.kv_used(i):
                        at = self.width + kind * self.kv_width + (head - self.first_kv[i]) * HEAD
                        total = total + g[i, :, at : at + HEAD].astype(F32)
                kv.append(total)
        return jnp.concatenate([q] + kv, axis=1)


def reblock(rows, have, want, total):
    n, me = lax.axis_size("seq"), lax.axis_index("seq")
    result = jnp.zeros((want,) + rows.shape[1:], rows.dtype)
    pad = jnp.pad(rows, ((want, want), (0, 0)))
    for shift in range(-(n - 1), n):
        pairs = []
        for i in range(n):
            j = i + shift
            if 0 <= j < n:
                low = max(i * have, j * want)
                high = min((i + 1) * have, (j + 1) * want, total)
                if low < high:
                    pairs.append((i, j))
        if not pairs:
            continue
        start = want + (me + shift) * want - me * have
        piece = lax.dynamic_slice_in_dim(pad, jnp.clip(start, 0, have + want), want, 0)
        if shift:
            piece = lax.ppermute(piece, "seq", pairs)
        else:
            ok = jnp.array([(i, i) in pairs for i in range(n)])[me]
            piece = jnp.where(ok, piece, jnp.zeros_like(piece))
        result = result + piece
    return result


def per_device(tokens, lengths, cotangent, w_qkv, w_ao, w_in, w_xp, w_dt, w_so, w_gu, w_down,
               norm_in, norm_attn, norm_ssm, norm_ffn, conv_w, conv_b, dt_bias, a_log, d_skip):
    seqs, slot_len, width = tokens.shape
    n, me, replicas = lax.axis_size("seq"), lax.axis_index("seq"), lax.axis_size("dp")
    local, rows = seqs * slot_len, seqs * slot_len * n
    cols = INNER // n
    plan = HeadPlan(n)
    w_rows, ao_rows = w_qkv.shape[0], w_ao.shape[0]
    pos = me * slot_len + jnp.arange(slot_len, dtype=jnp.int32)
    is_valid = pos[None, :] < lengths[:, None]
    table = plan.head_table()[me]
    tie = lax.optimization_barrier
    flat = lambda v: v.reshape(rows, v.shape[-1])
    later = lambda g, zero: g + zero.astype(g.dtype)
    nothing = lambda *sums: 0.0 * sum(g.reshape(-1)[0].astype(F32) for g in sums)
    mark = lambda zero: jnp.full((8, 128), zero)
    by_device = lambda m: m.reshape(n, local, m.shape[-1])
    exchange = lambda v: lax.all_to_all(v, "seq", 0, 0, tiled=True)
    blocks = lambda v: v.reshape(n, seqs, slot_len, v.shape[-1])
    mine = lambda v: lax.dynamic_slice_in_dim(v, me * cols, cols, v.ndim - 1)
    over = lambda g: lax.psum(g, "dp")

    def one_step(work):
        shapes = jax.eval_shape(work, 0)
        none = lambda _: jax.tree.map(lambda t: jnp.zeros(t.shape, t.dtype), shapes)
        return lax.cond(lengths[0] > 0, work, none, 0)

    def row_sums(a, b, cid):
        both = jnp.stack([a, b]).reshape(-1, 128)
        return small_sum(both, n, cid).reshape(2, rows)

    wdt = mine(w_dt)
    taps, bias, dtb, skip = mine(conv_w), mine(conv_b), mine(dt_bias), mine(d_skip)
    rate = -jnp.exp(mine(a_log))
    ssm_gain = mine(norm_ssm)
    attn_gain = lax.dynamic_slice_in_dim(
        jnp.pad(norm_attn, (0, n * plan.width - HEADS * HEAD)), me * plan.width, plan.width, 0
    )

    x = tokens.astype(F32).reshape(local, width)
    scale_in = lax.rsqrt(jnp.mean(x * x, axis=-1, keepdims=True) + EPSILON)
    normed, qkv_cols, in_x, in_z = gather_and_exchange(
        tokens.reshape(local, width), norm_in, w_qkv, plan.moves(), plan.width + 2 * plan.kv_width, w_in, n, 1
    )
    normed, qkv_cols = flat(normed), qkv_cols.reshape(n * w_rows, -1)
    wx, wz = exchange(in_x), exchange(in_z)
    heads = attn_forward(0, table, lengths, blocks(normed), qkv_cols, plan.width)
    behind = nothing(heads[1])
    for seq in range(1, seqs):
        heads = attn_forward(seq, table, lengths, blocks(normed), qkv_cols, plan.width, heads)
    attended, lse, q, k, v = heads
    ao_all = lax.all_gather(later(w_ao, behind), "seq", axis=0, tiled=True)
    ao_mine = lax.dynamic_slice_in_dim(
        jnp.pad(ao_all, ((0, n * plan.width - HEADS * HEAD), (0, 0))), me * plan.width, plan.width, 0
    )
    upstream = (cotangent.astype(F32) * is_valid[..., None]).reshape(local, width)
    upstream_all = lax.all_gather(later(upstream.astype(BF), behind), "seq", axis=0, tiled=True)
    wx = later(wx, nothing(lse)).reshape(n * w_rows, cols)
    wz = wz.reshape(n * w_rows, cols)
    xp = jnp.swapaxes(w_xp, 0, 1)
    xp = jnp.concatenate([xp[DTR:], xp[:DTR]], axis=0)
    x_conv, conv_pre, mixer_in, mixer_low, projected = signal_forward(blocks(normed), wx, taps, bias[None], xp)
    mixer_low = flat(mixer_low)
    projected = blocks(all_sum(by_device(projected), n, 15))
    core, z_gate, ssm_sq, start = scan_forward(
        projected, mixer_in, blocks(normed), wz, wdt, dtb[None], rate, skip[None]
    )
    squares = row_sums(jnp.sum(attended * attended, axis=3).reshape(rows), ssm_sq.reshape(rows), 2)
    r_attn = lax.rsqrt(squares[0] / (HEADS * HEAD) + EPSILON)
    r_ssm = lax.rsqrt(squares[1] / INNER + EPSILON)
    attn_low, ssm_low = map(flat, norm_both(
        by_device(squares.T), by_device(attended), attn_gain[None], by_device(core), by_device(z_gate), ssm_gain[None]
    ))
    mixed = product_scatter(((attn_low, ao_mine, False), (ssm_low, w_so, False)), n, 3)
    residual = x + 0.5 * mixed
    r_ffn = lax.rsqrt(jnp.mean(residual * residual, axis=-1, keepdims=True) + EPSILON)
    turned = jnp.transpose(w_gu, (1, 2, 0))
    w_gate, w_up = turned[0], turned[1]
    hidden = w_gate.shape[0]

    def gated_units(rows_in, gate_ref, up_ref):
        gate, up = ntdot(rows_in, gate_ref[...]), ntdot(rows_in, up_ref[...])
        return gate, up, jax.nn.silu(gate) * up

    normed_two, gate, up, activated = gather_product(
        gated_units, (residual * r_ffn * norm_ffn).astype(BF), (w_gate, w_up), ((hidden, BF),) * 3, n, 4
    )
    normed_two, activated = flat(normed_two), flat(activated)

    grad_gate, grad_up = map(flat, ffn_backward(by_device(upstream_all), w_down, gate, up))
    g_down = tndot(activated, upstream_all).astype(BF)
    g_gate, g_up = tndot(grad_gate, normed_two).astype(BF), tndot(grad_up, normed_two).astype(BF)
    g_down, g_gate, g_up = tie((g_down, g_gate, g_up))
    s_down, s_gate, s_up = over((g_down, g_gate, g_up))
    grad_two = product_scatter(
        ((grad_gate, w_gate, False), (grad_up, w_up, False)), n, 5, mark(nothing(g_gate, g_up))
    )

    def norm_pull(grad, values, r, gain):
        dotted = jnp.mean(grad * gain * values, axis=-1, keepdims=True)
        return r * (grad * gain - values * (r * r * dotted)), jnp.sum(grad * values * r, axis=0)

    add, g_norm_ffn = norm_pull(grad_two, residual, r_ffn, norm_ffn)
    grad_residual = upstream + add

    def heads_and_channels(rows_in, ao_ref, so_ref, head_gain, channel_gain, heads_out, core_out, gate_out):
        of_heads = 0.5 * ntdot(rows_in, ao_ref[...])
        of_channels = 0.5 * ntdot(rows_in, so_ref[...])
        gated = core_out * (gate_out * jax.nn.sigmoid(gate_out))
        sums = [
            jnp.sum(of_heads * head_gain[...] * heads_out, axis=1, keepdims=True),
            jnp.sum(of_channels * channel_gain[...] * gated, axis=1, keepdims=True),
        ]
        return of_heads, of_channels, jnp.concatenate(sums, axis=1)

    mix_low, d_attn, d_ssm, inner = gather_product(
        heads_and_channels, grad_residual.astype(BF), (ao_mine, w_so, attn_gain[None], ssm_gain[None]),
        ((plan.width, F32), (cols, F32), (2, F32)), n, 7, (by_device(attended), by_device(core), by_device(z_gate)),
    )
    mix_low, inner = flat(mix_low), inner.reshape(rows, 2)
    inner = row_sums(inner[:, 0], inner[:, 1], 8)
    stats = blocks(jnp.stack([
        r_attn, inner[0] / (HEADS * HEAD) * r_attn * r_attn, r_ssm, inner[1] / INNER * r_ssm * r_ssm
    ], axis=1))

    def mixers_back(_):
        gq, gk, gv, head_sums = attn_backward(
            table, lengths, q, k, v, blocks(d_attn), attended, lse, stats, attn_gain[None]
        )
        gpre, gmix, gz, gb, gc, grate, channel_sums = scan_backward(
            lengths, projected, mixer_in, blocks(d_ssm), core, z_gate, stats, start, wdt, dtb[None], rate, skip[None],
            ssm_gain[None],
        )
        grad_qkv, grad_z = flat(jnp.concatenate([gq, gk, gv], axis=3)), flat(gz)
        of_weights = (
            (0.5 * tndot(attn_low, mix_low)).astype(BF),
            (0.5 * tndot(ssm_low, mix_low)).astype(BF),
            tndot(normed, grad_z).astype(BF),
            tndot(normed, grad_qkv).astype(BF),
        )
        return head_sums[0], channel_sums, grad_qkv, grad_z, flat(gpre), gmix, flat(gb), flat(gc), grate, of_weights

    g_norm_attn, channel_sums, grad_qkv, grad_z, grad_step, gmix, gb, gc, grate, of_weights = one_step(mixers_back)
    g_norm_ssm, gskip, g_dt_bias = channel_sums[0], channel_sums[1:2], channel_sums[2]
    g_ao, g_so, g_z, g_qkv = of_weights
    g_ao = reblock(g_ao, plan.width, ao_rows, HEADS * HEAD)
    g_z = exchange(g_z.reshape(n, w_rows, cols))
    g_z = jnp.swapaxes(g_z, 0, 1).reshape(w_rows, INNER)
    g_qkv = exchange(g_qkv.reshape(n, w_rows, -1))
    g_qkv = plan.join_columns(g_qkv).astype(BF)
    first_sums = nothing(s_down, s_gate, s_up)
    grad_projected = jnp.concatenate([gb, gc, ntdot(grad_step, wdt)], axis=1)
    grad_projected = flat(all_sum(by_device(grad_projected.astype(BF)), n, 9, mark(first_sums)))
    after_one = first_sums + nothing(grad_projected)
    s_ao, s_so, s_qkv, s_z = over(tuple(later(g, after_one) for g in (g_ao, g_so, g_qkv, g_z)))

    def signal_back(_):
        grad_x, sums = signal_backward(gmix, blocks(grad_projected), xp, conv_pre, x_conv, taps)
        grad_x = flat(grad_x)
        return (
            grad_x,
            sums,
            tndot(normed, grad_x).astype(BF),
            tndot(grad_projected, mixer_low).astype(BF),
            tndot(grad_step, flat(projected)[:, 2 * NST :]).astype(BF),
        )

    grad_x, tap_sums, g_x, g_xp, g_wdt = one_step(signal_back)
    g_conv_w, g_conv_b = tap_sums[:KCONV], tap_sums[KCONV]
    g_x = exchange(g_x.reshape(n, w_rows, cols))
    g_x = jnp.swapaxes(g_x, 0, 1).reshape(w_rows, INNER)
    grad_normed = product_scatter(
        ((grad_x, wx, True), (grad_z, wz, True), (grad_qkv, qkv_cols, True)), n, 11
    )
    block_out = residual + product_scatter(
        ((activated, w_down, False),), n, 6, mark(nothing(grad_normed))
    )
    add_in, g_norm_in = norm_pull(grad_normed, x, scale_in, norm_in)
    grad_tokens = grad_residual + add_in

    s_gu = jnp.transpose(jnp.stack([s_gate, s_up]), (2, 0, 1))
    s_x, s_xp, s_wdt = chain_sum((g_x, g_xp, g_wdt), (5, 1, 1), replicas, 14, mark(nothing(block_out, s_ao, s_so, s_qkv, s_z)))
    s_in = jnp.concatenate([s_x, s_z.astype(F32)], axis=1)
    s_xp = jnp.swapaxes(jnp.concatenate([s_xp[2 * NST :], s_xp[: 2 * NST]], axis=0), 0, 1)
    s_wdt = jnp.swapaxes(s_wdt, 0, 1)

    place = lambda g: lax.dynamic_update_slice_in_dim(
        jnp.zeros((n * plan.width,), F32), g, me * plan.width, 0
    )[: HEADS * HEAD]

    def pad_rows(v):
        v = v.reshape(-1)
        return jnp.pad(v, (0, -v.size % 1024)).reshape(-1, 128)

    shared = jnp.stack([g_norm_in, place(g_norm_attn), g_norm_ffn])
    total = small_sum(pad_rows(shared), n, 12).reshape(-1)[: shared.size].reshape(shared.shape)
    shared = lax.dynamic_slice_in_dim(total, me * w_rows, w_rows, 1)
    owned = jnp.concatenate(
        [g_norm_ssm[None], g_conv_w, g_conv_b[None], g_dt_bias[None], grate * rate, gskip], axis=0
    )
    small = pad_rows(jnp.concatenate([shared.reshape(-1), owned.reshape(-1)]))
    small = small_sum(small, replicas, 13, "dp").reshape(-1)
    s_shared = small[: shared.size].reshape(shared.shape)
    s_owned = small[shared.size : shared.size + owned.size].reshape(owned.shape)
    full = lambda g: g.astype(F32)

    return (
        block_out.astype(BF).reshape(seqs, slot_len, width),
        grad_tokens.reshape(seqs, slot_len, width),
        full(s_qkv),
        full(s_ao),
        full(s_in),
        full(s_xp),
        full(s_wdt),
        full(s_so),
        full(s_gu),
        full(s_down),
        s_shared[0],
        s_shared[1],
        s_owned[0],
        s_shared[2],
        s_owned[1 : 1 + KCONV],
        s_owned[1 + KCONV],
        s_owned[2 + KCONV],
        s_owned[3 + KCONV : 3 + KCONV + NST],
        s_owned[3 + KCONV + NST],
    )


def solution(mesh):
    rows, cols, flat = P("seq", None), P(None, "seq"), P("seq")
    act = P("dp", "seq", None)
    hid = P(None, None, "seq")
    in_specs = (act, P("dp"), act, rows, rows, rows, rows, P(), rows, hid, rows) + (P(),) * 9
    out_specs = (act, act, rows, rows, rows, rows, cols, rows, hid, rows,
                 flat, flat, flat, flat, cols, flat, flat, cols, flat)
    return jax.shard_map(per_device, mesh=mesh, in_specs=in_specs, out_specs=out_specs, check_vma=False)
```

```python
import functools
import math

import jax
import jax.numpy as jnp
from jax import lax
from jax.experimental import pallas as pl
from jax.experimental.pallas import tpu as pltpu
from jax.sharding import PartitionSpec as P

HEADS = 25
HEAD = 64
KVH = 5
INNER = 3200
NST = 16
KCONV = 4
DTR = 100
EPSILON = 1e-05
NEGATIVE = -1e30
CHUNK = 16
LOG2E = math.log2(math.e)
LN2 = math.log(2.0)

BF = jnp.bfloat16
F32 = jnp.float32
NT = (((1,), (1,)), ((), ()))
TN = (((0,), (0,)), ((), ()))
GIANT = 60 * 1024 * 1024
MESH = pl.DeviceIdType.MESH


def ntdot(a, b):
    return lax.dot_general(a, b, NT, preferred_element_type=F32)


def tndot(a, b):
    return lax.dot_general(a, b, TN, preferred_element_type=F32)


def dot(a, b):
    return jnp.dot(a, b, preferred_element_type=F32)


def silu_grad(values):
    logistic = jax.nn.sigmoid(values)
    return logistic * (1.0 + values * (1.0 - logistic))


def chunk_masks():
    spread = NST * CHUNK
    row = lax.broadcasted_iota(jnp.int32, (CHUNK, spread), 0)
    col = lax.broadcasted_iota(jnp.int32, (CHUNK, spread), 1)
    own = (col // NST == row).astype(F32)
    tile = (col % NST == row).astype(BF)
    return own, tile


def turn_chunks(proj, bt_ref, ct_ref):
    turned = jnp.swapaxes(proj[:, : 8 * NST], 0, 1)
    for k in range(proj.shape[0] // CHUNK):
        at = slice(k * CHUNK, (k + 1) * CHUNK)
        bt_ref[k] = turned[:NST, at]
        if ct_ref is not None:
            ct_ref[k] = turned[NST : 2 * NST, at]


def scan_fwd_kernel(proj_ref, mix_ref, rows_ref, wz_ref, wdt_ref, dtb_ref, rate_ref, skip_ref,
                    core_ref, z_ref, sq_ref, start_ref, h_ref, dt_ref, u_ref, wide_ref, hs_ref, bt_ref):
    length, cols = mix_ref.shape[2:]
    own, tile = chunk_masks()

    @pl.when(pl.program_id(1) == 0)
    def _():
        for ref in (h_ref, dt_ref, u_ref, wide_ref):
            ref[...] = jnp.zeros_like(ref)
        wide_ref[:, :cols] = rate_ref[...] * LOG2E

    start_ref[0, 0] = h_ref[:, :cols]
    proj = proj_ref[0, 0].astype(F32)
    turn_chunks(proj, bt_ref, None)
    pre = dot(proj[:, 2 * NST :].astype(BF), wdt_ref[...]) + dtb_ref[...]
    dt = jax.nn.softplus(pre)
    dt_ref[:, :cols] = dt
    u_ref[:, :cols] = dt * mix_ref[0, 0]
    rate = wide_ref[...]
    spread = NST * CHUNK

    def chunk(k, h):
        base = pl.multiple_of(k * CHUNK, CHUNK)
        bt = bt_ref[k]
        for t in range(CHUNK):
            a = jnp.exp2(dt_ref[pl.ds(base + t, 1), :] * rate)
            h = a * h + bt[:, t : t + 1] * u_ref[pl.ds(base + t, 1), :]
            hs_ref[pl.ds(pl.multiple_of((base + t) * NST, NST), NST), :] = h.astype(BF)
        return h

    h_ref[...] = lax.fori_loop(0, length // CHUNK, chunk, h_ref[...])
    z = dot(rows_ref[0, 0], wz_ref[...])
    z_ref[0, 0] = z
    crep = dot(proj[:, NST : 2 * NST].astype(BF), tile)
    for k in range(length // CHUNK):
        at = slice(k * CHUNK, (k + 1) * CHUNK)
        cb = (crep[at] * own).astype(BF)
        core_ref[0, 0, at, :] = (
            dot(cb, hs_ref[k * spread : (k + 1) * spread])[:, :cols] + skip_ref[...] * mix_ref[0, 0, at, :]
        )
    gated = core_ref[0, 0] * (z * jax.nn.sigmoid(z))
    sq_ref[0, 0] = jnp.sum(gated * gated, axis=1, keepdims=True)


def scan_forward(proj, mix, rows, wz, wdt, dtb, rate, skip):
    n, seqs, length, cols = mix.shape
    wide = -(-cols // 128) * 128
    big = lambda w: pl.BlockSpec((1, 1, length, w), lambda s, i: (i, s, 0, 0))
    whole = lambda a: pl.BlockSpec(a.shape, lambda s, i: (0, 0))
    shape = lambda w: jax.ShapeDtypeStruct((n, seqs, length, w), F32)
    return pl.pallas_call(
        scan_fwd_kernel,
        grid=(seqs, n),
        in_specs=[big(proj.shape[3]), big(cols), big(rows.shape[3])] + [whole(a) for a in (wz, wdt, dtb, rate, skip)],
        out_specs=[big(cols), big(cols), big(1), pl.BlockSpec((1, 1, NST, cols), lambda s, i: (i, s, 0, 0))],
        out_shape=[shape(cols), shape(cols), shape(1), jax.ShapeDtypeStruct((n, seqs, NST, cols), F32)],
        scratch_shapes=[
            pltpu.VMEM((NST, wide), F32),
            pltpu.VMEM((length, wide), F32),
            pltpu.VMEM((length, wide), F32),
            pltpu.VMEM((NST, wide), F32),
            pltpu.VMEM((NST * length, wide), BF),
            pltpu.VMEM((length // CHUNK, NST, CHUNK), F32),
        ],
        compiler_params=pltpu.CompilerParams(vmem_limit_bytes=GIANT),
    )(proj, mix, rows, wz, wdt, dtb, rate, skip)


def scan_bwd_kernel(len_ref, proj_ref, mix_ref, d_ref, core_ref, z_ref, stat_ref, start_ref, wdt_ref, dtb_ref, rate_ref, skip_ref,
                    gain_ref, gpre_ref, gmix_ref, gz_ref, gb_ref, gc_ref, grate_ref, sums_ref,
                    carry_ref, dt_ref, u_ref, gy_ref, wide_ref, hs_ref, gs_ref, q_ref, bt_ref, ct_ref):
    length, cols = mix_ref.shape[2:]
    own, tile = chunk_masks()
    spread = NST * CHUNK
    half = NST // 2
    folded = (lax.broadcasted_iota(jnp.int32, (2 * CHUNK, spread), 1) // half
              == lax.broadcasted_iota(jnp.int32, (2 * CHUNK, spread), 0)).astype(BF)

    @pl.when(pl.program_id(1) == 0)
    def _():
        carry_ref[...] = jnp.zeros_like(carry_ref)

    @pl.when((pl.program_id(1) == 0) & (pl.program_id(0) == 0))
    def _():
        grate_ref[...] = jnp.zeros_like(grate_ref)
        sums_ref[...] = jnp.zeros_like(sums_ref)
        for ref in (dt_ref, u_ref, gy_ref, wide_ref):
            ref[...] = jnp.zeros_like(ref)
        wide_ref[0:NST, :cols] = rate_ref[...] * LOG2E

    filled = (pl.num_programs(1) - 1 - pl.program_id(1)) * length < len_ref[pl.program_id(0)]

    @pl.when(jnp.logical_not(filled))
    def _():
        for ref in (gpre_ref, gmix_ref, gz_ref, gb_ref, gc_ref):
            ref[...] = jnp.zeros_like(ref)

    @pl.when(filled)
    def _():
        scale, shift = stat_ref[0, 0][:, 2:3], stat_ref[0, 0][:, 3:4]
        d, core, z = d_ref[0, 0], core_ref[0, 0], z_ref[0, 0]
        logistic = jax.nn.sigmoid(z)
        gated = core * (z * logistic)
        grad_gated = scale * (d * gain_ref[...] - gated * shift)
        gy_ref[:, :cols] = grad_gated * (z * logistic)
        gz_ref[0, 0] = (grad_gated * core * (logistic * (1.0 + z * (1.0 - logistic)))).astype(BF)
        sums_ref[0:1] += jnp.sum(d * gated * scale, axis=0, keepdims=True)
        sums_ref[1:2] += jnp.sum(gy_ref[:, :cols] * mix_ref[0, 0], axis=0, keepdims=True)
        proj = proj_ref[0, 0].astype(F32)
        turn_chunks(proj, bt_ref, ct_ref)
        pre = dot(proj[:, 2 * NST :].astype(BF), wdt_ref[...]) + dtb_ref[...]
        dt = jax.nn.softplus(pre)
        dt_ref[:, :cols] = dt
        u_ref[:, :cols] = dt * mix_ref[0, 0]
        wide_ref[NST:, :cols] = start_ref[0, 0]
        rate = wide_ref[0:NST]
        hs_ref[0:NST] = wide_ref[NST:].astype(BF)

        def ahead(k, h):
            base = pl.multiple_of(k * CHUNK, CHUNK)
            bt = bt_ref[k]
            for t in range(CHUNK):
                a = jnp.exp2(dt_ref[pl.ds(base + t, 1), :] * rate)
                h = a * h + bt[:, t : t + 1] * u_ref[pl.ds(base + t, 1), :]
                hs_ref[pl.ds(pl.multiple_of((base + t + 1) * NST, NST), NST), :] = h.astype(BF)
            return h

        lax.fori_loop(0, length // CHUNK, ahead, wide_ref[NST:])

        def back(r, state):
            carry, grate = state
            k = length // CHUNK - 1 - r
            base = pl.multiple_of(k * CHUNK, CHUNK)
            ct = ct_ref[k]
            qr_late = None
            for t in reversed(range(CHUNK)):
                at = pl.ds(pl.multiple_of((base + t) * NST, NST), NST)
                dt_row = dt_ref[pl.ds(base + t, 1), :]
                a = jnp.exp2(dt_row * rate)
                g = ct[:, t : t + 1] * gy_ref[pl.ds(base + t, 1), :] + carry
                carry = a * g
                q = carry * hs_ref[at, :].astype(F32)
                grate = grate + q * dt_row
                gs_ref[at, :] = g.astype(BF)
                qr = q * rate
                qr = qr[:half] + qr[half:]
                if t % 2:
                    qr_late = qr
                else:
                    both = jnp.concatenate([qr, qr_late], axis=0).astype(BF)
                    q_ref[pl.ds(pl.multiple_of((base + t) * half, NST), NST), :] = both
            return carry, grate

        carry, grate = lax.fori_loop(
            0, length // CHUNK, back, (carry_ref[...], jnp.zeros(carry_ref.shape, F32))
        )
        carry_ref[...] = carry
        grate_ref[...] += grate[:, :cols]
        brep = dot(proj[:, :NST].astype(BF), tile)
        gy_low = gy_ref[...].astype(BF)
        u_low = u_ref[...].astype(BF)
        gcs, gbs = [], []
        for pair in range(length // CHUNK // 2):
            gdts = dot(folded, q_ref[pair * spread : (pair + 1) * spread]) * LN2
            for k in (2 * pair, 2 * pair + 1):
                rows = slice(k * CHUNK, (k + 1) * CHUNK)
                deep = slice(k * spread, (k + 1) * spread)
                mix, dt_now, gy = mix_ref[0, 0, rows, :], dt_ref[rows, :cols], gy_ref[rows, :cols]
                gs = gs_ref[deep]
                gu = dot((brep[rows] * own).astype(BF), gs)[:, :cols]
                gdt = gdts[(k % 2) * CHUNK : (k % 2 + 1) * CHUNK, :cols] + gu * mix
                gpre = gdt * jax.nn.sigmoid(pre[rows])
                gpre_ref[0, 0, rows, :] = gpre.astype(BF)
                sums_ref[2:3] += jnp.sum(gpre, axis=0, keepdims=True)
                gmix_ref[0, 0, rows, :] = gu * dt_now + skip_ref[...] * gy
                hs = hs_ref[k * spread + NST : (k + 1) * spread + NST]
                gcs.append((ntdot(gy_low[rows], hs) * own).astype(BF))
                gbs.append((ntdot(u_low[rows], gs) * own).astype(BF))
        gc_ref[0, 0] = ntdot(jnp.concatenate(gcs, axis=0), tile)
        gb_ref[0, 0] = ntdot(jnp.concatenate(gbs, axis=0), tile)


def scan_backward(lengths, proj, mix, d, core, z, stats, start, wdt, dtb, rate, skip, gain):
    n, seqs, length, cols = mix.shape
    wide = -(-cols // 128) * 128
    at = lambda s, i: (n - 1 - i, s, 0, 0)
    big = lambda w: pl.BlockSpec((1, 1, length, w), at)
    whole = lambda a: pl.BlockSpec(a.shape, lambda s, i: (0, 0))
    shape = lambda w, t: jax.ShapeDtypeStruct((n, seqs, length, w), t)
    return pl.pallas_call(
        scan_bwd_kernel,
        grid=(seqs, n),
        in_specs=[pl.BlockSpec(memory_space=pltpu.SMEM),
                  big(proj.shape[3]), big(cols), big(cols), big(cols), big(cols), big(stats.shape[3]),
                  pl.BlockSpec((1, 1, NST, cols), at)] + [whole(a) for a in (wdt, dtb, rate, skip, gain)],
        out_specs=[big(cols), big(cols), big(cols), big(NST), big(NST), whole(rate),
                   pl.BlockSpec((8, cols), lambda s, i: (0, 0))],
        out_shape=[
            shape(cols, BF), shape(cols, F32), shape(cols, BF), shape(NST, F32), shape(NST, F32),
            jax.ShapeDtypeStruct((NST, cols), F32),
            jax.ShapeDtypeStruct((8, cols), F32),
        ],
        scratch_shapes=[
            pltpu.VMEM((NST, wide), F32),
            pltpu.VMEM((length, wide), F32),
            pltpu.VMEM((length, wide), F32),
            pltpu.VMEM((length, wide), F32),
            pltpu.VMEM((2 * NST, wide), F32),
            pltpu.VMEM((length * NST + NST, wide), BF),
            pltpu.VMEM((length * NST, wide), BF),
            pltpu.VMEM((length * NST // 2, wide), BF),
            pltpu.VMEM((length // CHUNK, NST, CHUNK), F32),
            pltpu.VMEM((length // CHUNK, NST, CHUNK), F32),
        ],
        compiler_params=pltpu.CompilerParams(vmem_limit_bytes=GIANT),
    )(lengths, proj, mix, d, core, z, stats, start, wdt, dtb, rate, skip, gain)


def pick(ref, blocks, slots, slot):
    value = ref[0:blocks, 0, :, 0:HEAD].reshape(-1, HEAD)
    for other in range(1, slots):
        here = ref[0:blocks, 0, :, other * HEAD : (other + 1) * HEAD].reshape(-1, HEAD)
        value = jnp.where(slot == other, here, value)
    return value


def masked_scores(queries, keys, first, length):
    scores = ntdot(queries, keys)
    rows = first + lax.broadcasted_iota(jnp.int32, (scores.shape[0], 1), 0)
    bound = jnp.minimum(rows, length - 1)
    return jnp.where(lax.broadcasted_iota(jnp.int32, scores.shape, 1) <= bound, scores, NEGATIVE)


def attn_fwd_kernel(seq, slot_ref, len_ref, rows_ref, w_ref, *refs):
    out_ref, lse_ref, q_ref, k_ref, v_ref = refs[-5:]
    n, _, length, width = q_ref.shape
    heads, slots = width // HEAD, k_ref.shape[3] // HEAD
    group = 2
    seq_length = len_ref[seq]
    kv_width = k_ref.shape[3]

    def project(i, _):
        y = dot(rows_ref[i, 0], w_ref[...]).astype(BF)
        q_ref[i, 0] = y[:, :width]
        k_ref[i, 0] = y[:, width : width + kv_width]
        v_ref[i, 0] = y[:, width + kv_width :]
        return 0

    lax.fori_loop(0, n, project, 0)
    for i in range(n // group):
        at = slice(i * group, (i + 1) * group)
        for j in range(heads):
            lanes = slice(j * HEAD, (j + 1) * HEAD)
            blocks = (i + 1) * group
            queries = q_ref[at, 0, :, lanes].reshape(group * length, HEAD) * HEAD ** (-0.5)
            keys = pick(k_ref, blocks, slots, slot_ref[j])
            values = pick(v_ref, blocks, slots, slot_ref[j])
            scores = masked_scores(queries.astype(BF), keys, i * group * length, seq_length)
            top = jnp.max(scores, axis=1, keepdims=True)
            probs = jnp.exp(scores - top)
            total = jnp.sum(probs, axis=1, keepdims=True)
            mixed = dot(probs.astype(BF), values) * (slot_ref[heads + j].astype(F32) / total)
            out_ref[at, 0, :, lanes] = mixed.reshape(group, length, HEAD)
            lse_ref[at, 0, :, j : j + 1] = (top + jnp.log(total)).reshape(group, length, 1)


def attn_forward(seq, slot, lengths, rows, w, width, before=()):
    n, seqs, length, depth = rows.shape
    kv_width = (w.shape[1] - width) // 2
    big = lambda w: pl.BlockSpec((n, 1, length, w), lambda s: (0, seq, 0, 0))
    smem = pl.BlockSpec(memory_space=pltpu.SMEM)
    outs = ((width, F32), (width // HEAD, F32), (width, BF), (kv_width, BF), (kv_width, BF))
    return pl.pallas_call(
        functools.partial(attn_fwd_kernel, seq),
        grid=(1,),
        in_specs=[smem, smem, big(depth), pl.BlockSpec(w.shape, lambda s: (0, 0))]
        + [pl.BlockSpec(memory_space=pl.ANY)] * len(before),
        out_specs=[big(c) for c, _ in outs],
        out_shape=[jax.ShapeDtypeStruct((n, seqs, length, c), t) for c, t in outs],
        input_output_aliases={4 + i: i for i in range(len(before))},
        compiler_params=pltpu.CompilerParams(vmem_limit_bytes=GIANT),
        cost_estimate=pl.CostEstimate(
            flops=2 * n * length * w.shape[1] * depth + 16 * (n * length) ** 2 * width,
            bytes_accessed=2 * n * length * (depth + 6 * width),
            transcendentals=(n * length) ** 2 * (width // HEAD),
        ),
    )(slot, lengths, rows, w, *before)


def attn_bwd_kernel(slot_ref, len_ref, q_ref, k_ref, v_ref, d_ref, att_ref, lse_ref, stat_ref, gain_ref,
                    gq_ref, gk_ref, gv_ref, sums_ref, gk_acc, gv_acc, gh_ref):
    n, _, length, width = q_ref.shape
    heads, slots = width // HEAD, k_ref.shape[3] // HEAD
    group = 2
    seq_length = len_ref[pl.program_id(0)]
    @pl.when(pl.program_id(0) == 0)
    def _():
        sums_ref[...] = jnp.zeros_like(sums_ref)

    for i in range(n):
        scale, shift = stat_ref[i, 0][:, 0:1], stat_ref[i, 0][:, 1:2]
        d, attended = d_ref[i, 0], att_ref[i, 0]
        gh_ref[i] = (scale * (d * gain_ref[...] - attended * shift)).astype(BF)
        sums_ref[0:1] += jnp.sum(d * attended * scale, axis=0, keepdims=True)
    gk_acc[...] = jnp.zeros_like(gk_acc)
    gv_acc[...] = jnp.zeros_like(gv_acc)
    def block(i):
        at = slice(i * group, (i + 1) * group)
        blocks = (i + 1) * group
        for j in range(heads):
            lanes = slice(j * HEAD, (j + 1) * HEAD)
            slot = slot_ref[j]
            queries = q_ref[at, 0, :, lanes].reshape(group * length, HEAD) * HEAD ** (-0.5)
            queries = queries.astype(BF)
            keys = pick(k_ref, blocks, slots, slot)
            values = pick(v_ref, blocks, slots, slot)
            grad = gh_ref[at, :, lanes].reshape(group * length, HEAD)
            attended = att_ref[at, 0, :, lanes].reshape(group * length, HEAD)
            delta = jnp.sum(grad.astype(F32) * attended, axis=1, keepdims=True)
            lse = lse_ref[at, 0, :, j : j + 1].reshape(group * length, 1)
            scores = masked_scores(queries, keys, i * group * length, seq_length)
            probs = jnp.exp(scores - lse)
            grad_scores = (probs * (ntdot(grad, values) - delta)).astype(BF)
            gq = dot(grad_scores, keys) * HEAD ** (-0.5)
            gq_ref[at, 0, :, lanes] = gq.astype(BF).reshape(group, length, HEAD)
            rows = slice(0, blocks * length)
            gk_acc[slot, rows] += tndot(grad_scores, queries)
            gv_acc[slot, rows] += tndot(probs.astype(BF), grad)

    for i in range(n // group):
        pl.when(i * group * length < seq_length)(functools.partial(block, i))

        @pl.when(i * group * length >= seq_length)
        def _():
            gq_ref[i * group : (i + 1) * group] = jnp.zeros((group,) + gq_ref.shape[1:], BF)

    for other in range(slots):
        lanes = slice(other * HEAD, (other + 1) * HEAD)
        gk_ref[:, 0, :, lanes] = gk_acc[other].astype(BF).reshape(n, length, HEAD)
        gv_ref[:, 0, :, lanes] = gv_acc[other].astype(BF).reshape(n, length, HEAD)


def attn_backward(slot, lengths, q, k, v, d, att, lse, stats, gain):
    n, seqs, length, width = q.shape
    big = lambda w: pl.BlockSpec((n, 1, length, w), lambda s: (0, s, 0, 0))
    whole = lambda r: pl.BlockSpec((r, width), lambda s: (0, 0))
    smem = pl.BlockSpec(memory_space=pltpu.SMEM)
    kw = k.shape[3]
    return pl.pallas_call(
        attn_bwd_kernel,
        grid=(seqs,),
        in_specs=[smem, smem, big(width), big(kw), big(kw), big(width), big(width), big(width // HEAD),
                  big(stats.shape[3]), whole(1)],
        out_specs=[big(width), big(kw), big(kw), whole(8)],
        out_shape=[jax.ShapeDtypeStruct(x.shape, BF) for x in (q, k, v)]
        + [jax.ShapeDtypeStruct((8, width), F32)],
        scratch_shapes=[pltpu.VMEM((kw // HEAD, n * length, HEAD), F32)] * 2 + [pltpu.VMEM((n, length, width), BF)],
        compiler_params=pltpu.CompilerParams(vmem_limit_bytes=GIANT),
    )(slot, lengths, q, k, v, d, att, lse, stats, gain)


def signal_fwd_kernel(rows_ref, wx_ref, taps_ref, bias_ref, xp_ref, x_ref, pre_ref, mix_ref, low_ref, part_ref, xs_ref):
    length = rows_ref.shape[2]

    @pl.when(pl.program_id(1) == 0)
    def _():
        xs_ref[0:8] = jnp.zeros((8, xs_ref.shape[1]), F32)

    x = dot(rows_ref[0, 0], wx_ref[...]).astype(BF)
    x_ref[0, 0] = x
    xs_ref[8:] = x.astype(F32)
    first = 8 - (KCONV - 1)
    pre = bias_ref[...]
    for o in range(KCONV):
        pre = pre + taps_ref[o : o + 1] * xs_ref[first + o : first + o + length]
    xs_ref[0:8] = xs_ref[length : length + 8]
    pre_ref[0, 0] = pre
    mix = pre * jax.nn.sigmoid(pre)
    mix_ref[0, 0] = mix
    low_ref[0, 0] = mix.astype(BF)
    part_ref[0, 0] = ntdot(mix.astype(BF), xp_ref[...]).astype(BF)


def signal_forward(rows, wx, taps, bias, xp):
    n, seqs, length, width = rows.shape
    cols = wx.shape[1]
    big = lambda w: pl.BlockSpec((1, 1, length, w), lambda s, i: (i, s, 0, 0))
    whole = lambda a: pl.BlockSpec(a.shape, lambda s, i: (0, 0))
    shape = lambda w, t: jax.ShapeDtypeStruct((n, seqs, length, w), t)
    return pl.pallas_call(
        signal_fwd_kernel,
        grid=(seqs, n),
        in_specs=[big(width), whole(wx), whole(taps), whole(bias), whole(xp)],
        out_specs=[big(cols)] * 4 + [big(xp.shape[0])],
        out_shape=[shape(cols, BF), shape(cols, F32), shape(cols, F32), shape(cols, BF), shape(xp.shape[0], BF)],
        scratch_shapes=[pltpu.VMEM((length + 8, cols), F32)],
        compiler_params=pltpu.CompilerParams(vmem_limit_bytes=GIANT),
    )(rows, wx, taps, bias, xp)


def signal_bwd_kernel(gmix_ref, gproj_ref, xp_ref, pre_ref, x_ref, last_ref, taps_ref, gx_ref, sums_ref, gs_ref, xs_ref):
    length = gmix_ref.shape[2]
    edge = KCONV - 1
    i = pl.program_id(1)

    @pl.when((i == 0) & (pl.program_id(0) == 0))
    def _():
        sums_ref[...] = jnp.zeros_like(sums_ref)

    @pl.when(i == 0)
    def _():
        gs_ref[length:] = jnp.zeros((8, gs_ref.shape[1]), F32)

    grad = gmix_ref[0, 0] + dot(gproj_ref[0, 0], xp_ref[...])
    grad = grad * silu_grad(pre_ref[0, 0])
    gs_ref[:length] = grad
    first_block = (i == pl.num_programs(1) - 1).astype(F32)
    xs_ref[0:16] = last_ref[0, 0].astype(F32) * (1.0 - first_block)
    xs_ref[16:] = x_ref[0, 0].astype(F32)
    total = None
    for o in range(KCONV):
        term = taps_ref[o : o + 1] * gs_ref[edge - o : edge - o + length]
        total = term if total is None else total + term
        at = 16 - edge + o
        sums_ref[o : o + 1] += jnp.sum(grad * xs_ref[at : at + length], axis=0, keepdims=True)
    sums_ref[KCONV : KCONV + 1] += jnp.sum(grad, axis=0, keepdims=True)
    gx_ref[0, 0] = total.astype(BF)
    gs_ref[length:] = gs_ref[0:8]


def signal_backward(gmix, gproj, xp, pre, x, taps):
    n, seqs, length, cols = gmix.shape
    at = lambda s, i: (n - 1 - i, s, 0, 0)
    big = lambda w: pl.BlockSpec((1, 1, length, w), at)
    whole = lambda a: pl.BlockSpec(a.shape, lambda s, i: (0, 0))
    before = lambda s, i: (jnp.maximum(n - 2 - i, 0), s, length // 16 - 1, 0)
    return pl.pallas_call(
        signal_bwd_kernel,
        grid=(seqs, n),
        in_specs=[big(cols), big(xp.shape[0]), whole(xp), big(cols), big(cols),
                  pl.BlockSpec((1, 1, 16, cols), before), whole(taps)],
        out_specs=[big(cols), pl.BlockSpec((8, cols), lambda s, i: (0, 0))],
        out_shape=[jax.ShapeDtypeStruct(gmix.shape, BF), jax.ShapeDtypeStruct((8, cols), F32)],
        scratch_shapes=[pltpu.VMEM((length + 8, cols), F32), pltpu.VMEM((length + 16, cols), F32)],
        compiler_params=pltpu.CompilerParams(vmem_limit_bytes=GIANT),
    )(gmix, gproj, xp, pre, x, x, taps)


def norm_kernel(sq_ref, att_ref, again_ref, core_ref, z_ref, sgain_ref, attn_ref, ssm_ref):
    sq = sq_ref[0]
    r_attn = lax.rsqrt(sq[:, 0:1] / (HEADS * HEAD) + EPSILON)
    r_ssm = lax.rsqrt(sq[:, 1:2] / INNER + EPSILON)
    attn_ref[0] = (att_ref[0] * r_attn * again_ref[...]).astype(BF)
    z = z_ref[0]
    ssm_ref[0] = (core_ref[0] * (z * jax.nn.sigmoid(z)) * r_ssm * sgain_ref[...]).astype(BF)


def norm_both(squares, attended, attn_gain, core, z, ssm_gain):
    n, rows, _ = squares.shape
    block = lambda c: pl.BlockSpec((1, rows, c), lambda i: (i, 0, 0))
    whole = lambda a: pl.BlockSpec(a.shape, lambda i: (0, 0))
    aw, sw = attended.shape[2], core.shape[2]
    return pl.pallas_call(
        norm_kernel,
        grid=(n,),
        in_specs=[block(2), block(aw), whole(attn_gain), block(sw), block(sw), whole(ssm_gain)],
        out_specs=[block(aw), block(sw)],
        out_shape=[jax.ShapeDtypeStruct((n, rows, w), BF) for w in (aw, sw)],
        compiler_params=pltpu.CompilerParams(vmem_limit_bytes=GIANT),
    )(squares, attended, attn_gain, core, z, ssm_gain)


def ffn_bwd_kernel(u_ref, down_ref, gate_ref, up_ref, ggate_ref, gup_ref):
    grad = ntdot(u_ref[0], down_ref[...])
    gate, up = gate_ref[0].astype(F32), up_ref[0].astype(F32)
    logistic = jax.nn.sigmoid(gate)
    ggate_ref[0] = (grad * up * (logistic * (1.0 + gate * (1.0 - logistic)))).astype(BF)
    gup_ref[0] = (grad * (gate * logistic)).astype(BF)


def ffn_backward(upstream, w_down, gate, up):
    n, rows, hidden = gate.shape
    block = lambda c: pl.BlockSpec((1, rows, c), lambda i: (i, 0, 0))
    return pl.pallas_call(
        ffn_bwd_kernel,
        grid=(n,),
        in_specs=[block(upstream.shape[2]), pl.BlockSpec(w_down.shape, lambda i: (0, 0)), block(hidden), block(hidden)],
        out_specs=[block(hidden)] * 2,
        out_shape=[jax.ShapeDtypeStruct(gate.shape, BF)] * 2,
        compiler_params=pltpu.CompilerParams(vmem_limit_bytes=GIANT),
    )(upstream, w_down, gate, up)


def greet(peers, axis="seq"):
    barrier = pltpu.get_barrier_semaphore()
    for peer in peers:
        pl.semaphore_signal(barrier, inc=1, device_id={axis: peer}, device_id_type=MESH)
    pl.semaphore_wait(barrier, len(peers))

def send(src, dst, send_sem, recv_sem, peer, axis="seq"):
    return pltpu.make_async_remote_copy(src_ref=src, dst_ref=dst, send_sem=send_sem, recv_sem=recv_sem,
        device_id={axis: peer}, device_id_type=MESH)

def ag_parts(n, x_ref, o_ref, local_sem, far_send, far_recv, near_send, near_recv):
    me = lax.axis_index("seq")
    core, chip, chips = me % 2, me // 2, n // 2
    sib = me + 1 - 2 * core
    far = [((chip + d) % chips) * 2 + core for d in range(1, chips)]
    mine = pltpu.make_async_copy(x_ref, o_ref.at[me], local_sem)
    out = [
        send(x_ref, o_ref.at[me], far_send.at[d], far_recv.at[d], far[d - 1]) for d in range(1, chips)
    ]
    near = [send(x_ref, o_ref.at[me], near_send.at[0], near_recv.at[0], sib)]

    def begin():
        for c in [mine] + out + near:
            c.start()

    def finish():
        for d in range(1, chips):
            out[d - 1].wait_recv()
            block = ((chip + chips - d) % chips) * 2 + core
            c = send(o_ref.at[block], o_ref.at[block], near_send.at[d], near_recv.at[d], sib)
            c.start()
            near.append(c)
        mine.wait()
        for c in near:
            c.wait()
        for c in out:
            c.wait_send()

    return begin, finish


def ag_kernel(n, x_ref, o_ref, *sems):
    me = lax.axis_index("seq")
    core, chip, chips = me % 2, me // 2, n // 2
    greet([me + 1 - 2 * core] + [((chip + d) % chips) * 2 + core for d in range(1, chips)])
    begin, finish = ag_parts(n, x_ref, o_ref, *sems)
    begin()
    finish()


def all_gather_any(x, n, cid):
    chips = n // 2
    return pl.pallas_call(functools.partial(ag_kernel, n),
        out_shape=jax.ShapeDtypeStruct((n,) + x.shape, x.dtype),
        in_specs=[pl.BlockSpec(memory_space=pl.ANY)],
        out_specs=pl.BlockSpec(memory_space=pl.ANY),
        scratch_shapes=[pltpu.SemaphoreType.DMA] + [pltpu.SemaphoreType.DMA((chips,))] * 4,
        compiler_params=pltpu.CompilerParams(collective_id=cid, has_side_effects=True),
    )(x)

def rs_kernel(n, p_ref, after_ref, o_ref, own, near, sums, got, local_sem, near_send, near_recv, far_send, far_recv):
    me = lax.axis_index("seq")
    core, chip, chips = me % 2, me // 2, n // 2
    sib = me + 1 - 2 * core
    step = lambda d: (chip + d) % chips
    far = [step(d) * 2 + core for d in range(1, chips)]
    greet([sib] + far)
    order = list(range(1, chips)) + [0]
    loads, nears, fars = {}, {}, {}
    for d in order:
        nears[d] = send(p_ref.at[step(d) * 2 + 1 - core], near.at[d], near_send.at[d], near_recv.at[d], sib)
        nears[d].start()
        loads[d] = pltpu.make_async_copy(p_ref.at[step(d) * 2 + core], own.at[d], local_sem.at[d])
        loads[d].start()
    rows = own.shape[1]
    slab = 16
    def each(body):
        def run(i, _):
            body(pl.ds(pl.multiple_of(i * slab, slab), slab))
            return 0
        lax.fori_loop(0, rows // slab, run, 0, unroll=2)
    for d in order:
        loads[d].wait()
        nears[d].wait_recv()
        if d:
            def add(at):
                sums[d - 1, at] = (own[d, at].astype(F32) + near[d, at].astype(F32)).astype(BF)
            each(add)
            fars[d] = send(sums.at[d - 1], got.at[d - 1], far_send.at[d - 1], far_recv.at[d - 1], far[d - 1])
            fars[d].start()
        else:
            def add(at):
                o_ref[at] = own[0, at].astype(F32) + near[0, at].astype(F32)
            each(add)
    for d in range(1, chips):
        fars[d].wait_recv()
        def add(at):
            o_ref[at] = o_ref[at] + got[d - 1, at].astype(F32)
        each(add)
    for d in order:
        nears[d].wait_send()
        if d: fars[d].wait_send()

def reduce_scatter_any(p, after, n, cid):
    chips = n // 2
    blk = p.shape[1:]
    return pl.pallas_call(functools.partial(rs_kernel, n),
        out_shape=jax.ShapeDtypeStruct(blk, F32),
        in_specs=[pl.BlockSpec(memory_space=pl.ANY)] * 2,
        out_specs=pl.BlockSpec(memory_space=pltpu.VMEM),
        scratch_shapes=[pltpu.VMEM((chips,) + blk, p.dtype), pltpu.VMEM((chips,) + blk, p.dtype),
            pltpu.VMEM((chips-1,) + blk, p.dtype), pltpu.VMEM((chips-1,) + blk, p.dtype),
            pltpu.SemaphoreType.DMA((chips,)), pltpu.SemaphoreType.DMA((chips,)), pltpu.SemaphoreType.DMA((chips,)),
            pltpu.SemaphoreType.DMA((chips-1,)), pltpu.SemaphoreType.DMA((chips-1,))],
        compiler_params=pltpu.CompilerParams(collective_id=cid, has_side_effects=True, vmem_limit_bytes=GIANT),
    )(p, after)

def stat_kernel(n, axis, x_ref, o_ref, got, send_sem, recv_sem):
    me = lax.axis_index(axis)
    peers = [(me + d) % n for d in range(1, n)]
    greet(peers, axis)
    copies = []
    for d in range(1, n):
        c = send(x_ref, got.at[d - 1], send_sem.at[d - 1], recv_sem.at[d - 1], peers[d - 1], axis)
        c.start()
        copies.append(c)
    total = x_ref[...]
    for d in range(1, n):
        copies[d - 1].wait_recv()
        total = total + got[d - 1]
    o_ref[...] = total
    for c in copies:
        c.wait_send()


def small_sum(x, n, cid, axis="seq"):
    return pl.pallas_call(
        functools.partial(stat_kernel, n, axis),
        out_shape=jax.ShapeDtypeStruct(x.shape, F32),
        in_specs=[pl.BlockSpec(memory_space=pltpu.VMEM)],
        out_specs=pl.BlockSpec(memory_space=pltpu.VMEM),
        scratch_shapes=[pltpu.VMEM((n - 1,) + x.shape, F32)] + [pltpu.SemaphoreType.DMA((n - 1,))] * 2,
        compiler_params=pltpu.CompilerParams(collective_id=cid, has_side_effects=True, vmem_limit_bytes=GIANT),
    )(x)


def square(me):
    core, x, y = me % 2, (me // 2) % 2, me // 4
    seat = lambda yy, xx, cc: (yy * 2 + xx) * 2 + cc
    return core, (seat(y, x, 1 - core), seat(y, 1 - x, core), seat(1 - y, x, core), seat(1 - y, 1 - x, core))

def ag4_parts(n, x_ref, o_ref, local_sem, far_send, far_recv, near_send, near_recv):
    me = lax.axis_index("seq")
    core, (sib, east, north, across) = square(me)
    half = x_ref.shape[0] // 2
    cut = (pl.ds(0, half), pl.ds(half, half))
    mine = pltpu.make_async_copy(x_ref, o_ref.at[me], local_sem)
    far, near = {}, []
    for slot, h, peer in ((0, 0, east), (2, 1, north), (1, 1, east), (3, 0, north)):
        far[slot] = send(x_ref.at[cut[h]], o_ref.at[me, cut[h]], far_send.at[slot], far_recv.at[slot], peer)
    near.append(send(x_ref, o_ref.at[me], near_send.at[6], near_recv.at[6], sib))

    def begin():
        mine.start()
        for slot in (0, 2, 1, 3):
            far[slot].start()
        near[0].start()

    def pass_on(slot, block, h):
        ref = o_ref.at[block, cut[h]]
        c = send(ref, ref, near_send.at[slot], near_recv.at[slot], sib)
        c.start()
        near.append(c)

    def finish():
        for slot, block, h, relay, to in (
            (0, east, 0, 4, north), (2, north, 1, 5, east), (1, east, 1, None, None), (3, north, 0, None, None)
        ):
            far[slot].wait_recv()
            if relay is not None:
                ref = o_ref.at[block, cut[h]]
                far[relay] = send(ref, ref, far_send.at[relay], far_recv.at[relay], to)
                far[relay].start()
            pass_on(slot, block, h)
        for slot, h in ((4, 0), (5, 1)):
            far[slot].wait_recv()
            pass_on(slot, across, h)
        mine.wait()
        for c in near:
            c.wait()
        for c in far.values():
            c.wait_send()

    return begin, finish


def ag4_kernel(x_ref, o_ref, *sems):
    core, (sib, east, north, across) = square(lax.axis_index("seq"))
    greet([sib, east, north])
    begin, finish = ag4_parts(8, x_ref, o_ref, *sems)
    begin()
    finish()


def all_gather4(x, n, cid):
    return pl.pallas_call(ag4_kernel,
        out_shape=jax.ShapeDtypeStruct((n,) + x.shape, x.dtype),
        in_specs=[pl.BlockSpec(memory_space=pl.ANY)],
        out_specs=pl.BlockSpec(memory_space=pl.ANY),
        scratch_shapes=[pltpu.SemaphoreType.DMA] + [pltpu.SemaphoreType.DMA((6,))] * 2 + [pltpu.SemaphoreType.DMA((7,))] * 2,
        compiler_params=pltpu.CompilerParams(collective_id=cid, has_side_effects=True),
    )(x)

def rs4_kernel(p_ref, after_ref, o_ref, own, near, got, local_sem, near_send, near_recv, far_send, far_recv):
    me = lax.axis_index("seq")
    core, (sib, east, north, across) = square(me)
    greet([sib, east, north])
    rows = own.shape[1]
    half = rows // 2
    cut = (pl.ds(0, half), pl.ds(half, half))
    seats = (across, east, north, me)
    loads, nears, far = [], [], {}
    for i, seat in enumerate(seats):
        other = seat + 1 - 2 * core
        c = send(p_ref.at[other], near.at[i], near_send.at[i], near_recv.at[i], sib)
        c.start(); nears.append(c)
        c = pltpu.make_async_copy(p_ref.at[seat], own.at[i], local_sem.at[i])
        c.start(); loads.append(c)
    slab = 16
    def each(first, count, body):
        def run(i, _):
            body(pl.ds(pl.multiple_of(first + i * slab, slab), slab), pl.ds(pl.multiple_of(i * slab, slab), slab))
            return 0
        lax.fori_loop(0, count // slab, run, 0, unroll=2)
    def fold(i):
        loads[i].wait(); nears[i].wait_recv()
        def add(at, _):
            own[i, at] = (own[i, at].astype(F32) + near[i, at].astype(F32)).astype(own.dtype)
        each(0, rows, add)
    def go(slot, i, h, peer):
        far[slot] = send(own.at[i, cut[h]], got.at[slot], far_send.at[slot], far_recv.at[slot], peer)
        far[slot].start()
    fold(0)
    go(0, 0, 0, east)
    go(1, 0, 1, north)
    fold(1)
    go(2, 1, 0, east)
    fold(2)
    go(3, 2, 1, north)
    def join(i, h, slot):
        far[slot].wait_recv()
        def add(at, src):
            own[i, at] = (own[i, at].astype(F32) + got[slot, src].astype(F32)).astype(own.dtype)
        each(h * half, half, add)
    join(2, 0, 0)
    go(4, 2, 0, north)
    join(1, 1, 1)
    go(5, 1, 1, east)
    loads[3].wait(); nears[3].wait_recv()
    def first(h, slot):
        far[slot].wait_recv()
        def add(at, src):
            o_ref[at] = own[3, at].astype(F32) + near[3, at].astype(F32) + got[slot, src].astype(F32)
        each(h * half, half, add)
    first(0, 2)
    first(1, 3)
    def last(h, slot):
        far[slot].wait_recv()
        def add(at, src):
            o_ref[at] = o_ref[at] + got[slot, src].astype(F32)
        each(h * half, half, add)
    last(0, 4)
    last(1, 5)
    for c in nears: c.wait_send()
    for c in far.values(): c.wait_send()

def reduce_scatter4(p, after, n, cid):
    blk = p.shape[1:]
    return pl.pallas_call(rs4_kernel,
        out_shape=jax.ShapeDtypeStruct(blk, F32),
        in_specs=[pl.BlockSpec(memory_space=pl.ANY)] * 2,
        out_specs=pl.BlockSpec(memory_space=pltpu.VMEM),
        scratch_shapes=[pltpu.VMEM((4,) + blk, p.dtype), pltpu.VMEM((4,) + blk, p.dtype),
            pltpu.VMEM((6, blk[0] // 2) + blk[1:], p.dtype)] + [pltpu.SemaphoreType.DMA((4,))] * 3 + [pltpu.SemaphoreType.DMA((6,))] * 2,
        compiler_params=pltpu.CompilerParams(collective_id=cid, has_side_effects=True, vmem_limit_bytes=GIANT),
    )(p, after)


def start_kernel(n, moves, x_ref, gain_ref, w_ref, in_ref, o_ref, c_ref, first_ref, second_ref,
                 normed_ref, cols_ref, swap_sem, swap_send, swap_recv, *sems):
    me = lax.axis_index("seq")
    others = [(me + d) % n for d in range(1, n)]
    barrier = pltpu.get_barrier_semaphore()
    for peer in others:
        pl.semaphore_signal(barrier, inc=1, device_id={"seq": peer}, device_id_type=MESH)
    x = x_ref[...].astype(F32)
    scale = lax.rsqrt(jnp.mean(x * x, axis=-1, keepdims=True) + EPSILON)
    normed_ref[...] = (x * scale * gain_ref[...]).astype(BF)
    pl.semaphore_wait(barrier, n - 1)
    gather_start, gather_end = (ag4_parts if n == 8 else ag_parts)(n, normed_ref, o_ref, *sems)
    gather_start()
    for i in range(n):
        if sum(size for _, _, size in moves[i]) < cols_ref.shape[2]:
            cols_ref[i] = jnp.zeros(cols_ref.shape[1:], BF)
        for dst, src, size in moves[i]:
            cols_ref[i, :, dst : dst + size] = w_ref[:, src : src + size]
    own = pltpu.make_async_copy(cols_ref.at[me], c_ref.at[me], swap_sem)
    own.start()
    swaps = []
    for d in range(1, n):
        peer = others[d - 1]
        c = send(cols_ref.at[peer], c_ref.at[me], swap_send.at[d - 1], swap_recv.at[d - 1], peer)
        c.start()
        swaps.append(c)
    width = first_ref.shape[2]
    for i in range(n):
        first_ref[i] = in_ref[:, i * width : (i + 1) * width]
        second_ref[i] = in_ref[:, (n + i) * width : (n + i + 1) * width]
    gather_end()
    own.wait()
    for c in swaps:
        c.wait()


def gather_and_exchange(x, gain, w, moves, width, w_in, n, cid):
    far, near = (6, 7) if n == 8 else (n // 2, n // 2)
    anywhere = pl.BlockSpec(memory_space=pl.ANY)
    vmem = pl.BlockSpec(memory_space=pltpu.VMEM)
    dma = pltpu.SemaphoreType.DMA
    cols = jax.ShapeDtypeStruct((n, w.shape[0], width), BF)
    part = jax.ShapeDtypeStruct((n, w_in.shape[0], w_in.shape[1] // (2 * n)), BF)
    return pl.pallas_call(
        functools.partial(start_kernel, n, moves),
        out_shape=[jax.ShapeDtypeStruct((n,) + x.shape, BF), cols, part, part],
        in_specs=[vmem] * 4,
        out_specs=[anywhere] * 2 + [vmem] * 2,
        scratch_shapes=[pltpu.VMEM(x.shape, BF), pltpu.VMEM(cols.shape, BF), dma, dma((n - 1,)), dma((n - 1,)),
                        dma, dma((far,)), dma((far,)), dma((near,)), dma((near,))],
        compiler_params=pltpu.CompilerParams(collective_id=cid, has_side_effects=True, vmem_limit_bytes=GIANT),
    )(x, gain[None], w, w_in)


def sum4_kernel(p_ref, after_ref, o_ref, total, low, *rest):
    rs4_kernel(p_ref, after_ref, total, *rest[:8])
    low[...] = total[...].astype(BF)
    begin, finish = ag4_parts(8, low, o_ref, *rest[8:])
    begin()
    finish()


def all_sum(p, n, cid, after=None):
    after = jnp.zeros((8, 128), F32) if after is None else after
    if n != 8:
        return all_gather(reduce_scatter(p, n, cid, after).astype(BF), n, cid + 1)
    blk = p.shape[1:]
    dma = pltpu.SemaphoreType.DMA
    return pl.pallas_call(
        sum4_kernel,
        out_shape=jax.ShapeDtypeStruct(p.shape, BF),
        in_specs=[pl.BlockSpec(memory_space=pl.ANY)] * 2,
        out_specs=pl.BlockSpec(memory_space=pl.ANY),
        scratch_shapes=[
            pltpu.VMEM(blk, F32), pltpu.VMEM(blk, BF),
            pltpu.VMEM((4,) + blk, BF), pltpu.VMEM((4,) + blk, BF), pltpu.VMEM((6, blk[0] // 2) + blk[1:], BF),
            dma((4,)), dma((4,)), dma((4,)), dma((6,)), dma((6,)),
            dma, dma((6,)), dma((6,)), dma((7,)), dma((7,)),
        ],
        compiler_params=pltpu.CompilerParams(collective_id=cid, has_side_effects=True, vmem_limit_bytes=GIANT),
    )(p, after)


def all_gather(x, n, cid):
    return (all_gather4 if n == 8 else all_gather_any)(x, n, cid)


def reduce_scatter(p, n, cid, after=None):
    after = jnp.zeros((8, 128), F32) if after is None else after
    return (reduce_scatter4 if n == 8 else reduce_scatter_any)(p, after, n, cid)


def mm_rs4_kernel(turned, seconds, firsts, *refs):
    terms = len(turned)
    count = max(seconds) + 1
    a_refs, b_refs = refs[:terms], refs[terms : terms + count]
    after_ref, o_ref, part, near, got, near_send, near_recv, far_send, far_recv = refs[terms + count :]
    me = lax.axis_index("seq")
    core, (sib, east, north, across) = square(me)
    x, y = (me // 2) % 2, me // 4
    greet([sib, east, north])
    rows = part.shape[2]
    half = rows // 2
    cut = (pl.ds(0, half), pl.ds(half, half))
    slab = 16
    own = part.at[1]

    def near_copy(i):
        return send(part.at[0, i], near.at[i], near_send.at[i], near_recv.at[i], sib)

    hops = ((0, 0, east), (0, 1, north), (1, 0, east), (2, 1, north), (2, 0, north), (1, 1, east))

    def far_copy(slot):
        i, h, peer = hops[slot]
        return send(own.at[i, cut[h]], got.at[slot], far_send.at[slot], far_recv.at[slot], peer)

    def each(first, count, body):
        def run(i, _):
            at = pl.multiple_of(i * slab, slab)
            body(pl.ds(pl.multiple_of(first + at, slab), slab), pl.ds(at, slab))
            return 0

        lax.fori_loop(0, count // slab, run, 0, unroll=2)

    def fold(i):
        near_copy(i).wait_recv()

        def add(at, _):
            own[i, at] = (own[i, at].astype(F32) + near[i, at].astype(F32)).astype(BF)

        each(0, rows, add)

    def step(s, _):
        i, mine = s // 2, s % 2
        yy, xx = (y + (i + 1) % 2) % 2, (x + 1 - i // 2) % 2
        seat = (yy * 2 + xx) * 2 + (core + 1 - mine) % 2
        total = None
        for a, t, at, first in zip(a_refs, turned, seconds, firsts):
            b = b_refs[at]
            term = ntdot(a[seat], b[...]) if t else dot(a[seat], b[first : first + a.shape[2]])
            total = term if total is None else total + term
        part[mine, i] = total.astype(BF)

        @pl.when(mine == 0)
        def _():
            near_copy(i).start()

        @pl.when(s == 2)
        def _():
            fold(0)
            far_copy(0).start()
            far_copy(1).start()

        @pl.when(s == 4)
        def _():
            fold(1)
            far_copy(2).start()

        @pl.when(s == 6)
        def _():
            fold(2)
            far_copy(3).start()

        return 0

    lax.fori_loop(0, 8, step, 0)

    def join(i, h, slot):
        far_copy(slot).wait_recv()

        def add(at, src):
            own[i, at] = (own[i, at].astype(F32) + got[slot, src].astype(F32)).astype(BF)

        each(h * half, half, add)

    join(2, 0, 0)
    far_copy(4).start()
    join(1, 1, 1)
    far_copy(5).start()
    near_copy(3).wait_recv()

    def first(h, slot):
        far_copy(slot).wait_recv()

        def add(at, src):
            o_ref[at] = own[3, at].astype(F32) + near[3, at].astype(F32) + got[slot, src].astype(F32)

        each(h * half, half, add)

    first(0, 2)
    first(1, 3)

    def last(h, slot):
        far_copy(slot).wait_recv()

        def add(at, src):
            o_ref[at] = o_ref[at] + got[slot, src].astype(F32)

        each(h * half, half, add)

    last(0, 4)
    last(1, 5)
    for i in range(4):
        near_copy(i).wait_send()
    for slot in range(6):
        far_copy(slot).wait_send()


def product_scatter(pairs, n, cid, after=None):
    after = jnp.zeros((8, 128), F32) if after is None else after
    rows = pairs[0][0].shape[0] // n
    cols = pairs[0][1].shape[0 if pairs[0][2] else 1]
    bs, seconds, firsts, used = [], [], [], []
    for a, b, t in pairs:
        if not any(b is other for other in bs):
            bs.append(b)
            used.append(0)
        at = [b is other for other in bs].index(True)
        seconds.append(at)
        firsts.append(used[at])
        used[at] += a.shape[1]
    if n != 8:
        total = sum(
            ntdot(a, b) if t else dot(a, b[first : first + a.shape[1]])
            for (a, b, t), first in zip(pairs, firsts)
        )
        return reduce_scatter(total.astype(BF).reshape(n, rows, cols), n, cid, after)
    vmem = pl.BlockSpec(memory_space=pltpu.VMEM)
    dma = pltpu.SemaphoreType.DMA
    return pl.pallas_call(
        functools.partial(mm_rs4_kernel, tuple(t for _, _, t in pairs), tuple(seconds), tuple(firsts)),
        out_shape=jax.ShapeDtypeStruct((rows, cols), F32),
        in_specs=[vmem] * (len(pairs) + len(bs)) + [pl.BlockSpec(memory_space=pl.ANY)],
        out_specs=vmem,
        scratch_shapes=[
            pltpu.VMEM((2, 4, rows, cols), BF),
            pltpu.VMEM((4, rows, cols), BF),
            pltpu.VMEM((6, rows // 2, cols), BF),
            dma((4,)), dma((4,)), dma((6,)), dma((6,)),
        ],
        compiler_params=pltpu.CompilerParams(collective_id=cid, has_side_effects=True, vmem_limit_bytes=GIANT),
    )(*(a.reshape(n, rows, a.shape[1]) for a, _, _ in pairs), *bs, after)


def chain_kernel(axis, count, cuts, *refs):
    arrays = len(cuts)
    x_refs, after_ref, o_refs = refs[:arrays], refs[arrays], refs[arrays + 1 : 2 * arrays + 1]
    rest = refs[2 * arrays + 1 :]
    up_in, up_out, down_in, down_out = (rest[k * arrays : (k + 1) * arrays] for k in range(4))
    up_send, up_recv, down_send, down_recv = rest[4 * arrays :]
    me = lax.axis_index(axis)
    first, last = me == 0, me == count - 1
    above, below = (me + 1) % count, (me + count - 1) % count
    barrier = pltpu.get_barrier_semaphore()

    @pl.when(me > 0)
    def _():
        pl.semaphore_signal(barrier, inc=1, device_id={axis: below}, device_id_type=MESH)

    @pl.when(me < count - 1)
    def _():
        pl.semaphore_signal(barrier, inc=1, device_id={axis: above}, device_id_type=MESH)

    @pl.when((me > 0) & (me < count - 1))
    def _():
        pl.semaphore_wait(barrier, 2)

    @pl.when(first | last)
    def _():
        pl.semaphore_wait(barrier, 1)

    pieces = [(k, c) for k in range(arrays) for c in range(cuts[k])]
    lane = lambda k: x_refs[k].shape[1] // cuts[k]
    at = lambda k, c: slice(c * lane(k), (c + 1) * lane(k))

    def up(s, k, c):
        return send(up_out[k].at[c], up_in[k].at[c], up_send.at[s], up_recv.at[s], above, axis)

    def down(s, k, c):
        return send(down_out[k].at[c], down_in[k].at[c], down_send.at[s], down_recv.at[s], below, axis)

    for s, (k, c) in enumerate(pieces):
        own = x_refs[k][:, at(k, c)]

        @pl.when(first)
        def _():
            up_out[k][c] = own
            up(s, k, c).start()

        @pl.when(last)
        def _():
            down_out[k][c] = own
            down(s, k, c).start()

    own = lambda s: x_refs[pieces[s][0]][:, at(*pieces[s])].astype(F32)

    def serve_up(s):
        k, c = pieces[s]

        @pl.when(me > 0)
        def _():
            up(s, k, c).wait_recv()

            @pl.when(me < count - 1)
            def _():
                up_out[k][c] = (own(s) + up_in[k][c].astype(F32)).astype(BF)
                up(s, k, c).start()

    def serve_down(s):
        k, c = pieces[s]

        @pl.when(me < count - 1)
        def _():
            down(s, k, c).wait_recv()

            @pl.when(me > 0)
            def _():
                down_out[k][c] = (own(s) + down_in[k][c].astype(F32)).astype(BF)
                down(s, k, c).start()

    def finish(s):
        k, c = pieces[s]
        put = lambda value: o_refs[k].__setitem__((slice(None), at(k, c)), value)

        @pl.when(first)
        def _():
            put(own(s) + down_in[k][c].astype(F32))

        @pl.when(last)
        def _():
            put(own(s) + up_in[k][c].astype(F32))

        @pl.when((me > 0) & (me < count - 1))
        def _():
            put(own(s) + up_in[k][c].astype(F32) + down_in[k][c].astype(F32))

    for s in range(len(pieces) + 1):
        for side, early, late in ((me * 2 < count, serve_up, serve_down), (me * 2 >= count, serve_down, serve_up)):
            @pl.when(side)
            def _():
                if s < len(pieces):
                    early(s)
                if s:
                    late(s - 1)

        if s:
            finish(s - 1)

    for s, (k, c) in enumerate(pieces):
        @pl.when(me < count - 1)
        def _():
            up(s, k, c).wait_send()

        @pl.when(me > 0)
        def _():
            down(s, k, c).wait_send()


def chain_sum(arrays, cuts, count, cid, after, axis="dp"):
    vmem = pl.BlockSpec(memory_space=pltpu.VMEM)
    total = sum(cuts)
    slots = [pltpu.VMEM((c, a.shape[0], a.shape[1] // c), BF) for a, c in zip(arrays, cuts)]
    return pl.pallas_call(
        functools.partial(chain_kernel, axis, count, tuple(cuts)),
        out_shape=[jax.ShapeDtypeStruct(a.shape, F32) for a in arrays],
        in_specs=[vmem] * len(arrays) + [pl.BlockSpec(memory_space=pl.ANY)],
        out_specs=[vmem] * len(arrays),
        scratch_shapes=slots * 4 + [pltpu.SemaphoreType.DMA((total,))] * 4,
        compiler_params=pltpu.CompilerParams(collective_id=cid, has_side_effects=True, vmem_limit_bytes=GIANT),
    )(*arrays, after)


def gather_product4_kernel(body, weights, aligned, x_ref, *refs):
    w_refs, refs = refs[:weights], refs[weights:]
    row_refs, o_ref = refs[:aligned], refs[aligned]
    results, (mine_sem, far_send, far_recv, near_send, near_recv) = refs[aligned + 1 : -5], refs[-5:]
    me = lax.axis_index("seq")
    core, (sib, east, north, across) = square(me)
    x, y = (me // 2) % 2, me // 4
    greet([sib, east, north])
    half = x_ref.shape[0] // 2
    cut = (pl.ds(0, half), pl.ds(half, half))
    hops = (
        (me, 0, east), (me, 1, east), (me, 1, north), (me, 0, north), (east, 0, north), (north, 1, east)
    )
    handed = ((east, 0), (east, 1), (north, 1), (north, 0), (across, 0), (across, 1))

    def far(slot):
        block, h, peer = hops[slot]
        ref = o_ref.at[block, cut[h]]
        return send(x_ref.at[cut[h]] if slot < 4 else ref, ref, far_send.at[slot], far_recv.at[slot], peer)

    def near(slot):
        if slot == 6:
            return send(x_ref, o_ref.at[me], near_send.at[6], near_recv.at[6], sib)
        block, h = handed[slot]
        ref = o_ref.at[block, cut[h]]
        return send(ref, ref, near_send.at[slot], near_recv.at[slot], sib)

    mine = pltpu.make_async_copy(x_ref, o_ref.at[me], mine_sem)
    mine.start()
    for slot in (0, 2, 1, 3):
        far(slot).start()
    near(6).start()

    def arrive(slot, relay=None):
        far(slot).wait_recv()
        if relay is not None:
            far(relay).start()
        near(slot).start()

    def step(s, _):
        @pl.when(s == 0)
        def _():
            mine.wait()

        @pl.when(s == 1)
        def _():
            near(6).wait_recv()

        @pl.when(s == 2)
        def _():
            arrive(0, 4)
            arrive(2, 5)
            arrive(1)

        @pl.when(s == 3)
        def _():
            near(0).wait_recv()
            near(1).wait_recv()

        @pl.when(s == 4)
        def _():
            arrive(3)

        @pl.when(s == 5)
        def _():
            near(2).wait_recv()
            near(3).wait_recv()

        @pl.when(s == 6)
        def _():
            arrive(4)
            arrive(5)

        @pl.when(s == 7)
        def _():
            near(4).wait_recv()
            near(5).wait_recv()

        pair = s // 2
        seat = (((y + pair // 2) % 2) * 2 + (x + pair % 2) % 2) * 2 + (core + s) % 2
        for ref, value in zip(results, body(o_ref[seat], *w_refs, *(ref[seat] for ref in row_refs))):
            ref[seat] = value.astype(ref.dtype)
        return 0

    lax.fori_loop(0, 8, step, 0)
    for slot in range(7):
        near(slot).wait_send()
    for slot in range(6):
        far(slot).wait_send()


def gather_product(body, x, weights, outs, n, cid, by_rows=()):
    rows = x.shape[0]
    if n != 8:
        whole = all_gather(x, n, cid)
        values = body(
            whole.reshape(n * rows, -1), *weights, *(a.reshape(n * rows, a.shape[2]) for a in by_rows)
        )
        return [whole] + [v.astype(t).reshape(n, rows, -1) for v, (_, t) in zip(values, outs)]
    vmem = pl.BlockSpec(memory_space=pltpu.VMEM)
    dma = pltpu.SemaphoreType.DMA
    return pl.pallas_call(
        functools.partial(gather_product4_kernel, body, len(weights), len(by_rows)),
        out_shape=[jax.ShapeDtypeStruct((n,) + x.shape, x.dtype)]
        + [jax.ShapeDtypeStruct((n, rows, c), t) for c, t in outs],
        in_specs=[vmem] * (1 + len(weights) + len(by_rows)),
        out_specs=[vmem] * (1 + len(outs)),
        scratch_shapes=[dma, dma((6,)), dma((6,)), dma((7,)), dma((7,))],
        compiler_params=pltpu.CompilerParams(collective_id=cid, has_side_effects=True, vmem_limit_bytes=GIANT),
    )(x, *weights, *by_rows)


class HeadPlan:
    def __init__(self, n):
        self.n = n
        self.per = -(-HEADS // n)
        group = HEADS // KVH
        self.first_kv, self.slots = [], 1
        for i in range(n):
            low, high = i * self.per, min((i + 1) * self.per, HEADS) - 1
            if low >= HEADS:
                self.first_kv.append(KVH)
            else:
                self.first_kv.append(low // group)
                self.slots = max(self.slots, high // group - low // group + 1)
        self.width = self.per * HEAD
        self.kv_width = self.slots * HEAD

    def head_table(self):
        group = HEADS // KVH
        rows = []
        for i in range(self.n):
            heads = [i * self.per + j for j in range(self.per)]
            rows.append(
                [h // group - self.first_kv[i] if h < HEADS else 0 for h in heads]
                + [int(h < HEADS) for h in heads]
            )
        return jnp.array(rows, jnp.int32)

    def kv_used(self, i):
        group = HEADS // KVH
        heads = range(i * self.per, min((i + 1) * self.per, HEADS))
        return sorted({h // group for h in heads})

    def moves(self):
        lists = []
        for i in range(self.n):
            first = i * self.width
            mine = [(0, first, min(self.width, HEADS * HEAD - first))] if first < HEADS * HEAD else []
            for kind in range(2):
                start = HEADS * HEAD + kind * KVH * HEAD
                for g in self.kv_used(i):
                    slot = g - self.first_kv[i]
                    mine.append((self.width + kind * self.kv_width + slot * HEAD, start + g * HEAD, HEAD))
            lists.append(tuple(mine))
        return tuple(lists)

    def join_columns(self, g):
        q = [g[i, :, : self.width] for i in range(self.n)]
        q = jnp.concatenate(q, axis=1)[:, : HEADS * HEAD].astype(F32)
        kv = []
        for kind in range(2):
            for head in range(KVH):
                total = 0.0
                for i in range(self.n):
                    if head in self.kv_used(i):
                        at = self.width + kind * self.kv_width + (head - self.first_kv[i]) * HEAD
                        total = total + g[i, :, at : at + HEAD].astype(F32)
                kv.append(total)
        return jnp.concatenate([q] + kv, axis=1)


def reblock(rows, have, want, total):
    n, me = lax.axis_size("seq"), lax.axis_index("seq")
    result = jnp.zeros((want,) + rows.shape[1:], rows.dtype)
    pad = jnp.pad(rows, ((want, want), (0, 0)))
    for shift in range(-(n - 1), n):
        pairs = []
        for i in range(n):
            j = i + shift
            if 0 <= j < n:
                low = max(i * have, j * want)
                high = min((i + 1) * have, (j + 1) * want, total)
                if low < high:
                    pairs.append((i, j))
        if not pairs:
            continue
        start = want + (me + shift) * want - me * have
        piece = lax.dynamic_slice_in_dim(pad, jnp.clip(start, 0, have + want), want, 0)
        if shift:
            piece = lax.ppermute(piece, "seq", pairs)
        else:
            ok = jnp.array([(i, i) in pairs for i in range(n)])[me]
            piece = jnp.where(ok, piece, jnp.zeros_like(piece))
        result = result + piece
    return result


def per_device(tokens, lengths, cotangent, w_qkv, w_ao, w_in, w_xp, w_dt, w_so, w_gu, w_down,
               norm_in, norm_attn, norm_ssm, norm_ffn, conv_w, conv_b, dt_bias, a_log, d_skip):
    seqs, slot_len, width = tokens.shape
    n, me, replicas = lax.axis_size("seq"), lax.axis_index("seq"), lax.axis_size("dp")
    local, rows = seqs * slot_len, seqs * slot_len * n
    cols = INNER // n
    plan = HeadPlan(n)
    w_rows, ao_rows = w_qkv.shape[0], w_ao.shape[0]
    pos = me * slot_len + jnp.arange(slot_len, dtype=jnp.int32)
    is_valid = pos[None, :] < lengths[:, None]
    table = plan.head_table()[me]
    tie = lax.optimization_barrier
    flat = lambda v: v.reshape(rows, v.shape[-1])
    later = lambda g, zero: g + zero.astype(g.dtype)
    nothing = lambda *sums: 0.0 * sum(g.reshape(-1)[0].astype(F32) for g in sums)
    mark = lambda zero: jnp.full((8, 128), zero)
    by_device = lambda m: m.reshape(n, local, m.shape[-1])
    exchange = lambda v: lax.all_to_all(v, "seq", 0, 0, tiled=True)
    blocks = lambda v: v.reshape(n, seqs, slot_len, v.shape[-1])
    mine = lambda v: lax.dynamic_slice_in_dim(v, me * cols, cols, v.ndim - 1)
    over = lambda g: lax.psum(g, "dp")

    def one_step(work):
        shapes = jax.eval_shape(work, 0)
        none = lambda _: jax.tree.map(lambda t: jnp.zeros(t.shape, t.dtype), shapes)
        return lax.cond(lengths[0] > 0, work, none, 0)

    def row_sums(a, b, cid):
        both = jnp.stack([a, b]).reshape(-1, 128)
        return small_sum(both, n, cid).reshape(2, rows)

    wdt = mine(w_dt)
    taps, bias, dtb, skip = mine(conv_w), mine(conv_b), mine(dt_bias), mine(d_skip)
    rate = -jnp.exp(mine(a_log))
    ssm_gain = mine(norm_ssm)
    attn_gain = lax.dynamic_slice_in_dim(
        jnp.pad(norm_attn, (0, n * plan.width - HEADS * HEAD)), me * plan.width, plan.width, 0
    )

    x = tokens.astype(F32).reshape(local, width)
    scale_in = lax.rsqrt(jnp.mean(x * x, axis=-1, keepdims=True) + EPSILON)
    normed, qkv_cols, in_x, in_z = gather_and_exchange(
        tokens.reshape(local, width), norm_in, w_qkv, plan.moves(), plan.width + 2 * plan.kv_width, w_in, n, 1
    )
    normed, qkv_cols = flat(normed), qkv_cols.reshape(n * w_rows, -1)
    wx, wz = exchange(in_x), exchange(in_z)
    heads = attn_forward(0, table, lengths, blocks(normed), qkv_cols, plan.width)
    behind = nothing(heads[1])
    for seq in range(1, seqs):
        heads = attn_forward(seq, table, lengths, blocks(normed), qkv_cols, plan.width, heads)
    attended, lse, q, k, v = heads
    ao_all = lax.all_gather(later(w_ao, behind), "seq", axis=0, tiled=True)
    ao_mine = lax.dynamic_slice_in_dim(
        jnp.pad(ao_all, ((0, n * plan.width - HEADS * HEAD), (0, 0))), me * plan.width, plan.width, 0
    )
    upstream = (cotangent.astype(F32) * is_valid[..., None]).reshape(local, width)
    upstream_all = lax.all_gather(later(upstream.astype(BF), behind), "seq", axis=0, tiled=True)
    wx = later(wx, nothing(lse)).reshape(n * w_rows, cols)
    wz = wz.reshape(n * w_rows, cols)
    xp = jnp.swapaxes(w_xp, 0, 1)
    xp = jnp.concatenate([xp[DTR:], xp[:DTR]], axis=0)
    x_conv, conv_pre, mixer_in, mixer_low, projected = signal_forward(blocks(normed), wx, taps, bias[None], xp)
    mixer_low = flat(mixer_low)
    projected = blocks(all_sum(by_device(projected), n, 15))
    core, z_gate, ssm_sq, start = scan_forward(
        projected, mixer_in, blocks(normed), wz, wdt, dtb[None], rate, skip[None]
    )
    squares = row_sums(jnp.sum(attended * attended, axis=3).reshape(rows), ssm_sq.reshape(rows), 2)
    r_attn = lax.rsqrt(squares[0] / (HEADS * HEAD) + EPSILON)
    r_ssm = lax.rsqrt(squares[1] / INNER + EPSILON)
    attn_low, ssm_low = map(flat, norm_both(
        by_device(squares.T), by_device(attended), attn_gain[None], by_device(core), by_device(z_gate), ssm_gain[None]
    ))
    mixed = product_scatter(((attn_low, ao_mine, False), (ssm_low, w_so, False)), n, 3)
    residual = x + 0.5 * mixed
    r_ffn = lax.rsqrt(jnp.mean(residual * residual, axis=-1, keepdims=True) + EPSILON)
    turned = jnp.transpose(w_gu, (1, 2, 0))
    w_gate, w_up = turned[0], turned[1]
    hidden = w_gate.shape[0]

    def gated_units(rows_in, gate_ref, up_ref):
        gate, up = ntdot(rows_in, gate_ref[...]), ntdot(rows_in, up_ref[...])
        return gate, up, jax.nn.silu(gate) * up

    normed_two, gate, up, activated = gather_product(
        gated_units, (residual * r_ffn * norm_ffn).astype(BF), (w_gate, w_up), ((hidden, BF),) * 3, n, 4
    )
    normed_two, activated = flat(normed_two), flat(activated)

    grad_gate, grad_up = map(flat, ffn_backward(by_device(upstream_all), w_down, gate, up))
    g_down = tndot(activated, upstream_all).astype(BF)
    g_gate, g_up = tndot(grad_gate, normed_two).astype(BF), tndot(grad_up, normed_two).astype(BF)
    g_down, g_gate, g_up = tie((g_down, g_gate, g_up))
    s_down, s_gate, s_up = over((g_down, g_gate, g_up))
    grad_two = product_scatter(
        ((grad_gate, w_gate, False), (grad_up, w_up, False)), n, 5, mark(nothing(g_gate, g_up))
    )

    def norm_pull(grad, values, r, gain):
        dotted = jnp.mean(grad * gain * values, axis=-1, keepdims=True)
        return r * (grad * gain - values * (r * r * dotted)), jnp.sum(grad * values * r, axis=0)

    add, g_norm_ffn = norm_pull(grad_two, residual, r_ffn, norm_ffn)
    grad_residual = upstream + add

    def heads_and_channels(rows_in, ao_ref, so_ref, head_gain, channel_gain, heads_out, core_out, gate_out):
        of_heads = 0.5 * ntdot(rows_in, ao_ref[...])
        of_channels = 0.5 * ntdot(rows_in, so_ref[...])
        gated = core_out * (gate_out * jax.nn.sigmoid(gate_out))
        sums = [
            jnp.sum(of_heads * head_gain[...] * heads_out, axis=1, keepdims=True),
            jnp.sum(of_channels * channel_gain[...] * gated, axis=1, keepdims=True),
        ]
        return of_heads, of_channels, jnp.concatenate(sums, axis=1)

    mix_low, d_attn, d_ssm, inner = gather_product(
        heads_and_channels, grad_residual.astype(BF), (ao_mine, w_so, attn_gain[None], ssm_gain[None]),
        ((plan.width, F32), (cols, F32), (2, F32)), n, 7, (by_device(attended), by_device(core), by_device(z_gate)),
    )
    mix_low, inner = flat(mix_low), inner.reshape(rows, 2)
    inner = row_sums(inner[:, 0], inner[:, 1], 8)
    stats = blocks(jnp.stack([
        r_attn, inner[0] / (HEADS * HEAD) * r_attn * r_attn, r_ssm, inner[1] / INNER * r_ssm * r_ssm
    ], axis=1))

    def mixers_back(_):
        gq, gk, gv, head_sums = attn_backward(
            table, lengths, q, k, v, blocks(d_attn), attended, lse, stats, attn_gain[None]
        )
        gpre, gmix, gz, gb, gc, grate, channel_sums = scan_backward(
            lengths, projected, mixer_in, blocks(d_ssm), core, z_gate, stats, start, wdt, dtb[None], rate, skip[None],
            ssm_gain[None],
        )
        grad_qkv, grad_z = flat(jnp.concatenate([gq, gk, gv], axis=3)), flat(gz)
        of_weights = (
            (0.5 * tndot(attn_low, mix_low)).astype(BF),
            (0.5 * tndot(ssm_low, mix_low)).astype(BF),
            tndot(normed, grad_z).astype(BF),
            tndot(normed, grad_qkv).astype(BF),
        )
        return head_sums[0], channel_sums, grad_qkv, grad_z, flat(gpre), gmix, flat(gb), flat(gc), grate, of_weights

    g_norm_attn, channel_sums, grad_qkv, grad_z, grad_step, gmix, gb, gc, grate, of_weights = one_step(mixers_back)
    g_norm_ssm, gskip, g_dt_bias = channel_sums[0], channel_sums[1:2], channel_sums[2]
    g_ao, g_so, g_z, g_qkv = of_weights
    g_ao = reblock(g_ao, plan.width, ao_rows, HEADS * HEAD)
    g_z = exchange(g_z.reshape(n, w_rows, cols))
    g_z = jnp.swapaxes(g_z, 0, 1).reshape(w_rows, INNER)
    g_qkv = exchange(g_qkv.reshape(n, w_rows, -1))
    g_qkv = plan.join_columns(g_qkv).astype(BF)
    first_sums = nothing(s_down, s_gate, s_up)
    grad_projected = jnp.concatenate([gb, gc, ntdot(grad_step, wdt)], axis=1)
    grad_projected = flat(all_sum(by_device(grad_projected.astype(BF)), n, 9, mark(first_sums)))
    after_one = first_sums + nothing(grad_projected)
    s_ao, s_so, s_qkv, s_z = over(tuple(later(g, after_one) for g in (g_ao, g_so, g_qkv, g_z)))

    def signal_back(_):
        grad_x, sums = signal_backward(gmix, blocks(grad_projected), xp, conv_pre, x_conv, taps)
        grad_x = flat(grad_x)
        return (
            grad_x,
            sums,
            tndot(normed, grad_x).astype(BF),
            tndot(grad_projected, mixer_low).astype(BF),
            tndot(grad_step, flat(projected)[:, 2 * NST :]).astype(BF),
        )

    grad_x, tap_sums, g_x, g_xp, g_wdt = one_step(signal_back)
    g_conv_w, g_conv_b = tap_sums[:KCONV], tap_sums[KCONV]
    g_x = exchange(g_x.reshape(n, w_rows, cols))
    g_x = jnp.swapaxes(g_x, 0, 1).reshape(w_rows, INNER)
    grad_normed = product_scatter(
        ((grad_x, wx, True), (grad_z, wz, True), (grad_qkv, qkv_cols, True)), n, 11
    )
    block_out = residual + product_scatter(
        ((activated, w_down, False),), n, 6, mark(nothing(grad_normed))
    )
    add_in, g_norm_in = norm_pull(grad_normed, x, scale_in, norm_in)
    grad_tokens = grad_residual + add_in

    s_gu = jnp.transpose(jnp.stack([s_gate, s_up]), (2, 0, 1))
    s_x, s_xp, s_wdt = chain_sum((g_x, g_xp, g_wdt), (5, 1, 1), replicas, 14, mark(nothing(block_out, s_ao, s_so, s_qkv, s_z)))
    s_in = jnp.concatenate([s_x, s_z.astype(F32)], axis=1)
    s_xp = jnp.swapaxes(jnp.concatenate([s_xp[2 * NST :], s_xp[: 2 * NST]], axis=0), 0, 1)
    s_wdt = jnp.swapaxes(s_wdt, 0, 1)

    place = lambda g: lax.dynamic_update_slice_in_dim(
        jnp.zeros((n * plan.width,), F32), g, me * plan.width, 0
    )[: HEADS * HEAD]

    def pad_rows(v):
        v = v.reshape(-1)
        return jnp.pad(v, (0, -v.size % 1024)).reshape(-1, 128)

    shared = jnp.stack([g_norm_in, place(g_norm_attn), g_norm_ffn]) + nothing(g_x)
    total = small_sum(pad_rows(shared), n, 12).reshape(-1)[: shared.size].reshape(shared.shape)
    shared = lax.dynamic_slice_in_dim(total, me * w_rows, w_rows, 1)
    owned = jnp.concatenate(
        [g_norm_ssm[None], g_conv_w, g_conv_b[None], g_dt_bias[None], grate * rate, gskip], axis=0
    )
    small = pad_rows(jnp.concatenate([shared.reshape(-1), owned.reshape(-1)]))
    small = small_sum(small, replicas, 13, "dp").reshape(-1)
    s_shared = small[: shared.size].reshape(shared.shape)
    s_owned = small[shared.size : shared.size + owned.size].reshape(owned.shape)
    full = lambda g: g.astype(F32)

    return (
        block_out.astype(BF).reshape(seqs, slot_len, width),
        grad_tokens.reshape(seqs, slot_len, width),
        full(s_qkv),
        full(s_ao),
        full(s_in),
        full(s_xp),
        full(s_wdt),
        full(s_so),
        full(s_gu),
        full(s_down),
        s_shared[0],
        s_shared[1],
        s_owned[0],
        s_shared[2],
        s_owned[1 : 1 + KCONV],
        s_owned[1 + KCONV],
        s_owned[2 + KCONV],
        s_owned[3 + KCONV : 3 + KCONV + NST],
        s_owned[3 + KCONV + NST],
    )


def solution(mesh):
    rows, cols, flat = P("seq", None), P(None, "seq"), P("seq")
    act = P("dp", "seq", None)
    hid = P(None, None, "seq")
    in_specs = (act, P("dp"), act, rows, rows, rows, rows, P(), rows, hid, rows) + (P(),) * 9
    out_specs = (act, act, rows, rows, rows, rows, cols, rows, hid, rows,
                 flat, flat, flat, flat, cols, flat, flat, cols, flat)
    return jax.shard_map(per_device, mesh=mesh, in_specs=in_specs, out_specs=out_specs, check_vma=False)
```
